32 devices in a mesh: wide: 16 (over z, x, core), narrow: 2 (over y).
Axes of the slice: x: 2, y: 2, z: 4, core: 2. Of those that a mesh axis runs over, the one named last changes fastest.
Arguments:
- tokens: bfloat16 [32768, 768], P(('wide', 'narrow')), may hold values from -6 to 6
- patch_grid: int32 [64, 4, 2], P(('wide', 'narrow')), may hold values from 8 to 11
- qkv_rows: bfloat16 [13824, 128], P(('wide', 'narrow')), may hold values from -0.21875 to 0.21875
- proj_rows: bfloat16 [4608, 128], P(('wide', 'narrow')), may hold values from -0.625 to 0.625
- fc1_rows: bfloat16 [18432, 128], P(('wide', 'narrow')), may hold values from -0.21875 to 0.21875
- fc2_rows: bfloat16 [18432, 128], P(('wide', 'narrow')), may hold values from -0.15625 to 0.15625
- norm_gain: float32 [2, 768], replicated, may hold values from 0.5 to 1.5
- norm_bias: float32 [2, 768], replicated, may hold values from -2 to 2
- qv_bias: float32 [2, 768], replicated, may hold values from -2 to 2
- proj_bias: float32 [768], replicated, may hold values from -2 to 2
- fc1_bias: float32 [3072], replicated, may hold values from -2 to 2
- fc2_bias: float32 [768], replicated, may hold values from -2 to 2
- layer_scale: float32 [2, 768], replicated, may hold values from 0.1 to 0.4
- cotangent: bfloat16 [32768, 768], P(('wide', 'narrow')), may hold values from -6 to 6
Outputs:
- layer_out: bfloat16 [32768, 768], P(('wide', 'narrow'))
- input_grad: float32 [32768, 768], P(('wide', 'narrow'))
- qkv_grad: float32 [13824, 128], P(('wide', 'narrow'))
- proj_grad: float32 [4608, 128], P(('wide', 'narrow'))
- fc1_grad: float32 [18432, 128], P(('wide', 'narrow'))
- fc2_grad: float32 [18432, 128], P(('wide', 'narrow'))
- gain_grad: float32 [2, 768], replicated
- norm_bias_grad: float32 [2, 768], replicated
- qv_bias_grad: float32 [2, 768], replicated
- proj_bias_grad: float32 [768], replicated
- fc1_bias_grad: float32 [3072], replicated
- fc2_bias_grad: float32 [768], replicated
- scale_grad: float32 [2, 768], replicated
The draws below stay inside these ranges and needn't reach their ends.
All inputs are finite; a program needn't handle non-finite values.
Results may differ from the reference program's by a relative error of at most 0.0087.
Values may be sent and summed in bfloat16 or wider, within the bound.
No kernel may reach another device: no remote copies, remote signals or barrier semaphores. Data moves between devices by JAX's collectives and lax.ppermute only.
A program may use at most 192 MiB of HBM per device.

```python
import math
import jax
import jax.numpy as jnp
from jax import lax

D = 768
H = 12
HD = 64
FF = 3072
ROW = 128
PACK = 512
IMGS = 4
PREFIX = 5
GRID_LO = 8
GRID_HI = 11
PACKS = 64
TOKENS = 32768
QKV_ROWS = 13824
PROJ_ROWS = 4608
FC_ROWS = 18432


def plant(array, rng, low, largest):
    longest = array.shape.index(max(array.shape))
    spots = []
    for shift in (0, 1):
        where = [jax.random.randint(jax.random.fold_in(rng, axis), (), 0, length) for axis, length in enumerate(array.shape)]
        where[longest] = (where[longest] + shift) % array.shape[longest]
        spots.append(tuple(where))
    return array.at[spots[0]].set(low).at[spots[1]].set(largest)


def level_of(key, dims, split, least, largest):
    loudness, own = 1.0, jax.random.fold_in(key, 6)
    for dim, shards_of in split:
        steps = jnp.exp(jax.random.uniform(jax.random.fold_in(own, dim), (shards_of,), jnp.float32, least / len(split), largest / len(split)))
        loudness = loudness * jnp.repeat(steps, dims[dim] // shards_of).reshape([-1 if axis == dim else 1 for axis in range(len(dims))])
    return loudness


def normal_values(key, shape, spread, limit, cuts=(), kind=jnp.bfloat16):
    entries = jax.random.normal(key, shape, jnp.float32) * spread
    if len(cuts) > 0:
        entries = level_of(key, shape, cuts, -0.22, 0.18) * entries
    return jnp.clip(entries, min=-limit, max=limit).astype(kind)


def setup_inputs(seed: int = 0) -> dict:
    key_of = jax.random.split(jax.random.key(seed), 15)
    return {
        "tokens": normal_values(key_of[0], (TOKENS, D), 1.0, 6.0, ((0, 32),)),
        "patch_grid": plant(jax.random.randint(key_of[1], (PACKS, IMGS, 2), GRID_LO, GRID_HI + 1), jax.random.fold_in(key_of[1], 1), GRID_LO, GRID_HI).astype(jnp.int32),
        "qkv_rows": normal_values(key_of[2], (QKV_ROWS, ROW), D ** -0.5, 0.21875, ((0, 32),)),
        "proj_rows": normal_values(key_of[3], (PROJ_ROWS, ROW), (D // 8) ** -0.5, 0.625, ((0, 32),)),
        "fc1_rows": normal_values(key_of[4], (FC_ROWS, ROW), D ** -0.5, 0.21875, ((0, 32),)),
        "fc2_rows": normal_values(key_of[5], (FC_ROWS, ROW), (FF // 2) ** -0.5, 0.15625, ((0, 32),)),
        "norm_gain": jnp.clip(1.0 + 0.1 * jax.random.normal(key_of[6], (2, D), jnp.float32), 0.5, 1.5),
        "norm_bias": normal_values(key_of[7], (2, D), 0.3, 2.0, (), jnp.float32),
        "qv_bias": normal_values(key_of[8], (2, D), 0.3, 2.0, (), jnp.float32),
        "proj_bias": normal_values(key_of[9], (D,), 0.3, 2.0, (), jnp.float32),
        "fc1_bias": normal_values(key_of[10], (FF,), 0.3, 2.0, (), jnp.float32),
        "fc2_bias": normal_values(key_of[11], (D,), 0.3, 2.0, (), jnp.float32),
        "layer_scale": jnp.clip(jnp.exp(jax.random.uniform(key_of[12], (2, D), jnp.float32, math.log(0.1), math.log(0.4))), 0.1, 0.4),
        "cotangent": normal_values(key_of[13], (TOKENS, D), 1.0, 6.0, ((0, 32),)),
    }


EPSILON = 1e-06
HIGHEST = lax.Precision.HIGHEST

@jax.custom_vjp
def low(v):
    return lax.optimization_barrier(v.astype(jnp.bfloat16)).astype(jnp.float32)

@jax.custom_vjp
def low_back(v):
    return v

def low_keep(v):
    return (low(v), None)

def low_pass(kept, grad):
    return (grad,)

def back_keep(v):
    return (v, None)

def back_low(kept, grad):
    return (low(grad),)
low.defvjp(low_keep, low_pass)
low_back.defvjp(back_keep, back_low)

def layout(patch_grid):
    lengths = (PREFIX + patch_grid[:, :, 0] * patch_grid[:, :, 1]).astype(jnp.int32)
    image_ends = jnp.cumsum(lengths, axis=1).astype(jnp.int32)
    position = jnp.arange(PACK, dtype=jnp.int32)
    segment = lax.optimization_barrier(jnp.sum((position[None, :, None] >= image_ends[:, None, :]).astype(jnp.int32), axis=2)).astype(jnp.int32)
    usable = segment < IMGS
    joined = (segment[:, :, None] == segment[:, None, :]) & usable[:, None, :]
    itself = position[:, None] == position[None, :]
    return (usable, joined | itself[None])

def layer_norm(inputs, factor, offset):
    average = lax.optimization_barrier(jnp.mean(inputs, axis=-1, keepdims=True))
    centered = inputs - average
    variance = lax.optimization_barrier(jnp.mean(centered * centered, axis=-1, keepdims=True))
    return centered * lax.rsqrt(variance + EPSILON) * factor + offset

def attend(queries, key_rows, values, joined):
    scores = jnp.einsum('gqhd,gkhd->ghqk', queries, key_rows, precision=HIGHEST) * HD ** (-0.5)
    scores = low_back(scores)
    masked = jnp.where(joined[:, None], scores, -1e+30)
    row_top = lax.optimization_barrier(jnp.max(masked, axis=-1, keepdims=True))
    exponent = jnp.exp(masked - row_top)
    probability = exponent / lax.optimization_barrier(jnp.sum(exponent, axis=-1, keepdims=True))
    return jnp.einsum('ghqk,gkhd->gqhd', low(probability), values, precision=HIGHEST)

def forward(inputs, usable, joined, params):
    qkv_w, proj_w, fc1_w, fc2_w, norm_gain, norm_bias, qv_bias, proj_bias, fc1_bias, fc2_bias, layer_scale = params
    inputs = inputs * usable
    normed_one = low(layer_norm(inputs, norm_gain[0], norm_bias[0]))
    offset = jnp.concatenate([qv_bias[0], jnp.zeros_like(qv_bias[0]), qv_bias[1]])
    projected = low(low_back(jnp.einsum('gtd,de->gte', normed_one, qkv_w, precision=HIGHEST) + offset))
    head_shape = inputs.shape[:2] + (H, HD)
    queries = projected[..., :D].reshape(head_shape)
    key_rows = projected[..., D:2 * D].reshape(head_shape)
    values = projected[..., 2 * D:].reshape(head_shape)
    attended = jax.checkpoint(attend)(queries, key_rows, values, joined).reshape(inputs.shape)
    attended = low(low_back(attended))
    branch_one = low_back(jnp.einsum('gtd,de->gte', attended, proj_w, precision=HIGHEST) + proj_bias)
    middle = inputs + layer_scale[0] * branch_one
    normed_two = low(layer_norm(middle, norm_gain[1], norm_bias[1]))
    hidden = low_back(jnp.einsum('gtd,df->gtf', normed_two, fc1_w, precision=HIGHEST) + fc1_bias)
    activated = low(jax.nn.gelu(hidden, approximate=False))
    branch_two = low_back(jnp.einsum('gtf,fd->gtd', activated, fc2_w, precision=HIGHEST) + fc2_bias)
    return usable * (middle + layer_scale[1] * branch_two)

def reference(tokens, patch_grid, qkv_rows, proj_rows, fc1_rows, fc2_rows, norm_gain, norm_bias, qv_bias, proj_bias, fc1_bias, fc2_bias, layer_scale, cotangent):
    params = (qkv_rows.astype(jnp.float32).reshape(D, 3 * D), proj_rows.astype(jnp.float32).reshape(D, D), fc1_rows.astype(jnp.float32).reshape(D, FF), fc2_rows.astype(jnp.float32).reshape(FF, D), norm_gain, norm_bias, qv_bias, proj_bias, fc1_bias, fc2_bias, layer_scale)
    pack_group = math.gcd(PACKS, max(1, 4096 // PACK))
    rounds = PACKS // pack_group
    token_blocks = tokens.reshape(rounds, pack_group, PACK, D)
    grid_blocks = patch_grid.reshape(rounds, pack_group, IMGS, 2)
    upstream_blocks = cotangent.reshape(rounds, pack_group, PACK, D)

    def one_block(totals, element):
        token_block, grid_block, upstream_block = element
        usable_rows, joined = layout(grid_block)
        usable = usable_rows[:, :, None].astype(jnp.float32)

        def apply(inputs, weights):
            return forward(inputs, usable, joined, weights)
        result, pullback = jax.vjp(apply, token_block.astype(jnp.float32), params)
        input_grad, weight_grads = pullback(upstream_block.astype(jnp.float32))
        totals = jax.tree.map(lambda total, term: total + term, totals, weight_grads)
        return (totals, (result.astype(jnp.bfloat16), input_grad))
    zeros = jax.tree.map(jnp.zeros_like, params)
    totals, (outputs, input_grads) = lax.scan(one_block, zeros, (token_blocks, grid_blocks, upstream_blocks))
    return (outputs.reshape(TOKENS, D), input_grads.reshape(TOKENS, D), totals[0].reshape(QKV_ROWS, ROW), totals[1].reshape(PROJ_ROWS, ROW), totals[2].reshape(FC_ROWS, ROW), totals[3].reshape(FC_ROWS, ROW), totals[4], totals[5], totals[6], totals[7], totals[8], totals[9], totals[10])
```

```python
from functools import partial

import jax
import jax.numpy as jnp
from jax import lax
from jax.experimental import pallas as pl
from jax.experimental.pallas import tpu as pltpu
from jax.sharding import PartitionSpec as P

H = 12
PREFIX = 5
EPSILON = 1e-06
NEGATIVE = -1e30
AXES = ("wide", "narrow")
COLUMNS = 8
BF16 = jnp.bfloat16
F32 = jnp.float32


def dot(a, b):
    return lax.dot_general(a, b, (((1,), (0,)), ((), ())), preferred_element_type=F32)


def dot_nt(a, b):
    return lax.dot_general(a, b, (((1,), (1,)), ((), ())), preferred_element_type=F32)


def dot_tn(a, b):
    return lax.dot_general(a, b, (((0,), (0,)), ((), ())), preferred_element_type=F32)


def params(mib=48):
    return pltpu.CompilerParams(vmem_limit_bytes=mib * 2**20)


def full(shape):
    return pl.BlockSpec(shape, lambda *_: (0,) * len(shape))


def standardize(v):
    centered = v - jnp.mean(v, axis=-1, keepdims=True)
    inverse = lax.rsqrt(jnp.mean(centered * centered, axis=-1, keepdims=True) + EPSILON)
    return centered * inverse, inverse


def standardize_back(grad, scaled, inverse):
    return inverse * (
        grad
        - jnp.mean(grad, axis=-1, keepdims=True)
        - scaled * jnp.mean(grad * scaled, axis=-1, keepdims=True)
    )


def length_of(grid_ref, image):
    return PREFIX + grid_ref[2 * image] * grid_ref[2 * image + 1]


def spans(grid_ref, pack, images):
    found, start = [], 0
    for i in range(images):
        length = length_of(grid_ref, pack * images + i)
        found.append((start, length))
        start = start + length
    return found


def join(scr, core, own, other):
    for i in range(scr.shape[0]):
        scr[i, core] = own[i]
        scr[i, 1 - core] = other[i]
    blocks, cores, rows, columns = scr.shape
    return scr[...].reshape(blocks * cores * rows, columns)


def part(core, matrix, own, other):
    blocks, rows, columns = own.shape
    cut = matrix.reshape(blocks, 2, rows, columns)
    own[...] = jnp.where(core == 0, cut[:, 0], cut[:, 1])
    other[...] = jnp.where(core == 0, cut[:, 1], cut[:, 0])


def prepare_kernel(grid_ref, tok, cot, gain, bias, ls, x, n1, up, b2g, sums, *, images):
    pack = pl.program_id(0)
    slot = tok.shape[0] // images
    row = lax.broadcasted_iota(jnp.int32, (slot, tok.shape[0]), 0)
    column = lax.broadcasted_iota(jnp.int32, (slot, tok.shape[0]), 1)
    total = jnp.zeros((1, tok.shape[1]), F32)
    for i, (start, length) in enumerate(spans(grid_ref, pack, images)):
        place = jnp.where((column - row == start) & (row < length), 1.0, 0.0).astype(BF16)
        rows = pl.ds(i * slot, slot)
        moved = dot(place, tok[...])
        x[rows] = moved.astype(BF16)
        scaled, _ = standardize(moved)
        n1[rows] = (scaled * gain[0:1] + bias[0:1]).astype(BF16)
        upstream = dot(place, cot[...])
        up[rows] = upstream.astype(BF16)
        low = (ls[1:2] * upstream).astype(BF16)
        b2g[rows] = low
        total = total + jnp.sum(low.astype(F32), axis=0, keepdims=True)

    @pl.when(pack == 0)
    def _():
        sums[...] = jnp.zeros_like(sums)

    sums[...] += total


def unplace(grid_ref, pack, images, size):
    slot = size // images
    row = lax.broadcasted_iota(jnp.int32, (size, slot), 0)
    column = lax.broadcasted_iota(jnp.int32, (size, slot), 1)
    return jnp.concatenate(
        [
            jnp.where((row - column == start) & (column < length), 1.0, 0.0).astype(BF16)
            for start, length in spans(grid_ref, pack, images)
        ],
        axis=1,
    )


def lanes(rows, width, head):
    return lax.broadcasted_iota(jnp.int32, (rows, width), 1) < head


def stacked(v, low):
    zero = jnp.zeros_like(v)
    return jnp.concatenate([jnp.where(low, v, zero), jnp.where(low, zero, v)], axis=0)


def softmax(scores, column_ok):
    masked = jnp.where(column_ok, scores, NEGATIVE)
    exponent = jnp.exp(masked - jnp.max(masked, axis=1, keepdims=True))
    return exponent * (1.0 / jnp.sum(exponent, axis=1, keepdims=True))


def attend_kernel(grid_ref, sc, n1, own, other, offset, proj, att, scr, *, slot, head):
    step = pl.program_id(0)
    width = n1.shape[1]
    per = n1.shape[0] // slot
    pair = 2 * head

    @pl.when(step == 0)
    def _():
        join(scr, sc[0], own, other)

    w = scr[...].reshape(width, 3 * width)
    proj[...] = (dot(n1[...], w) + offset[...]).astype(BF16)
    low = lanes(slot, pair, head)
    key_at = lax.broadcasted_iota(jnp.int32, (slot, slot), 1)
    for i in range(per):
        ok = key_at < length_of(grid_ref, step * per + i)
        rows = pl.ds(i * slot, slot)
        for j in range(width // pair):
            q, k, v = (proj[rows, pl.ds(t * width + j * pair, pair)] for t in range(3))
            scores = dot_nt(q, stacked(k, low)) * head ** (-0.5)
            p0 = softmax(scores[:, :slot], ok)
            p1 = softmax(scores[:, slot:], ok)
            p = jnp.concatenate([p0, p1], axis=1).astype(BF16)
            att[rows, pl.ds(j * pair, pair)] = dot(p, stacked(v, low)).astype(BF16)


def hidden_kernel(sc, att, x, b2g, gain, bias, ls, proj_bias, fc1_bias, po, ps, fo, fs, b1, n2, act, slope, go, gs, pscr, fscr, *, tile):
    core = sc[0]

    @pl.when(pl.program_id(0) == 0)
    def _():
        w = join(pscr, core, po, ps)
        for r in range(0, att.shape[0], tile):
            rows = pl.ds(r, tile)
            branch = dot(att[rows], w) + proj_bias[...]
            b1[rows] = branch
            scaled, _ = standardize(x[rows].astype(F32) + ls[0:1] * branch)
            n2[rows] = (scaled * gain[1:2] + bias[1:2]).astype(BF16)

    w = join(fscr, core, fo, fs)
    for r in range(0, att.shape[0], tile):
        rows = pl.ds(r, tile)
        hidden = dot(n2[rows], w) + fc1_bias[...]
        normal = 0.5 * (1.0 + lax.erf(hidden * 0.5**0.5))
        act[rows] = (hidden * normal).astype(BF16)
        slope[rows] = normal + hidden * ((0.5 / jnp.pi) ** 0.5 * jnp.exp(-0.5 * hidden * hidden))
    part(core, dot_tn(act[...], b2g[...]).astype(BF16), go, gs)


def hidden_back_kernel(sc, b2g, n2, slope, wo, ws, hg, sums, go, gs, scr, *, tile):
    core = sc[0]
    w = join(scr, core, wo, ws)
    total = jnp.zeros(sums.shape, F32)
    for r in range(0, b2g.shape[0], tile):
        rows = pl.ds(r, tile)
        low = (dot_nt(b2g[rows], w) * slope[rows]).astype(BF16)
        hg[rows] = low
        total = total + jnp.sum(low.astype(F32), axis=0, keepdims=True)
    sums[...] = total
    part(core, dot_tn(n2[...], hg[...]).astype(BF16), go, gs)


def middle_back_kernel(sc, hg, fo, fs, po, ps, b1, x, up, gain, ls, mg, b1g, ag, sums, acc, fscr, pscr, *, tile):
    core = sc[0]
    step = pl.program_id(0)
    w = join(fscr, core, fo, fs)

    @pl.when(step == 0)
    def _():
        acc[...] = dot_nt(hg[...], w)

    @pl.when(step > 0)
    def _():
        acc[...] += dot_nt(hg[...], w)

    @pl.when(step == pl.num_programs(0) - 1)
    def _():
        wp = join(pscr, core, po, ps)
        totals = [jnp.zeros((1, x.shape[1]), F32) for _ in range(4)]
        for r in range(0, x.shape[0], tile):
            rows = pl.ds(r, tile)
            branch = b1[rows]
            scaled, inverse = standardize(x[rows].astype(F32) + ls[0:1] * branch)
            grad = acc[rows]
            back = up[rows].astype(F32) + standardize_back(grad * gain[1:2], scaled, inverse)
            mg[rows] = back
            low = (ls[0:1] * back).astype(BF16)
            b1g[rows] = low
            ag[rows] = dot_nt(low, wp).astype(BF16)
            terms = (back * branch, low.astype(F32), grad * scaled, grad)
            totals = [t + jnp.sum(v, axis=0, keepdims=True) for t, v in zip(totals, terms)]
        sums[...] = jnp.concatenate(totals, axis=0)


def attend_back_kernel(grid_ref, proj, ag, pg, sums, *, slot, head):
    step = pl.program_id(0)
    width = ag.shape[1]
    per = ag.shape[0] // slot
    pair = 2 * head
    factor = head ** (-0.5)
    low = lanes(slot, pair, head)
    key_at = lax.broadcasted_iota(jnp.int32, (slot, slot), 1)
    for i in range(per):
        ok = key_at < length_of(grid_ref, step * per + i)
        rows = pl.ds(i * slot, slot)
        for j in range(width // pair):
            q, k, v = (proj[rows, pl.ds(t * width + j * pair, pair)] for t in range(3))
            out = ag[rows, pl.ds(j * pair, pair)]
            k2 = stacked(k, low)
            scores = dot_nt(q, k2) * factor
            pull = dot_nt(out, stacked(v, low))
            ps, ss = [], []
            for half in (slice(0, slot), slice(slot, 2 * slot)):
                p = softmax(scores[:, half], ok)
                g = pull[:, half]
                ps.append(p)
                ss.append(p * (g - jnp.sum(g * p, axis=1, keepdims=True)))
            p = jnp.concatenate(ps, axis=1).astype(BF16)
            s = jnp.concatenate(ss, axis=1).astype(BF16)
            dq = dot(s, k2) * factor
            dk = dot_tn(s, q) * factor
            dv = dot_tn(p, out)
            dk = jnp.where(low, dk[:slot], dk[slot:])
            dv = jnp.where(low, dv[:slot], dv[slot:])
            for t, d in enumerate((dq, dk, dv)):
                pg[rows, pl.ds(t * width + j * pair, pair)] = d.astype(BF16)

    @pl.when(step == 0)
    def _():
        sums[...] = jnp.zeros_like(sums)

    sums[...] += jnp.sum(pg[...].astype(F32), axis=0, keepdims=True)


def weight_kernel(sc, n1, att, pg, b1g, go, gs):
    step = pl.program_id(0)
    last = pl.num_programs(0) - 1

    @pl.when(step < last)
    def _():
        part(sc[0], dot_tn(n1[...], pg[...]).astype(BF16), go, gs)

    @pl.when(step == last)
    def _():
        part(sc[0], dot_tn(att[...], b1g[...]).astype(BF16), go, gs)


def input_back_kernel(grid_ref, sc, pg, own, other, x, mg, gain, out, sums, scr, *, images):
    pack = pl.program_id(0)

    @pl.when(pack == 0)
    def _():
        join(scr, sc[0], own, other)
        sums[...] = jnp.zeros_like(sums)

    width = x.shape[1]
    grad = dot_nt(pg[...], scr[...].reshape(width, 3 * width))
    scaled, inverse = standardize(x[...].astype(F32))
    back = mg[...] + standardize_back(grad * gain[0:1], scaled, inverse)
    sums[...] += jnp.concatenate(
        [jnp.sum(grad * scaled, axis=0, keepdims=True), jnp.sum(grad, axis=0, keepdims=True)], axis=0
    )
    place = unplace(grid_ref, pack, images, x.shape[0])
    high = back.astype(BF16)
    rest = back - high.astype(F32)
    mid = rest.astype(BF16)
    lowest = (rest - mid.astype(F32)).astype(BF16)
    out[...] = dot(place, high) + dot(place, mid) + dot(place, lowest)


def layer_out_kernel(grid_ref, sc, act, wo, ws, x, b1, up, ls, fc2_bias, out, sums, acc, scr, *, images):
    step = pl.program_id(0)
    w = join(scr, sc[0], wo, ws)

    @pl.when(step == 0)
    def _():
        acc[...] = dot(act[...], w)

    @pl.when(step > 0)
    def _():
        acc[...] += dot(act[...], w)

    @pl.when(step == pl.num_programs(0) - 1)
    def _():
        size = out.shape[0] // (grid_ref.shape[0] // (2 * images))
        total = jnp.zeros(sums.shape, F32)
        for pack in range(out.shape[0] // size):
            rows = pl.ds(pack * size, size)
            branch = acc[rows] + fc2_bias[...]
            total = total + jnp.sum(up[rows].astype(F32) * branch, axis=0, keepdims=True)
            middle = x[rows].astype(F32) + ls[0:1] * b1[rows]
            result = (middle + ls[1:2] * branch).astype(BF16)
            place = unplace(grid_ref, pack, images, size)
            out[rows] = dot(place, result).astype(BF16)
        sums[...] = total


def gather(block, core):
    whole = lax.all_gather(block, AXES, axis=0, tiled=True)
    cut = whole.reshape(COLUMNS, 2, whole.shape[0] // (2 * COLUMNS), whole.shape[1])
    return cut[:, 0], cut[:, 1]


def scatter(own, other):
    matrix = jnp.stack([own, other], axis=1).reshape(-1, own.shape[-1])
    return lax.psum_scatter(matrix, AXES, scatter_dimension=0, tiled=True).astype(F32)


def reduce_all(v):
    return lax.psum(v, AXES)


def body(
    tokens,
    patch_grid,
    qkv_rows,
    proj_rows,
    fc1_rows,
    fc2_rows,
    norm_gain,
    norm_bias,
    qv_bias,
    proj_bias,
    fc1_bias,
    fc2_bias,
    layer_scale,
    cotangent,
):
    rows, width = tokens.shape
    packs, images, _ = patch_grid.shape
    pack = rows // packs
    slot = pack // images
    head = width // H
    hidden = fc1_bias.shape[0]
    row_width = qkv_rows.shape[1]
    tiles = hidden // width
    tile = min(256, rows)
    sc = jnp.zeros((1,), jnp.int32)
    grid_flat = patch_grid.reshape(-1)
    s = jax.ShapeDtypeStruct
    qkv_own, qkv_other = gather(qkv_rows.reshape(-1, 3 * width), sc)
    both = jnp.concatenate([proj_rows.reshape(-1, width), fc1_rows.reshape(-1, hidden)], axis=1)
    pf_own, pf_other = gather(both, sc)
    fc2_own, fc2_other = gather(fc2_rows.reshape(-1, width), sc)
    thin, wide_rows = width // (2 * COLUMNS), hidden // (2 * COLUMNS)
    per_tile = COLUMNS // tiles

    by_pack = pl.BlockSpec((pack, width), lambda i, *_: (i, 0))
    vec2 = full((2, width))
    x, n1, up, b2g, fc2_sums = pl.pallas_call(
        partial(prepare_kernel, images=images),
        grid_spec=pltpu.PrefetchScalarGridSpec(
            num_scalar_prefetch=1,
            grid=(packs,),
            in_specs=[by_pack, by_pack, vec2, vec2, vec2],
            out_specs=[by_pack] * 4 + [full((1, width))],
        ),
        out_shape=[s((rows, width), BF16)] * 4 + [s((1, width), F32)],
        compiler_params=params(),
    )(grid_flat, tokens, cotangent, norm_gain, norm_bias, layer_scale)

    offset = jnp.concatenate([qv_bias[0], jnp.zeros_like(qv_bias[0]), qv_bias[1]])[None]
    by_tile = lambda w: pl.BlockSpec((tile, w), lambda i, *_: (i, 0))
    proj, att = pl.pallas_call(
        partial(attend_kernel, slot=slot, head=head),
        grid_spec=pltpu.PrefetchScalarGridSpec(
            num_scalar_prefetch=2,
            grid=(rows // tile,),
            in_specs=[by_tile(width), full((COLUMNS, thin, 3 * width)), full((COLUMNS, thin, 3 * width)), full((1, 3 * width))],
            out_specs=[by_tile(3 * width), by_tile(width)],
            scratch_shapes=[pltpu.VMEM((COLUMNS, 2, thin, 3 * width), BF16)],
        ),
        out_shape=[s((rows, 3 * width), BF16), s((rows, width), BF16)],
        compiler_params=params(),
    )(grid_flat, sc, n1, qkv_own, qkv_other, offset)

    whole = full((rows, width))
    proj_blocks = pl.BlockSpec((COLUMNS, thin, width), lambda i, *_: (0, 0, 0))
    fc1_blocks = pl.BlockSpec((COLUMNS, thin, width), lambda i, *_: (0, 0, 1 + i))
    fc2_blocks = pl.BlockSpec((per_tile, wide_rows, width), lambda i, *_: (i, 0, 0))
    hidden_tile = pl.BlockSpec((rows, width), lambda i, *_: (0, i))
    thin_scr = pltpu.VMEM((COLUMNS, 2, thin, width), BF16)
    wide_scr = pltpu.VMEM((per_tile, 2, wide_rows, width), BF16)
    vec1 = full((1, width))
    hidden_vec = pl.BlockSpec((1, width), lambda i, *_: (0, i))
    b1, n2, act, slope, fc2g_own, fc2g_other = pl.pallas_call(
        partial(hidden_kernel, tile=tile),
        grid_spec=pltpu.PrefetchScalarGridSpec(
            num_scalar_prefetch=1,
            grid=(tiles,),
            in_specs=[whole, whole, whole, vec2, vec2, vec2, vec1, hidden_vec, proj_blocks, proj_blocks, fc1_blocks, fc1_blocks],
            out_specs=[whole, whole, hidden_tile, hidden_tile, fc2_blocks, fc2_blocks],
            scratch_shapes=[thin_scr, thin_scr],
        ),
        out_shape=[s((rows, width), F32), s((rows, width), BF16), s((rows, hidden), BF16), s((rows, hidden), F32)]
        + [s((COLUMNS, wide_rows, width), BF16)] * 2,
        compiler_params=params(56),
    )(sc, att, x, b2g, norm_gain, norm_bias, layer_scale, proj_bias[None], fc1_bias[None], pf_own, pf_other, pf_own, pf_other)
    fc2_grad = scatter(fc2g_own, fc2g_other)

    column_blocks = pl.BlockSpec((COLUMNS, thin, width), lambda i, *_: (0, 0, i))
    hg, fc1_sums, fc1g_own, fc1g_other = pl.pallas_call(
        partial(hidden_back_kernel, tile=tile),
        grid_spec=pltpu.PrefetchScalarGridSpec(
            num_scalar_prefetch=1,
            grid=(tiles,),
            in_specs=[whole, whole, hidden_tile, fc2_blocks, fc2_blocks],
            out_specs=[hidden_tile, hidden_vec, column_blocks, column_blocks],
            scratch_shapes=[wide_scr],
        ),
        out_shape=[s((rows, hidden), BF16), s((1, hidden), F32)] + [s((COLUMNS, thin, hidden), BF16)] * 2,
        compiler_params=params(56),
    )(sc, b2g, n2, slope, fc2_own, fc2_other)
    fc1_grad = scatter(fc1g_own, fc1g_other)

    mg, b1g, ag, middle_sums = pl.pallas_call(
        partial(middle_back_kernel, tile=tile),
        grid_spec=pltpu.PrefetchScalarGridSpec(
            num_scalar_prefetch=1,
            grid=(tiles,),
            in_specs=[hidden_tile, fc1_blocks, fc1_blocks, proj_blocks, proj_blocks, whole, whole, whole, vec2, vec2],
            out_specs=[whole, whole, whole, full((4, width))],
            scratch_shapes=[pltpu.VMEM((rows, width), F32), thin_scr, thin_scr],
        ),
        out_shape=[s((rows, width), F32), s((rows, width), BF16), s((rows, width), BF16), s((4, width), F32)],
        compiler_params=params(56),
    )(sc, hg, pf_own, pf_other, pf_own, pf_other, b1, x, up, norm_gain, layer_scale)

    pg, proj_sums = pl.pallas_call(
        partial(attend_back_kernel, slot=slot, head=head),
        grid_spec=pltpu.PrefetchScalarGridSpec(
            num_scalar_prefetch=1,
            grid=(rows // tile,),
            in_specs=[by_tile(3 * width), by_tile(width)],
            out_specs=[by_tile(3 * width), full((1, 3 * width))],
        ),
        out_shape=[s((rows, 3 * width), BF16), s((1, 3 * width), F32)],
        compiler_params=params(),
    )(grid_flat, proj, ag)

    qp_own, qp_other = pl.pallas_call(
        weight_kernel,
        grid_spec=pltpu.PrefetchScalarGridSpec(
            num_scalar_prefetch=1,
            grid=(4,),
            in_specs=[whole, whole, pl.BlockSpec((rows, width), lambda i, *_: (0, jnp.minimum(i, 2))), whole],
            out_specs=[column_blocks, column_blocks],
        ),
        out_shape=[s((COLUMNS, thin, 4 * width), BF16)] * 2,
        compiler_params=params(),
    )(sc, n1, att, pg, b1g)
    qp_grad = scatter(qp_own, qp_other)

    input_grad, input_sums = pl.pallas_call(
        partial(input_back_kernel, images=images),
        grid_spec=pltpu.PrefetchScalarGridSpec(
            num_scalar_prefetch=2,
            grid=(packs,),
            in_specs=[pl.BlockSpec((pack, 3 * width), lambda i, *_: (i, 0)), full((COLUMNS, thin, 3 * width)), full((COLUMNS, thin, 3 * width)), by_pack, by_pack, vec2],
            out_specs=[by_pack, vec2],
            scratch_shapes=[pltpu.VMEM((COLUMNS, 2, thin, 3 * width), BF16)],
        ),
        out_shape=[s((rows, width), F32), s((2, width), F32)],
        compiler_params=params(),
    )(grid_flat, sc, pg, qkv_own, qkv_other, x, mg, norm_gain)

    layer_out, out_sums = pl.pallas_call(
        partial(layer_out_kernel, images=images),
        grid_spec=pltpu.PrefetchScalarGridSpec(
            num_scalar_prefetch=2,
            grid=(tiles,),
            in_specs=[hidden_tile, fc2_blocks, fc2_blocks, whole, whole, whole, vec2, vec1],
            out_specs=[whole, vec1],
            scratch_shapes=[pltpu.VMEM((rows, width), F32), wide_scr],
        ),
        out_shape=[s((rows, width), BF16), s((1, width), F32)],
        compiler_params=params(),
    )(grid_flat, sc, act, fc2_own, fc2_other, x, b1, up, layer_scale, fc2_bias[None])

    sums = jnp.concatenate(
        [
            input_sums[0:1],
            middle_sums[2:3],
            input_sums[1:2],
            middle_sums[3:4],
            proj_sums[:, :width],
            proj_sums[:, 2 * width :],
            middle_sums[1:2],
            fc2_sums,
            middle_sums[0:1],
            out_sums,
            fc1_sums.reshape(tiles, width),
        ],
        axis=0,
    )
    sums = reduce_all(sums)
    return (
        layer_out,
        input_grad,
        qp_grad[:, : 3 * width].reshape(-1, row_width),
        qp_grad[:, 3 * width :].reshape(-1, row_width),
        fc1_grad.reshape(-1, row_width),
        fc2_grad.reshape(-1, row_width),
        sums[0:2],
        sums[2:4],
        sums[4:6],
        sums[6],
        sums[10:].reshape(-1),
        sums[7],
        sums[8:10],
    )


def solution(mesh):
    split = P(AXES, None)
    return jax.shard_map(
        body,
        mesh=mesh,
        in_specs=(split, P(AXES, None, None)) + (split,) * 4 + (P(),) * 7 + (split,),
        out_specs=(split,) * 6 + (P(),) * 7,
        check_vma=False,
    )
```

```python
from functools import partial

import jax
import jax.numpy as jnp
from jax import lax
from jax.experimental import pallas as pl
from jax.experimental.pallas import tpu as pltpu
from jax.sharding import PartitionSpec as P

H = 12
PREFIX = 5
EPSILON = 1e-06
NEGATIVE = -1e30
AXES = ("wide", "narrow")
COLUMNS = 8
BF16 = jnp.bfloat16
F32 = jnp.float32


def dot(a, b):
    return lax.dot_general(a, b, (((1,), (0,)), ((), ())), preferred_element_type=F32)


def dot_nt(a, b):
    return lax.dot_general(a, b, (((1,), (1,)), ((), ())), preferred_element_type=F32)


def dot_tn(a, b):
    return lax.dot_general(a, b, (((0,), (0,)), ((), ())), preferred_element_type=F32)


def call(kernel, grid, scalars, ins, outs, scratch=(), after=(), mib=48):
    n = len(scalars) + len(ins)

    def run(*refs):
        kernel(*refs[:n], *refs[n + len(after) :])

    anywhere = pl.BlockSpec(memory_space=pl.ANY)
    return pl.pallas_call(
        run,
        grid_spec=pltpu.PrefetchScalarGridSpec(
            num_scalar_prefetch=len(scalars),
            grid=grid,
            in_specs=[spec for _, spec in ins] + [anywhere] * len(after),
            out_specs=[spec for _, _, spec in outs],
            scratch_shapes=list(scratch),
        ),
        out_shape=[jax.ShapeDtypeStruct(shape, kind) for shape, kind, _ in outs],
        compiler_params=pltpu.CompilerParams(vmem_limit_bytes=mib * 2**20),
        cost_estimate=pl.CostEstimate(flops=1, bytes_accessed=1, transcendentals=0),
    )(*scalars, *(array for array, _ in ins), *after)


def full(shape):
    return pl.BlockSpec(shape, lambda *_: (0,) * len(shape))


def standardize(v):
    centered = v - jnp.mean(v, axis=-1, keepdims=True)
    inverse = lax.rsqrt(jnp.mean(centered * centered, axis=-1, keepdims=True) + EPSILON)
    return centered * inverse, inverse


def standardize_back(grad, scaled, inverse):
    return inverse * (
        grad
        - jnp.mean(grad, axis=-1, keepdims=True)
        - scaled * jnp.mean(grad * scaled, axis=-1, keepdims=True)
    )


def length_of(grid_ref, image):
    return PREFIX + grid_ref[2 * image] * grid_ref[2 * image + 1]


def spans(grid_ref, pack, images):
    found, start = [], 0
    for i in range(images):
        length = length_of(grid_ref, pack * images + i)
        found.append((start, length))
        start = start + length
    return found


def join(scr, core, own, other):
    for i in range(scr.shape[0]):
        scr[i, core] = own[i]
        scr[i, 1 - core] = other[i]
    blocks, cores, rows, columns = scr.shape
    return scr[...].reshape(blocks * cores * rows, columns)


def part(core, matrix, own, other):
    blocks, rows, columns = own.shape
    cut = matrix.reshape(blocks, 2, rows, columns)
    own[...] = jnp.where(core == 0, cut[:, 0], cut[:, 1])
    other[...] = jnp.where(core == 0, cut[:, 1], cut[:, 0])


def prepare_kernel(grid_ref, tok, cot, gain, bias, ls, x, n1, up, b2g, sums, *, images):
    pack = pl.program_id(0)
    slot = tok.shape[0] // images
    row = lax.broadcasted_iota(jnp.int32, (slot, tok.shape[0]), 0)
    column = lax.broadcasted_iota(jnp.int32, (slot, tok.shape[0]), 1)
    total = jnp.zeros((1, tok.shape[1]), F32)
    for i, (start, length) in enumerate(spans(grid_ref, pack, images)):
        place = jnp.where((column - row == start) & (row < length), 1.0, 0.0).astype(BF16)
        rows = pl.ds(i * slot, slot)
        moved = dot(place, tok[...])
        x[rows] = moved.astype(BF16)
        scaled, _ = standardize(moved)
        n1[rows] = (scaled * gain[0:1] + bias[0:1]).astype(BF16)
        upstream = dot(place, cot[...])
        up[rows] = upstream.astype(BF16)
        low = (ls[1:2] * upstream).astype(BF16)
        b2g[rows] = low
        total = total + jnp.sum(low.astype(F32), axis=0, keepdims=True)

    @pl.when(pack == 0)
    def _():
        sums[...] = jnp.zeros_like(sums)

    sums[...] += total


def unplace(grid_ref, pack, images, size):
    slot = size // images
    row = lax.broadcasted_iota(jnp.int32, (size, slot), 0)
    column = lax.broadcasted_iota(jnp.int32, (size, slot), 1)
    return jnp.concatenate(
        [
            jnp.where((row - column == start) & (column < length), 1.0, 0.0).astype(BF16)
            for start, length in spans(grid_ref, pack, images)
        ],
        axis=1,
    )


def lanes(rows, width, head):
    return lax.broadcasted_iota(jnp.int32, (rows, width), 1) < head


def stacked(v, low):
    zero = jnp.zeros_like(v)
    return jnp.concatenate([jnp.where(low, v, zero), jnp.where(low, zero, v)], axis=0)


def softmax(scores, column_ok):
    masked = jnp.where(column_ok, scores, NEGATIVE)
    exponent = jnp.exp(masked - jnp.max(masked, axis=1, keepdims=True))
    return exponent * (1.0 / jnp.sum(exponent, axis=1, keepdims=True))


def attend_kernel(grid_ref, sc, n1, own, other, offset, proj, att, scr, *, slot, head):
    step = pl.program_id(0)
    width = n1.shape[1]
    per = n1.shape[0] // slot
    pair = 2 * head

    @pl.when(step == 0)
    def _():
        join(scr, sc[0], own, other)

    w = scr[...].reshape(width, 3 * width)
    proj[...] = (dot(n1[...], w) + offset[...]).astype(BF16)
    low = lanes(slot, pair, head)
    key_at = lax.broadcasted_iota(jnp.int32, (slot, slot), 1)
    for i in range(per):
        ok = key_at < length_of(grid_ref, step * per + i)
        rows = pl.ds(i * slot, slot)
        for j in range(width // pair):
            q, k, v = (proj[rows, pl.ds(t * width + j * pair, pair)] for t in range(3))
            scores = dot_nt(q, stacked(k, low)) * head ** (-0.5)
            p0 = softmax(scores[:, :slot], ok)
            p1 = softmax(scores[:, slot:], ok)
            p = jnp.concatenate([p0, p1], axis=1).astype(BF16)
            att[rows, pl.ds(j * pair, pair)] = dot(p, stacked(v, low)).astype(BF16)


def hidden_kernel(sc, att, x, b2g, gain, bias, ls, proj_bias, fc1_bias, po, ps, fo, fs, b1, n2, act, slope, go, gs, pscr, fscr, *, tile):
    core = sc[0]

    @pl.when(pl.program_id(0) == 0)
    def _():
        w = join(pscr, core, po, ps)
        for r in range(0, att.shape[0], tile):
            rows = pl.ds(r, tile)
            branch = dot(att[rows], w) + proj_bias[...]
            b1[rows] = branch
            scaled, _ = standardize(x[rows].astype(F32) + ls[0:1] * branch)
            n2[rows] = (scaled * gain[1:2] + bias[1:2]).astype(BF16)

    w = join(fscr, core, fo, fs)
    for r in range(0, att.shape[0], tile):
        rows = pl.ds(r, tile)
        hidden = dot(n2[rows], w) + fc1_bias[...]
        normal = 0.5 * (1.0 + lax.erf(hidden * 0.5**0.5))
        act[rows] = (hidden * normal).astype(BF16)
        slope[rows] = normal + hidden * ((0.5 / jnp.pi) ** 0.5 * jnp.exp(-0.5 * hidden * hidden))
    part(core, dot_tn(act[...], b2g[...]).astype(BF16), go, gs)


def hidden_back_kernel(sc, b2g, n2, slope, fc2, hg, sums, go, gs, *, tile):
    core = sc[0]
    w = fc2[...]
    total = jnp.zeros(sums.shape, F32)
    for r in range(0, b2g.shape[0], tile):
        rows = pl.ds(r, tile)
        low = (dot_nt(b2g[rows], w) * slope[rows]).astype(BF16)
        hg[rows] = low
        total = total + jnp.sum(low.astype(F32), axis=0, keepdims=True)
    sums[...] = total
    part(core, dot_tn(n2[...], hg[...]).astype(BF16), go, gs)


def middle_back_kernel(sc, hg, fo, fs, po, ps, b1, x, up, gain, ls, mg, b1g, ag, sums, acc, fscr, pscr, *, tile):
    core = sc[0]
    step = pl.program_id(0)
    w = join(fscr, core, fo, fs)

    @pl.when(step == 0)
    def _():
        acc[...] = dot_nt(hg[...], w)

    @pl.when(step > 0)
    def _():
        acc[...] += dot_nt(hg[...], w)

    @pl.when(step == pl.num_programs(0) - 1)
    def _():
        wp = join(pscr, core, po, ps)
        totals = [jnp.zeros((1, x.shape[1]), F32) for _ in range(4)]
        for r in range(0, x.shape[0], tile):
            rows = pl.ds(r, tile)
            branch = b1[rows]
            scaled, inverse = standardize(x[rows].astype(F32) + ls[0:1] * branch)
            grad = acc[rows]
            back = up[rows].astype(F32) + standardize_back(grad * gain[1:2], scaled, inverse)
            mg[rows] = back
            low = (ls[0:1] * back).astype(BF16)
            b1g[rows] = low
            ag[rows] = dot_nt(low, wp).astype(BF16)
            terms = (back * branch, low.astype(F32), grad * scaled, grad)
            totals = [t + jnp.sum(v, axis=0, keepdims=True) for t, v in zip(totals, terms)]
        sums[...] = jnp.concatenate(totals, axis=0)


def attend_back_kernel(grid_ref, proj, ag, pg, sums, *, slot, head):
    step = pl.program_id(0)
    width = ag.shape[1]
    per = ag.shape[0] // slot
    pair = 2 * head
    factor = head ** (-0.5)
    low = lanes(slot, pair, head)
    key_at = lax.broadcasted_iota(jnp.int32, (slot, slot), 1)
    for i in range(per):
        ok = key_at < length_of(grid_ref, step * per + i)
        rows = pl.ds(i * slot, slot)
        for j in range(width // pair):
            q, k, v = (proj[rows, pl.ds(t * width + j * pair, pair)] for t in range(3))
            out = ag[rows, pl.ds(j * pair, pair)]
            k2 = stacked(k, low)
            scores = dot_nt(q, k2) * factor
            pull = dot_nt(out, stacked(v, low))
            ps, ss = [], []
            for half in (slice(0, slot), slice(slot, 2 * slot)):
                p = softmax(scores[:, half], ok)
                g = pull[:, half]
                ps.append(p)
                ss.append(p * (g - jnp.sum(g * p, axis=1, keepdims=True)))
            p = jnp.concatenate(ps, axis=1).astype(BF16)
            s = jnp.concatenate(ss, axis=1).astype(BF16)
            dq = dot(s, k2) * factor
            dk = dot_tn(s, q) * factor
            dv = dot_tn(p, out)
            dk = jnp.where(low, dk[:slot], dk[slot:])
            dv = jnp.where(low, dv[:slot], dv[slot:])
            for t, d in enumerate((dq, dk, dv)):
                pg[rows, pl.ds(t * width + j * pair, pair)] = d.astype(BF16)

    @pl.when(step == 0)
    def _():
        sums[...] = jnp.zeros_like(sums)

    sums[...] += jnp.sum(pg[...].astype(F32), axis=0, keepdims=True)


def weight_kernel(sc, n1, att, pg, b1g, go, gs):
    step = pl.program_id(0)
    last = pl.num_programs(0) - 1

    @pl.when(step < last)
    def _():
        part(sc[0], dot_tn(n1[...], pg[...]).astype(BF16), go, gs)

    @pl.when(step == last)
    def _():
        part(sc[0], dot_tn(att[...], b1g[...]).astype(BF16), go, gs)


def input_back_kernel(grid_ref, sc, pg, own, other, x, mg, gain, out, sums, scr, *, images):
    pack = pl.program_id(0)

    @pl.when(pack == 0)
    def _():
        join(scr, sc[0], own, other)
        sums[...] = jnp.zeros_like(sums)

    width = x.shape[1]
    grad = dot_nt(pg[...], scr[...].reshape(width, 3 * width))
    scaled, inverse = standardize(x[...].astype(F32))
    back = mg[...] + standardize_back(grad * gain[0:1], scaled, inverse)
    sums[...] += jnp.concatenate(
        [jnp.sum(grad * scaled, axis=0, keepdims=True), jnp.sum(grad, axis=0, keepdims=True)], axis=0
    )
    place = unplace(grid_ref, pack, images, x.shape[0])
    high = back.astype(BF16)
    rest = back - high.astype(F32)
    mid = rest.astype(BF16)
    lowest = (rest - mid.astype(F32)).astype(BF16)
    out[...] = dot(place, high) + dot(place, mid) + dot(place, lowest)


def layer_out_kernel(grid_ref, act, fc2, x, b1, up, ls, fc2_bias, out, sums, acc, *, images):
    step = pl.program_id(0)
    w = fc2[...]

    @pl.when(step == 0)
    def _():
        acc[...] = dot(act[...], w)

    @pl.when(step > 0)
    def _():
        acc[...] += dot(act[...], w)

    @pl.when(step == pl.num_programs(0) - 1)
    def _():
        size = out.shape[0] // (grid_ref.shape[0] // (2 * images))
        total = jnp.zeros(sums.shape, F32)
        for pack in range(out.shape[0] // size):
            rows = pl.ds(pack * size, size)
            branch = acc[rows] + fc2_bias[...]
            total = total + jnp.sum(up[rows].astype(F32) * branch, axis=0, keepdims=True)
            middle = x[rows].astype(F32) + ls[0:1] * b1[rows]
            result = (middle + ls[1:2] * branch).astype(BF16)
            place = unplace(grid_ref, pack, images, size)
            out[rows] = dot(place, result).astype(BF16)
        sums[...] = total


Y, CORE, X, Z = 1, 2, 4, 8
ANY = pl.BlockSpec(memory_space=pl.ANY)


def swap(v, mask):
    return lax.ppermute(v, AXES, [(i, i ^ mask) for i in range(32)])


def move(plan, count, sc, ins, outs, after):
    def kernel(*refs):
        sem = refs[-1]
        copies = [pltpu.make_async_copy(a, b, sem.at[i]) for i, (a, b) in enumerate(plan(*refs[:-1]))]
        for copy in copies:
            copy.start()
        for copy in copies:
            copy.wait()

    return call(
        kernel,
        (1,),
        (sc,),
        [(v, ANY) for v in ins],
        [(shape, BF16, ANY) for shape in outs],
        [pltpu.SemaphoreType.DMA((count,))],
        after,
        mib=8,
    )


def gather_line(block):
    return [block] + [swap(block, Z * k) for k in (1, 2, 3)]


def gather_stack(line, sc, after):
    rows, columns = line[0].shape
    half = columns // 2

    def plan(sc, *refs):
        return [
            (refs[k].at[:, pl.ds(h * half, half)], refs[4 + h].at[k]) for k in range(4) for h in range(2)
        ]

    return move(plan, 8, sc, line, [(4, rows, half)] * 2, after)


def gather_pair(a, b, sc, after):
    def plan(sc, a, xa, b, yb, left, right):
        return [(a, left.at[0]), (xa, left.at[1]), (b, right.at[0]), (yb, right.at[1])]

    return move(plan, 4, sc, (a, swap(a, X), b, swap(b, Y)), [(2,) + a.shape] * 2, after)


def gather_place(left, right, sc, after):
    _, _, rows, half = left.shape

    def plan(sc, left, other_left, right, other_right, out):
        pairs = []
        for i in range(2):
            for j in range(2):
                for k in range(4):
                    z, x, y = sc[3] ^ k, sc[1], sc[2]
                    pairs.append(((left, other_left)[j].at[i, k], out.at[z, x ^ i, y ^ j, :, pl.ds(0, half)]))
                    pairs.append(((right, other_right)[j].at[i, k], out.at[z, x ^ j, y ^ i, :, pl.ds(half, half)]))
        return pairs

    [own] = move(plan, 32, sc, (left, swap(left, Y), right, swap(right, X)), [(4, 2, 2, rows, 2 * half)], after)
    return own.reshape(COLUMNS, 2 * rows, 2 * half), swap(own, CORE).reshape(COLUMNS, 2 * rows, 2 * half)


def add(a, b):
    return a.astype(F32) + b.astype(F32)


def fold_core(own, other, sc, after, order):
    _, rows2, columns = own.shape
    rows = rows2 // 2
    widths = {"yx": (columns, 0), "xy": (0, columns), "both": (columns // 2, columns // 2)}[order]
    by_z = pl.BlockSpec((1, 2, 2, rows, columns), lambda i, *_: (i, 0, 0, 0, 0))

    def kernel(sc, own, got, *outs):
        at = 0
        for first, width in enumerate(widths):
            if not width:
                continue
            cut = pl.ds(0 if first == 0 else widths[0], width)
            for i in range(2):
                for flip in range(2):
                    x, y = (i, sc[2] ^ flip) if first == 0 else (sc[1] ^ flip, i)
                    outs[at + flip][0, i] = add(own[0, x, y, :, cut], got[0, x, y, :, cut]).astype(BF16)
            at += 2

    got = swap(other, CORE).reshape(4, 2, 2, rows, columns)
    outs = [
        ((4, 2, rows, w), BF16, pl.BlockSpec((1, 2, rows, w), lambda i, *_: (i, 0, 0, 0)))
        for w in widths
        if w
        for _ in range(2)
    ]
    out = call(kernel, (4,), (sc,), [(own.reshape(4, 2, 2, rows, columns), by_z), (got, by_z)], outs, (), after)
    masks = [mask for mask, w in zip((Y, X), widths) if w]
    return [(out[2 * i], out[2 * i + 1], mask) for i, mask in enumerate(masks)]


def fold_first(parts, sc, after):
    ins, outs = [], []
    for keep, send, mask in parts:
        _, _, rows, width = keep.shape
        ins += [(keep, full(keep.shape)), (swap(send, mask), full(keep.shape))]
        outs += [((4, rows, width), BF16, full((4, rows, width)))] * 2

    def kernel(sc, *refs):
        ins, outs = refs[: 2 * len(parts)], refs[2 * len(parts) :]
        for n, (_, _, mask) in enumerate(parts):
            for z in range(4):
                for flip in range(2):
                    at = sc[1 if mask == Y else 2] ^ flip
                    outs[2 * n + flip][z] = add(ins[2 * n][z, at], ins[2 * n + 1][z, at]).astype(BF16)

    out = call(kernel, (1,), (sc,), ins, outs, (), after)
    return [(out[2 * i], out[2 * i + 1], X + Y - mask) for i, (_, _, mask) in enumerate(parts)]


def fold_second(parts, sc, after):
    ins = []
    for keep, send, mask in parts:
        ins += [(keep, full(keep.shape)), (swap(send, mask), full(keep.shape))]
    rows = min(keep.shape[1] for keep, _, _ in parts)
    pieces = []
    for n, (keep, _, _) in enumerate(parts):
        for first in range(0, keep.shape[1], rows):
            at = sum(width for _, _, _, width in pieces)
            pieces.append((n, first, at, keep.shape[2]))
    shape = (rows, sum(width for _, _, _, width in pieces))

    def kernel(sc, *refs):
        ins, outs = refs[: 2 * len(parts)], refs[2 * len(parts) :]
        for k, to in enumerate(outs):
            z = sc[3] ^ k
            for n, first, at, width in pieces:
                cut = pl.ds(first, rows)
                to[:, pl.ds(at, width)] = add(ins[2 * n][z, cut], ins[2 * n + 1][z, cut]).astype(to.dtype)

    outs = [(shape, F32, full(shape))] + [(shape, BF16, full(shape))] * 3
    return call(kernel, (1,), (sc,), ins, outs, (), after)


def fold_last(parts, after):
    keep, *sends = parts
    ins = [(keep, full(keep.shape))] + [(swap(v, Z * k), full(keep.shape)) for k, v in zip((1, 2, 3), sends)]

    def kernel(keep, r1, r2, r3, out):
        out[...] = keep[...] + (r1[...].astype(F32) + r2[...].astype(F32) + r3[...].astype(F32))

    return call(kernel, (1,), (), ins, [(keep.shape, F32, full(keep.shape))], (), after)[0]


def reduce_swaps(v):
    for mask in (CORE, Y, X, Z, 2 * Z):
        v = v + swap(v, mask)
    return v


def body(
    tokens,
    patch_grid,
    qkv_rows,
    proj_rows,
    fc1_rows,
    fc2_rows,
    norm_gain,
    norm_bias,
    qv_bias,
    proj_bias,
    fc1_bias,
    fc2_bias,
    layer_scale,
    cotangent,
):
    rows, width = tokens.shape
    packs, images, _ = patch_grid.shape
    pack = rows // packs
    slot = pack // images
    head = width // H
    hidden = fc1_bias.shape[0]
    row_width = qkv_rows.shape[1]
    tiles = hidden // width
    tile = min(256, rows)
    swaps = lax.axis_size("wide") == 16 and lax.axis_size("narrow") == 2
    if swaps:
        me = lax.axis_index(AXES)
        sc = jnp.stack([me // CORE % 2, me // X % 2, me % 2, me // Z]).astype(jnp.int32)
    else:
        sc = jnp.zeros((4,), jnp.int32)
    grid_flat = patch_grid.reshape(-1)
    thin, wide_rows = width // (2 * COLUMNS), hidden // (2 * COLUMNS)
    per_tile = COLUMNS // tiles

    by_pack = pl.BlockSpec((pack, width), lambda i, *_: (i, 0))
    by_tile = lambda w: pl.BlockSpec((tile, w), lambda i, *_: (i, 0))
    whole = full((rows, width))
    proj_blocks = pl.BlockSpec((COLUMNS, thin, width), lambda i, *_: (0, 0, 0))
    fc1_blocks = pl.BlockSpec((COLUMNS, thin, width), lambda i, *_: (0, 0, 1 + i))
    fc2_blocks = pl.BlockSpec((per_tile, wide_rows, width), lambda i, *_: (i, 0, 0))
    fc2_tile = pl.BlockSpec((width, width), lambda i, *_: (i, 0))
    column_blocks = pl.BlockSpec((COLUMNS, thin, width), lambda i, *_: (0, 0, i))
    hidden_tile = pl.BlockSpec((rows, width), lambda i, *_: (0, i))
    thin_scr = pltpu.VMEM((COLUMNS, 2, thin, width), BF16)
    vec1, vec2 = full((1, width)), full((2, width))
    hidden_vec = pl.BlockSpec((1, width), lambda i, *_: (0, i))
    qkv_blocks = full((COLUMNS, thin, 3 * width))

    qkv_block = qkv_rows.reshape(-1, 3 * width)
    both_block = jnp.concatenate([proj_rows.reshape(-1, width), fc1_rows.reshape(-1, hidden)], axis=1)
    fc2 = lax.all_gather(fc2_rows.reshape(-1, width), AXES, axis=0, tiled=True)

    x, n1, up, b2g, fc2_sums = call(
        partial(prepare_kernel, images=images),
        (packs,),
        (grid_flat,),
        [(tokens, by_pack), (cotangent, by_pack), (norm_gain, vec2), (norm_bias, vec2), (layer_scale, vec2)],
        [((rows, width), BF16, by_pack)] * 4 + [((1, width), F32, vec1)],
    )

    if swaps:
        qkv_ab = gather_stack(gather_line(qkv_block), sc, [fc2_sums])
        both_line = gather_line(both_block)
        qkv_pair = gather_pair(*qkv_ab, sc, [])
        both_ab = gather_stack(both_line, sc, [qkv_pair[0]])
        qkv_own, qkv_other = gather_place(*qkv_pair, sc, [both_ab[0]])
        both_pair = gather_pair(*both_ab, sc, [qkv_own])
        ready = [both_pair[0]]
    else:
        halves = lambda v: v.reshape(COLUMNS, 2, -1, v.shape[1]).transpose(1, 0, 2, 3)
        qkv_own, qkv_other = halves(lax.all_gather(qkv_block, AXES, axis=0, tiled=True))
        pf_own, pf_other = halves(lax.all_gather(both_block, AXES, axis=0, tiled=True))
        ready = []

    offset = jnp.concatenate([qv_bias[0], jnp.zeros_like(qv_bias[0]), qv_bias[1]])[None]
    proj, att = call(
        partial(attend_kernel, slot=slot, head=head),
        (rows // tile,),
        (grid_flat, sc),
        [(n1, by_tile(width)), (qkv_own, qkv_blocks), (qkv_other, qkv_blocks), (offset, full((1, 3 * width)))],
        [((rows, 3 * width), BF16, by_tile(3 * width)), ((rows, width), BF16, by_tile(width))],
        [pltpu.VMEM((COLUMNS, 2, thin, 3 * width), BF16)],
        ready,
    )
    if swaps:
        pf_own, pf_other = gather_place(*both_pair, sc, [att])

    b1, n2, act, slope, fc2g_own, fc2g_other = call(
        partial(hidden_kernel, tile=tile),
        (tiles,),
        (sc,),
        [(att, whole), (x, whole), (b2g, whole), (norm_gain, vec2), (norm_bias, vec2), (layer_scale, vec2)]
        + [(proj_bias[None], vec1), (fc1_bias[None], hidden_vec)]
        + [(pf_own, proj_blocks), (pf_other, proj_blocks), (pf_own, fc1_blocks), (pf_other, fc1_blocks)],
        [((rows, width), F32, whole), ((rows, width), BF16, whole)]
        + [((rows, hidden), BF16, hidden_tile), ((rows, hidden), F32, hidden_tile)]
        + [((COLUMNS, wide_rows, width), BF16, fc2_blocks)] * 2,
        [thin_scr, thin_scr],
    )

    hg, fc1_sums, fc1g_own, fc1g_other = call(
        partial(hidden_back_kernel, tile=tile),
        (tiles,),
        (sc,),
        [(b2g, whole), (n2, whole), (slope, hidden_tile), (fc2, fc2_tile)],
        [((rows, hidden), BF16, hidden_tile), ((1, hidden), F32, hidden_vec)]
        + [((COLUMNS, thin, hidden), BF16, column_blocks)] * 2,
    )
    chain = []
    if swaps:
        fc2_parts = fold_core(fc2g_own, fc2g_other, sc, [fc1_sums], "yx")
        chain = [fc2_parts[0][0]]

    mg, b1g, ag, middle_sums = call(
        partial(middle_back_kernel, tile=tile),
        (tiles,),
        (sc,),
        [(hg, hidden_tile), (pf_own, fc1_blocks), (pf_other, fc1_blocks), (pf_own, proj_blocks), (pf_other, proj_blocks)]
        + [(b1, whole), (x, whole), (up, whole), (norm_gain, vec2), (layer_scale, vec2)],
        [((rows, width), F32, whole), ((rows, width), BF16, whole), ((rows, width), BF16, whole), ((4, width), F32, full((4, width)))],
        [pltpu.VMEM((rows, width), F32), thin_scr, thin_scr],
        chain,
    )
    chain = []
    if swaps:
        fc1_parts = fold_core(fc1g_own, fc1g_other, sc, [ag], "xy")
        chain = [fc1_parts[0][0]]

    pg, proj_sums = call(
        partial(attend_back_kernel, slot=slot, head=head),
        (rows // tile,),
        (grid_flat,),
        [(proj, by_tile(3 * width)), (ag, by_tile(width))],
        [((rows, 3 * width), BF16, by_tile(3 * width)), ((1, 3 * width), F32, full((1, 3 * width)))],
        (),
        chain,
    )
    chain = []
    if swaps:
        fc2_parts = fold_first(fc2_parts, sc, [pg])
        fc1_parts = fold_first(fc1_parts, sc, [fc2_parts[0][0]])
        chain = [fc1_parts[0][0]]

    qp_own, qp_other = call(
        weight_kernel,
        (4,),
        (sc,),
        [(n1, whole), (att, whole), (pg, pl.BlockSpec((rows, width), lambda i, *_: (0, jnp.minimum(i, 2)))), (b1g, whole)],
        [((COLUMNS, thin, 4 * width), BF16, column_blocks)] * 2,
        (),
        chain,
    )
    layer_out, out_sums = call(
        partial(layer_out_kernel, images=images),
        (tiles,),
        (grid_flat,),
        [(act, hidden_tile), (fc2, fc2_tile), (x, whole), (b1, whole), (up, whole), (layer_scale, vec2), (fc2_bias[None], vec1)],
        [((rows, width), BF16, whole), ((1, width), F32, vec1)],
        [pltpu.VMEM((rows, width), F32)],
        [qp_own],
    )
    chain = []
    if swaps:
        fc_parts = fold_second(fc1_parts + fc2_parts, sc, [layer_out])
        qp_parts = fold_core(qp_own, qp_other, sc, [fc_parts[0]], "both")
        chain = [qp_parts[0][0]]

    input_grad, input_sums = call(
        partial(input_back_kernel, images=images),
        (packs,),
        (grid_flat, sc),
        [(pg, pl.BlockSpec((pack, 3 * width), lambda i, *_: (i, 0))), (qkv_own, qkv_blocks), (qkv_other, qkv_blocks)]
        + [(x, by_pack), (mg, by_pack), (norm_gain, vec2)],
        [((rows, width), F32, by_pack), ((2, width), F32, vec2)],
        [pltpu.VMEM((COLUMNS, 2, thin, 3 * width), BF16)],
        chain,
    )

    sums = jnp.concatenate(
        [
            input_sums[0:1],
            middle_sums[2:3],
            input_sums[1:2],
            middle_sums[3:4],
            proj_sums[:, :width],
            proj_sums[:, 2 * width :],
            middle_sums[1:2],
            fc2_sums,
            middle_sums[0:1],
            out_sums,
            fc1_sums.reshape(tiles, width),
        ],
        axis=0,
    )
    if swaps:
        qp_parts = fold_first(qp_parts, sc, [input_grad])
        fc_grad = fold_last(fc_parts, [qp_parts[0][0]])
        qp_parts = fold_second(qp_parts, sc, [fc_grad])
        qp_grad = fold_last(qp_parts, [])
        fc1_grad = fc_grad[:, :hidden]
        fc2_grad = fc_grad[:, hidden:].reshape(-1, tiles, width).transpose(1, 0, 2).reshape(-1, width)
        sums = reduce_swaps(sums)
    else:

        def scatter(own, other):
            matrix = jnp.stack([own, other], axis=1).reshape(-1, own.shape[-1])
            return lax.psum_scatter(matrix, AXES, scatter_dimension=0, tiled=True).astype(F32)

        fc2_grad = scatter(fc2g_own, fc2g_other)
        fc1_grad = scatter(fc1g_own, fc1g_other)
        qp_grad = scatter(qp_own, qp_other)
        sums = lax.psum(sums, AXES)
    return (
        layer_out,
        input_grad,
        qp_grad[:, : 3 * width].reshape(-1, row_width),
        qp_grad[:, 3 * width :].reshape(-1, row_width),
        fc1_grad.reshape(-1, row_width),
        fc2_grad.reshape(-1, row_width),
        sums[0:2],
        sums[2:4],
        sums[4:6],
        sums[6],
        sums[10:].reshape(-1),
        sums[7],
        sums[8:10],
    )


def solution(mesh):
    split = P(AXES, None)
    return jax.shard_map(
        body,
        mesh=mesh,
        in_specs=(split, P(AXES, None, None)) + (split,) * 4 + (P(),) * 7 + (split,),
        out_specs=(split,) * 6 + (P(),) * 7,
        check_vma=False,
    )
```

```python
from functools import partial

import jax
import jax.numpy as jnp
from jax import lax
from jax.experimental import pallas as pl
from jax.experimental.pallas import tpu as pltpu
from jax.sharding import PartitionSpec as P

H = 12
PREFIX = 5
EPSILON = 1e-06
NEGATIVE = -1e30
AXES = ("wide", "narrow")
COLUMNS = 8
BF16 = jnp.bfloat16
F32 = jnp.float32


def dot(a, b):
    return lax.dot_general(a, b, (((1,), (0,)), ((), ())), preferred_element_type=F32)


def dot_nt(a, b):
    return lax.dot_general(a, b, (((1,), (1,)), ((), ())), preferred_element_type=F32)


def dot_tn(a, b):
    return lax.dot_general(a, b, (((0,), (0,)), ((), ())), preferred_element_type=F32)


TOKEN = (8, 128)


def call(kernel, grid, scalars, ins, outs, scratch=(), after=(), mib=36):
    n, m = len(scalars) + len(ins), len(outs)

    def run(*refs):
        rest = refs[n + len(after) :]
        rest[m][...] = jnp.zeros(TOKEN, F32)
        kernel(*refs[:n], *rest[:m], *rest[m + 1 :])

    anywhere = pl.BlockSpec(memory_space=pl.ANY)
    return pl.pallas_call(
        run,
        grid_spec=pltpu.PrefetchScalarGridSpec(
            num_scalar_prefetch=len(scalars),
            grid=grid,
            in_specs=[spec for _, spec in ins] + [anywhere] * len(after),
            out_specs=[out[2] for out in outs] + [full(TOKEN)],
            scratch_shapes=list(scratch),
        ),
        out_shape=[
            pltpu.HBM(out[0], out[1]) if len(out) > 3 else jax.ShapeDtypeStruct(out[0], out[1]) for out in outs
        ]
        + [jax.ShapeDtypeStruct(TOKEN, F32)],
        compiler_params=pltpu.CompilerParams(vmem_limit_bytes=mib * 2**20),
        cost_estimate=pl.CostEstimate(flops=1, bytes_accessed=1, transcendentals=0),
    )(*scalars, *(array for array, _ in ins), *after)


def far(v):
    return pltpu.with_memory_space_constraint(v, pltpu.HBM)


def full(shape):
    return pl.BlockSpec(shape, lambda *_: (0,) * len(shape), pipeline_mode=pl.Buffered(1))


def standardize(v):
    centered = v - jnp.mean(v, axis=-1, keepdims=True)
    inverse = lax.rsqrt(jnp.mean(centered * centered, axis=-1, keepdims=True) + EPSILON)
    return centered * inverse, inverse


def standardize_back(grad, scaled, inverse):
    return inverse * (
        grad
        - jnp.mean(grad, axis=-1, keepdims=True)
        - scaled * jnp.mean(grad * scaled, axis=-1, keepdims=True)
    )


def length_of(grid_ref, image):
    return PREFIX + grid_ref[2 * image] * grid_ref[2 * image + 1]


def spans(grid_ref, pack, images):
    found, start = [], 0
    for i in range(images):
        length = length_of(grid_ref, pack * images + i)
        found.append((start, length))
        start = start + length
    return found


def join(scr, core, own, other):
    for i in range(scr.shape[0]):
        scr[i, core] = own[i]
        scr[i, 1 - core] = other[i]
    blocks, cores, rows, columns = scr.shape
    return scr[...].reshape(blocks * cores * rows, columns)


def part(core, matrix, own, other):
    blocks, rows, columns = own.shape
    cut = matrix.reshape(blocks, 2, rows, columns)
    own[...] = jnp.where(core == 0, cut[:, 0], cut[:, 1])
    other[...] = jnp.where(core == 0, cut[:, 1], cut[:, 0])


def prepare_kernel(grid_ref, tok, cot, gain, bias, ls, x, n1, up, b2g, sums, *, images):
    pack = pl.program_id(0)
    slot = tok.shape[0] // images
    row = lax.broadcasted_iota(jnp.int32, (slot, tok.shape[0]), 0)
    column = lax.broadcasted_iota(jnp.int32, (slot, tok.shape[0]), 1)
    total = jnp.zeros((1, tok.shape[1]), F32)
    for i, (start, length) in enumerate(spans(grid_ref, pack, images)):
        place = jnp.where((column - row == start) & (row < length), 1.0, 0.0).astype(BF16)
        rows = pl.ds(i * slot, slot)
        moved = dot(place, tok[...])
        x[rows] = moved.astype(BF16)
        scaled, _ = standardize(moved)
        n1[rows] = (scaled * gain[0:1] + bias[0:1]).astype(BF16)
        upstream = dot(place, cot[...])
        up[rows] = upstream.astype(BF16)
        low = (ls[1:2] * upstream).astype(BF16)
        b2g[rows] = low
        total = total + jnp.sum(low.astype(F32), axis=0, keepdims=True)

    @pl.when(pack == 0)
    def _():
        sums[...] = jnp.zeros_like(sums)

    sums[...] += total


def unplace(grid_ref, pack, images, size):
    slot = size // images
    row = lax.broadcasted_iota(jnp.int32, (size, slot), 0)
    column = lax.broadcasted_iota(jnp.int32, (size, slot), 1)
    return jnp.concatenate(
        [
            jnp.where((row - column == start) & (column < length), 1.0, 0.0).astype(BF16)
            for start, length in spans(grid_ref, pack, images)
        ],
        axis=1,
    )


def pieces(rows, size=128):
    return [pl.ds(r, size) for r in range(0, rows, size)]


def eights(v):
    return jnp.sum(v.reshape(-1, 8, v.shape[1]), axis=0)


def column_sum(v):
    return jnp.sum(v, axis=0, keepdims=True)


def stacked(v, low):
    zero = jnp.zeros_like(v)
    return jnp.concatenate([jnp.where(low, v, zero), jnp.where(low, zero, v)], axis=0)


def attend_kernel(grid_ref, sc, n1, own, other, offset, proj, att, log_total, scr, *, slot, head):
    step = pl.program_id(0)
    width = n1.shape[1]
    per = n1.shape[0] // slot
    pair = 2 * head
    heads = width // head

    @pl.when(step == 0)
    def _():
        join(scr, sc[0], own, other)

    w = scr[...].reshape(width, 3 * width)
    proj[...] = (dot(n1[...], w) + offset[...]).astype(BF16)
    low = lax.broadcasted_iota(jnp.int32, (slot, pair), 1) < head
    key_at = lax.broadcasted_iota(jnp.int32, (slot, slot), 0)
    for i in range(per):
        ok = key_at < length_of(grid_ref, step * per + i)
        rows = pl.ds(i * slot, slot)
        for j in range(width // pair):
            q, k, v = (proj[rows, pl.ds(t * width + j * pair, pair)] for t in range(3))
            scores = dot_nt(stacked(k, low), q * jnp.asarray(head ** (-0.5), BF16))
            halves = []
            for h in range(2):
                masked = jnp.where(ok, scores[h * slot : (h + 1) * slot], NEGATIVE)
                top = jnp.max(masked, axis=0, keepdims=True)
                exponent = jnp.exp(masked - top)
                total = column_sum(exponent)
                halves.append((exponent * (1.0 / total)).astype(BF16))
                log_total[pl.ds(i * heads + 2 * j + h, 1)] = top + jnp.log(total)
            att[rows, pl.ds(j * pair, pair)] = dot_tn(jnp.concatenate(halves, axis=0), stacked(v, low)).astype(BF16)


def middle_kernel(sc, att, x, gain, bias, ls, proj_bias, own, other, b1, n2, acc, scr):
    acc[...] = dot(att[...], join(scr, sc[0], own, other))
    for rows in pieces(acc.shape[0]):
        branch = acc[rows] + proj_bias[...]
        b1[rows] = branch
        scaled, _ = standardize(x[rows].astype(F32) + ls[0:1] * branch)
        n2[rows] = (scaled * gain[1:2] + bias[1:2]).astype(BF16)


def hidden_kernel(sc, n2, b2g, fc1_bias, own, other, act, slope, go, gs, scr):
    w1 = join(scr, sc[0], own, other)
    for rows in pieces(n2.shape[0], 256):
        hidden = dot(n2[rows], w1) + fc1_bias[...]
        normal = 0.5 * (1.0 + lax.erf(hidden * 0.5**0.5))
        act[rows] = (hidden * normal).astype(BF16)
        density = (0.5 / jnp.pi) ** 0.5 * jnp.exp(-0.5 * hidden * hidden)
        slope[rows] = normal + hidden * density
    part(sc[0], dot_tn(act[...], b2g[...]).astype(BF16), go, gs)


def hidden_back_kernel(sc, b2g, n2, slope, own, other, hg, sums, go, gs, n2t, scr):
    @pl.when(pl.program_id(0) == 0)
    def _():
        n2t[...] = n2[...].T

    w2 = join(scr, sc[0], own, other)
    total = jnp.zeros((8, sums.shape[1]), F32)
    for rows in pieces(b2g.shape[0], 256):
        low = (dot_nt(b2g[rows], w2) * slope[rows]).astype(BF16)
        hg[rows] = low
        total = total + eights(low.astype(F32))
    sums[...] = column_sum(total)
    part(sc[0], dot(n2t[...], hg[...]).astype(BF16), go, gs)


def middle_back_kernel(sc, hg, own, other, po, ps, b1, x, up, gain, ls, mg, b1g, ag, sums, acc, scr, pscr, *, tiles):
    step = pl.program_id(0)

    @pl.when(step == 0)
    def _():
        acc[...] = dot_nt(hg[...], join(scr, sc[0], own, other))

    @pl.when((step > 0) & (step < tiles))
    def _():
        acc[...] += dot_nt(hg[...], join(scr, sc[0], own, other))

    @pl.when(step == tiles)
    def _():
        join(pscr, sc[0], po, ps)
        sums[...] = jnp.zeros_like(sums)

    @pl.when(step >= tiles)
    def _():
        size = x.shape[0]
        totals = [jnp.zeros((8, x.shape[1]), F32) for _ in range(4)]
        for rows in pieces(size):
            branch = b1[rows]
            scaled, inverse = standardize(x[rows].astype(F32) + ls[0:1] * branch)
            grad = acc[pl.ds(pl.multiple_of((step - tiles) * size + rows.start, 128), rows.size)]
            back = up[rows].astype(F32) + standardize_back(grad * gain[1:2], scaled, inverse)
            mg[rows] = back
            low = (ls[0:1] * back).astype(BF16)
            b1g[rows] = low
            terms = (back * branch, low.astype(F32), grad * scaled, grad)
            totals = [t + eights(v) for t, v in zip(totals, terms)]
        ag[...] = dot_nt(b1g[...], pscr[...].reshape(x.shape[1], x.shape[1])).astype(BF16)
        sums[...] += jnp.concatenate([column_sum(t) for t in totals], axis=0)


def attend_back_kernel(grid_ref, proj, ag, log_total, pg, sums, *, slot, head):
    step = pl.program_id(0)
    width = ag.shape[1]
    per = ag.shape[0] // slot
    pair = 2 * head
    heads = width // head
    factor = head ** (-0.5)
    low = lax.broadcasted_iota(jnp.int32, (slot, pair), 1) < head
    key_at = lax.broadcasted_iota(jnp.int32, (slot, slot), 0)

    @pl.when(step == 0)
    def _():
        sums[...] = jnp.zeros_like(sums)

    for i in range(per):
        ok = key_at < length_of(grid_ref, step * per + i)
        rows = pl.ds(i * slot, slot)
        for j in range(width // pair):
            q, k, v = (proj[rows, pl.ds(t * width + j * pair, pair)] for t in range(3))
            out = ag[rows, pl.ds(j * pair, pair)]
            q = q * jnp.asarray(factor, BF16)
            k2 = stacked(k, low)
            scores = dot_nt(k2, q)
            pull = dot_nt(stacked(v, low), out)
            ps, ss = [], []
            for h in range(2):
                half = slice(h * slot, (h + 1) * slot)
                p = jnp.exp(jnp.where(ok, scores[half], NEGATIVE) - log_total[pl.ds(i * heads + 2 * j + h, 1)])
                g = pull[half]
                ps.append(p.astype(BF16))
                ss.append((p * (g - column_sum(g * p))).astype(BF16))
            s = jnp.concatenate(ss, axis=0)
            dq = dot_tn(s, k2) * factor
            dk = dot(s, q)
            dv = dot(jnp.concatenate(ps, axis=0), out)
            dk = jnp.where(low, dk[:slot], dk[slot:])
            dv = jnp.where(low, dv[:slot], dv[slot:])
            for t, d in enumerate((dq, dk, dv)):
                d = d.astype(BF16)
                columns = pl.ds(t * width + j * pair, pair)
                pg[rows, columns] = d
                if t != 1:
                    sums[:, columns] += eights(d.astype(F32))


def weight_kernel(sc, n1, att, pg, b1g, go, gs, n1t):
    step = pl.program_id(0)
    last = pl.num_programs(0) - 1

    @pl.when(step == 0)
    def _():
        n1t[...] = n1[...].T

    @pl.when(step < last)
    def _():
        part(sc[0], dot(n1t[...], pg[...]).astype(BF16), go, gs)

    @pl.when(step == last)
    def _():
        part(sc[0], dot_tn(att[...], b1g[...]).astype(BF16), go, gs)


def input_back_kernel(grid_ref, sc, pg, own, other, x, mg, gain, out, sums, scr, acc, high, mid, *, images):
    pack = pl.program_id(0)

    @pl.when(pack == 0)
    def _():
        join(scr, sc[0], own, other)
        sums[...] = jnp.zeros_like(sums)

    width = x.shape[1]
    acc[...] = dot_nt(pg[...], scr[...].reshape(width, 3 * width))
    totals = [jnp.zeros((8, width), F32) for _ in range(2)]
    for rows in pieces(acc.shape[0]):
        grad = acc[rows]
        scaled, inverse = standardize(x[rows].astype(F32))
        back = mg[rows] + standardize_back(grad * gain[0:1], scaled, inverse)
        totals = [t + eights(v) for t, v in zip(totals, (grad * scaled, grad))]
        big = back.astype(BF16)
        high[rows] = big
        mid[rows] = (back - big.astype(F32)).astype(BF16)
    sums[...] += jnp.concatenate([column_sum(t) for t in totals], axis=0)
    place = unplace(grid_ref, pack, images, x.shape[0])
    out[...] = dot(place, high[...]) + dot(place, mid[...])


def layer_out_kernel(grid_ref, sc, act, own, other, x, b1, up, ls, fc2_bias, out, sums, acc, result, scr, *, images, tiles):
    step = pl.program_id(0)

    @pl.when(step == 0)
    def _():
        acc[...] = dot(act[...], join(scr, sc[0], own, other))

    @pl.when((step > 0) & (step < tiles))
    def _():
        acc[...] += dot(act[...], join(scr, sc[0], own, other))

    @pl.when(step == tiles)
    def _():
        sums[...] = jnp.zeros_like(sums)

    @pl.when(step >= tiles)
    def _():
        pack, size = step - tiles, out.shape[0]
        total = jnp.zeros((8, x.shape[1]), F32)
        for rows in pieces(size):
            branch = acc[pl.ds(pl.multiple_of(pack * size + rows.start, 128), rows.size)] + fc2_bias[...]
            total = total + eights(up[rows].astype(F32) * branch)
            middle = x[rows].astype(F32) + ls[0:1] * b1[rows]
            result[rows] = (middle + ls[1:2] * branch).astype(BF16)
        out[...] = dot(unplace(grid_ref, pack, images, size), result[...]).astype(BF16)
        sums[...] += column_sum(total)


Y, CORE, X, Z = 1, 2, 4, 8


def swap(v, mask):
    return lax.ppermute(v, AXES, [(i, i ^ mask) for i in range(32)])


def move(plan, sc, ins, outs, after, mib=8):
    def kernel(*refs):
        for a, b in plan(*refs):
            b[...] = a[...]

    return call(
        kernel, (1,), (sc,), [(v, full(v.shape)) for v in ins], [(shape, BF16, full(shape)) for shape in outs], (), after, mib
    )


def gather_stack(first, *others, sc, after):
    near = jnp.concatenate([first, *others], axis=1)
    rows, columns = first.shape
    half = columns // 2
    line = (near, swap(near, Z), swap(first, 2 * Z), swap(first, 3 * Z))

    def plan(sc, *refs):
        pairs = [(refs[k].at[:, pl.ds(h * half, half)], refs[4 + h].at[k]) for k in range(4) for h in range(2)]
        at = columns
        for n, block in enumerate(others):
            cut = pl.ds(at, block.shape[1])
            pairs += [(refs[k].at[:, cut], refs[6 + n].at[k]) for k in range(2)]
            at += block.shape[1]
        return pairs

    return move(plan, sc, line, [(4, rows, half)] * 2 + [(2,) + block.shape for block in others], after)


def gather_rest(near, sc, after):
    _, rows, columns = near.shape
    half = columns // 2

    def plan(sc, near, distant, a, b):
        return [
            ((near, distant)[i].at[k, :, pl.ds(h * half, half)], (a, b)[h].at[2 * i + k])
            for i in range(2)
            for k in range(2)
            for h in range(2)
        ]

    return move(plan, sc, (near, swap(near, 2 * Z)), [(4, rows, half)] * 2, after)


def gather_pair(a, b, sc, after):
    def plan(sc, a, xa, b, yb, left, right):
        return [(a, left.at[0]), (xa, left.at[1]), (b, right.at[0]), (yb, right.at[1])]

    return move(plan, sc, (a, swap(a, X), b, swap(b, Y)), [(2,) + a.shape] * 2, after)


def gather_place(left, right, sc, after, runs=1):
    _, _, rows, half = left.shape
    width = 2 * half // runs

    def plan(sc, left, other_left, right, other_right, out):
        pairs = []
        for n, sides in enumerate(((left, other_left), (right, other_right))):
            for i in range(2):
                for j in range(2):
                    for k in range(4):
                        x, y = (i, j) if n == 0 else (j, i)
                        to = out.at[sc[3] ^ k, sc[1] ^ x, sc[2] ^ y]
                        if runs == 1:
                            pairs.append((sides[j].at[i, k], to.at[:, pl.ds(n * half, half)]))
                            continue
                        for r in range(runs // 2):
                            run = n * (runs // 2) + r
                            pairs.append((sides[j].at[i, k, :, pl.ds(r * width, width)], to.at[pl.ds(run * rows, rows)]))
        return pairs

    ins = [far(v) for v in (left, swap(left, Y), right, swap(right, X))]
    own, token = move(plan, sc, ins, [(4, 2, 2, runs * rows, width)], after, 12)
    shape = (COLUMNS, 2 * runs * rows, width)
    return own.reshape(shape), swap(own, CORE).reshape(shape), token


def add(a, b):
    return a.astype(F32) + b.astype(F32)


def fold_core(own, other, sc, after):
    _, rows2, columns = own.shape
    rows, half = rows2 // 2, columns // 2
    by_z = pl.BlockSpec((1, 2, 2, rows, columns), lambda i, *_: (i, 0, 0, 0, 0))
    to_z = pl.BlockSpec((1, 2, rows, half), lambda i, *_: (i, 0, 0, 0))
    left, right = pl.ds(0, half), pl.ds(half, half)

    def kernel(sc, own, got, ka, sa, kb, sb):
        for i in range(2):
            for a, b, flip in ((ka, kb, 0), (sa, sb, 1)):
                y, x = sc[2] ^ flip, sc[1] ^ flip
                a[0, i] = add(own[0, i, y, :, left], got[0, i, y, :, left]).astype(BF16)
                b[0, i] = add(own[0, x, i, :, right], got[0, x, i, :, right]).astype(BF16)

    ins = [(v.reshape(4, 2, 2, rows, columns), by_z) for v in (own, swap(other, CORE))]
    ka, sa, kb, sb, token = call(kernel, (4,), (sc,), ins, [((4, 2, rows, half), BF16, to_z)] * 4, (), after, mib=12)
    return [(ka, sa, Y), (kb, sb, X)], token


def columns_of(parts):
    rows = min(keep.shape[2] for keep, _, _ in parts)
    places, at = [], 0
    for n, (keep, _, _) in enumerate(parts):
        for first in range(0, keep.shape[2], rows):
            places.append((n, first, at, keep.shape[3]))
            at += keep.shape[3]
    return rows, at, places


def fold_first(parts, sc, after):
    groups = [[part for part in parts if part[2] == mask] for mask in (Y, X)]
    ins = [(v, full(v.shape)) for group in groups for keep, send, mask in group for v in (keep, swap(send, mask))]
    layouts = [columns_of(group) for group in groups]
    outs = [((4, rows, width), BF16, full((4, rows, width))) for rows, width, _ in layouts for _ in range(2)]

    def kernel(sc, *refs):
        ins, outs, base = refs[: len(ins_)], refs[len(ins_) :], 0
        for g, (rows, _, places) in enumerate(layouts):
            for n, first, at, width in places:
                keep, got = ins[base + 2 * n], ins[base + 2 * n + 1]
                cut = pl.ds(first, rows)
                for z in range(4):
                    for flip in range(2):
                        here = sc[1 + g] ^ flip
                        to = outs[2 * g + flip]
                        to[z, :, pl.ds(at, width)] = add(keep[z, here, cut], got[z, here, cut]).astype(BF16)
            base += 2 * len(groups[g])

    ins_ = ins
    out = call(kernel, (1,), (sc,), ins, outs, (), after, mib=16)
    return [(out[0], out[1], X), (out[2], out[3], Y)], out[4]


def fold_second(parts, sc, after):
    ins = [(v, full(v.shape)) for keep, send, mask in parts for v in (keep, swap(send, mask))]
    _, rows, width = parts[0][0].shape
    shape = (rows, 2 * width)

    def kernel(sc, *refs):
        ins, outs = refs[:4], refs[4:]
        for k, to in enumerate(outs):
            z = sc[3] ^ k
            for n in range(2):
                to[:, pl.ds(n * width, width)] = add(ins[2 * n][z], ins[2 * n + 1][z]).astype(to.dtype)

    outs = [(shape, F32, full(shape))] + [(shape, BF16, full(shape))] * 3
    return call(kernel, (1,), (sc,), ins, outs, (), after, mib=12)


def fold_sends(parts):
    keep, *sends, token = parts
    return token, [keep] + [swap(v, Z * k) for k, v in zip((1, 2, 3), sends)]


def fold_last(parts, shapes, runs, after):
    def kernel(keep, r1, r2, r3, *outs):
        rows = keep.shape[0]
        for i, (n, first, stride) in enumerate(runs):
            cut = (slice(None), pl.ds(i * 128, 128))
            total = keep[cut] + (r1[cut].astype(F32) + r2[cut].astype(F32) + r3[cut].astype(F32))
            outs[n][pl.ds(first, rows, stride=stride)] = total

    ins = [(v, full(v.shape)) for v in parts]
    return call(kernel, (1,), (), ins, [(shape, F32, full(shape)) for shape in shapes], (), after, mib=12)


def reduce_level(v, masks, at, sc, after, split=None):
    shapes, where = split or ([v.shape], [(0, pl.ds(i, 1)) for i in range(v.shape[0])])

    def kernel(sc, *refs):
        line, outs = refs[-1], refs[-1 - len(shapes) : -1]
        mine = sc[at[0]]
        for k in at[1:]:
            mine = 2 * mine + sc[k]
        for k, ref in enumerate(refs[: len(masks) + 1]):
            line[mine ^ k] = ref[...]
        total = line[0]
        for k in range(1, len(masks) + 1):
            total = total + line[k]
        for i, (n, place) in enumerate(where):
            outs[n][place] = total[i : i + 1]

    ins = [v] + [swap(v, mask) for mask in masks]
    outs = [(shape, F32, full(shape)) for shape in shapes]
    scratch = [pltpu.VMEM((len(ins),) + v.shape, F32)]
    return call(kernel, (1,), (sc,), [(u, full(v.shape)) for u in ins], outs, scratch, after, mib=8)


def body(
    tokens,
    patch_grid,
    qkv_rows,
    proj_rows,
    fc1_rows,
    fc2_rows,
    norm_gain,
    norm_bias,
    qv_bias,
    proj_bias,
    fc1_bias,
    fc2_bias,
    layer_scale,
    cotangent,
):
    rows, width = tokens.shape
    packs, images, _ = patch_grid.shape
    pack = rows // packs
    slot = pack // images
    head = width // H
    hidden = fc1_bias.shape[0]
    row_width = qkv_rows.shape[1]
    tiles = hidden // width
    tile = min(256, rows)
    swaps = lax.axis_size("wide") == 16 and lax.axis_size("narrow") == 2
    if swaps:
        me = lax.axis_index(AXES)
        sc = jnp.stack([me // CORE % 2, me // X % 2, me % 2, me // Z]).astype(jnp.int32)
    else:
        sc = jnp.zeros((4,), jnp.int32)
    grid_flat = patch_grid.reshape(-1)
    thin, wide_rows = width // (2 * COLUMNS), hidden // (2 * COLUMNS)
    per_tile = COLUMNS // tiles

    by_pack = pl.BlockSpec((pack, width), lambda i, *_: (i, 0))
    by_tile = lambda w: pl.BlockSpec((tile, w), lambda i, *_: (i, 0))
    whole = full((rows, width))
    proj_blocks = pl.BlockSpec((COLUMNS, thin, width), lambda i, *_: (0, 0, 3), pipeline_mode=pl.Buffered(1))
    fc2_blocks = pl.BlockSpec((per_tile, wide_rows, width), lambda i, *_: (i, 0, 0))
    column_blocks = pl.BlockSpec((COLUMNS, thin, width), lambda i, *_: (0, 0, i))
    hidden_tile = pl.BlockSpec((rows, width), lambda i, *_: (0, i))
    vec1, vec2 = full((1, width)), full((2, width))
    hidden_vec = pl.BlockSpec((1, width), lambda i, *_: (0, i))
    qkv_blocks = full((COLUMNS, thin, 3 * width))
    qkv_scr = pltpu.VMEM((COLUMNS, 2, thin, 3 * width), BF16)
    fc2_scr = pltpu.VMEM((per_tile, 2, wide_rows, width), BF16)
    thin_scr = pltpu.VMEM((COLUMNS, 2, thin, width), BF16)
    sum_scr = pltpu.VMEM((rows, width), F32)
    turned_scr = pltpu.VMEM((width, rows), BF16)
    log_block = pl.BlockSpec((tile // slot * H, slot), lambda i, *_: (i, 0))

    qp_block = jnp.concatenate([qkv_rows.reshape(-1, 3 * width), proj_rows.reshape(-1, width)], axis=1)
    fc1_block = fc1_rows.reshape(-1, hidden)
    fc2_block = fc2_rows.reshape(-1, width)
    halves = lambda v: v.reshape(COLUMNS, 2, -1, v.shape[1]).transpose(1, 0, 2, 3)
    ready = []
    if swaps:
        runs = fc2_block.reshape(tiles, -1, width)
        fc2_wide = jnp.concatenate([runs[k] for k in range(tiles)], axis=1)
        *qp_ab, fc1_near, fc2_near, _ = gather_stack(qp_block, fc1_block, fc2_wide, sc=sc, after=[])
        *qp_pair, token = gather_pair(*qp_ab, sc, [])
        ready = [token]
    else:
        qp_own, qp_other = halves(lax.all_gather(qp_block, AXES, axis=0, tiled=True))
        fc1_own, fc1_other = halves(lax.all_gather(fc1_block, AXES, axis=0, tiled=True))
        fc2_own, fc2_other = halves(lax.all_gather(fc2_block, AXES, axis=0, tiled=True))

    x, n1, up, b2g, fc2_sums, token = call(
        partial(prepare_kernel, images=images),
        (packs,),
        (grid_flat,),
        [(far(tokens), by_pack), (far(cotangent), by_pack), (norm_gain, vec2), (norm_bias, vec2), (layer_scale, vec2)],
        [((rows, width), BF16, by_pack, "far")] * 4 + [((1, width), F32, vec1)],
        (),
        ready,
        mib=14,
    )

    ready = []
    if swaps:
        *fc1_ab, token = gather_rest(fc1_near, sc, [token])
        qp_own, qp_other, token = gather_place(*qp_pair, sc, [token])
        *fc1_pair, token = gather_pair(*fc1_ab, sc, [token])
        ready = [token]

    offset = jnp.concatenate([qv_bias[0], jnp.zeros_like(qv_bias[0]), qv_bias[1]])[None]
    proj, att, log_total, token = call(
        partial(attend_kernel, slot=slot, head=head),
        (rows // tile,),
        (grid_flat, sc),
        [(far(n1), by_tile(width)), (qp_own, qkv_blocks), (qp_other, qkv_blocks), (offset, full((1, 3 * width)))],
        [((rows, 3 * width), BF16, by_tile(3 * width), "far"), ((rows, width), BF16, by_tile(width))]
        + [((rows // slot * H, slot), F32, log_block)],
        [qkv_scr],
        ready,
        mib=24,
    )
    ready = []
    if swaps:
        *fc2_ab, token = gather_rest(fc2_near, sc, [token])
        fc1_own, fc1_other, token = gather_place(*fc1_pair, sc, [token])
        ready = [token]
    b1, n2, token = call(
        middle_kernel,
        (1,),
        (sc,),
        [(att, whole), (x, whole), (norm_gain, vec2), (norm_bias, vec2), (layer_scale, vec2), (proj_bias[None], vec1)]
        + [(qp_own, proj_blocks), (qp_other, proj_blocks)],
        [((rows, width), F32, whole, "far"), ((rows, width), BF16, whole)],
        [sum_scr, thin_scr],
        ready,
        mib=20,
    )
    ready = []
    if swaps:
        *fc2_pair, token = gather_pair(*fc2_ab, sc, [token])
        ready = [token]
    act, slope, fc2g_own, fc2g_other, token = call(
        hidden_kernel,
        (tiles,),
        (sc,),
        [(n2, whole), (b2g, whole), (fc1_bias[None], hidden_vec), (fc1_own, column_blocks), (fc1_other, column_blocks)],
        [((rows, hidden), BF16, hidden_tile, "far"), ((rows, hidden), F32, hidden_tile, "far")]
        + [((COLUMNS, wide_rows, width), BF16, fc2_blocks, "far")] * 2,
        [thin_scr],
        ready,
        mib=24,
    )
    if swaps:
        fc2_own, fc2_other, _ = gather_place(*fc2_pair, sc, [token], tiles)

    hg, fc1_sums, fc1g_own, fc1g_other, token = call(
        hidden_back_kernel,
        (tiles,),
        (sc,),
        [(far(b2g), whole), (far(n2), whole), (far(slope), hidden_tile), (fc2_own, fc2_blocks), (fc2_other, fc2_blocks)],
        [((rows, hidden), BF16, hidden_tile, "far"), ((1, hidden), F32, hidden_vec)]
        + [((COLUMNS, thin, hidden), BF16, column_blocks, "far")] * 2,
        [turned_scr, fc2_scr],
        mib=28,
    )
    chain = []
    if swaps:
        fc2_parts, token = fold_core(fc2g_own, fc2g_other, sc, [token])
        chain = [token]

    bound = lambda i: jnp.minimum(i, tiles - 1)
    hidden_first = pl.BlockSpec((rows, width), lambda i, *_: (0, bound(i)))
    column_first = pl.BlockSpec((COLUMNS, thin, width), lambda i, *_: (0, 0, bound(i)))
    fc2_first = pl.BlockSpec((per_tile, wide_rows, width), lambda i, *_: (bound(i), 0, 0))
    then = lambda size: pl.BlockSpec((size, width), lambda i, *_: (jnp.maximum(i - tiles, 0), 0))
    mg, b1g, ag, middle_sums, token = call(
        partial(middle_back_kernel, tiles=tiles),
        (tiles + rows // tile,),
        (sc,),
        [(far(hg), hidden_first), (fc1_own, column_first), (fc1_other, column_first)]
        + [(qp_own, proj_blocks), (qp_other, proj_blocks)]
        + [(b1, then(tile)), (x, then(tile)), (up, then(tile)), (norm_gain, vec2), (layer_scale, vec2)],
        [((rows, width), F32, then(tile), "far"), ((rows, width), BF16, then(tile)), ((rows, width), BF16, then(tile))]
        + [((4, width), F32, full((4, width)))],
        [sum_scr, thin_scr, thin_scr],
        chain,
        mib=28,
    )
    chain = []
    if swaps:
        fc1_parts, token = fold_core(fc1g_own, fc1g_other, sc, [token])
        chain = [token]

    pg, proj_sums, token = call(
        partial(attend_back_kernel, slot=slot, head=head),
        (rows // tile,),
        (grid_flat,),
        [(far(proj), by_tile(3 * width)), (ag, by_tile(width)), (log_total, log_block)],
        [((rows, 3 * width), BF16, by_tile(3 * width)), ((8, 3 * width), F32, full((8, 3 * width)))],
        (),
        chain,
        mib=14,
    )
    chain = []
    if swaps:
        fc_parts, token = fold_first(fc1_parts + fc2_parts, sc, [token])
        chain = [token]

    qp_grad_own, qp_grad_other, token = call(
        weight_kernel,
        (4,),
        (sc,),
        [(n1, whole), (att, whole), (pg, pl.BlockSpec((rows, width), lambda i, *_: (0, jnp.minimum(i, 2)))), (b1g, whole)],
        [((COLUMNS, thin, 4 * width), BF16, column_blocks)] * 2,
        [turned_scr],
        chain,
        mib=18,
    )
    layer_out, out_sums, token = call(
        partial(layer_out_kernel, images=images, tiles=tiles),
        (tiles + packs,),
        (grid_flat, sc),
        [(far(act), hidden_first), (fc2_own, fc2_first), (fc2_other, fc2_first), (x, then(pack)), (b1, then(pack)), (up, then(pack))]
        + [(layer_scale, vec2), (fc2_bias[None], vec1)],
        [((rows, width), BF16, then(pack), "far"), ((1, width), F32, vec1)],
        [sum_scr, pltpu.VMEM((pack, width), BF16), fc2_scr],
        [token],
        mib=26,
    )
    chain = []
    if swaps:
        qp_parts, token = fold_core(qp_grad_own, qp_grad_other, sc, [token])
        token, fc_parts = fold_sends(fold_second(fc_parts, sc, [token]))
        chain = [token]

    input_grad, input_sums, token = call(
        partial(input_back_kernel, images=images),
        (packs,),
        (grid_flat, sc),
        [(pg, pl.BlockSpec((pack, 3 * width), lambda i, *_: (i, 0))), (qp_own, qkv_blocks), (qp_other, qkv_blocks)]
        + [(x, by_pack), (mg, by_pack), (norm_gain, vec2)],
        [((rows, width), F32, by_pack, "far"), ((2, width), F32, vec2)],
        [qkv_scr, pltpu.VMEM((pack, width), F32)] + [pltpu.VMEM((pack, width), BF16)] * 2,
        chain,
        mib=26,
    )

    chain = []
    if swaps:
        qp_parts, token = fold_first(qp_parts, sc, [token, fc_parts[1], fc_parts[3]])
        chain = [token]

    def gather_sums(input_sums, middle, proj, fc2, out, fc1, to):
        q, v = column_sum(proj[:, pl.ds(0, width)]), column_sum(proj[:, pl.ds(2 * width, width)])
        lines = (input_sums[0:1], middle[2:3], input_sums[1:2], middle[3:4], q, v, middle[1:2], fc2[...], middle[0:1], out[...])
        for i, line in enumerate(lines):
            to[pl.ds(i, 1)] = line
        for i in range(tiles):
            to[pl.ds(len(lines) + i, 1)] = fc1[:, pl.ds(i * width, width)]

    sums_in = (input_sums, middle_sums, proj_sums, fc2_sums, out_sums, fc1_sums)
    sums, token = call(
        gather_sums,
        (1,),
        (),
        [(v, full(v.shape)) for v in sums_in],
        [((10 + tiles, width), F32, full((10 + tiles, width)))],
        (),
        chain,
    )
    if swaps:
        fc2_rows_of = fc2_rows.shape[0] // tiles
        n1_runs, n2_runs = hidden // 256, width // 256
        fc_runs = []
        for half in range(2):
            fc_runs += [(0, half * n1_runs + i, hidden // 128) for i in range(n1_runs)]
            fc_runs += [(1, k * fc2_rows_of + half * n2_runs + i, width // 128) for k in range(tiles) for i in range(n2_runs)]
        sums, token = reduce_level(sums, (CORE,), (0,), sc, [token])
        token, qp_parts = fold_sends(fold_second(qp_parts, sc, [token]))
        sums, token = reduce_level(sums, (Y, X, X + Y), (1, 2), sc, [token, qp_parts[1]])
        fc1_grad, fc2_grad, token = fold_last(fc_parts, (fc1_rows.shape, fc2_rows.shape), fc_runs, [token, qp_parts[3]])
        line = lambda i: (slice(None), pl.ds(i * width, width))
        shapes = [(2, width)] * 3 + [(1, width), (1, hidden), (1, width), (2, width)]
        where = [(i // 2, pl.ds(i % 2, 1)) for i in range(6)] + [(3, pl.ds(0, 1)), (5, pl.ds(0, 1))]
        where += [(6, pl.ds(0, 1)), (6, pl.ds(1, 1))] + [(4, line(i)) for i in range(tiles)]
        *small, token = reduce_level(sums, (Z, 2 * Z, 3 * Z), (3,), sc, [token, qp_parts[2]], (shapes, where))
        qkv_runs, proj_runs = 3 * width // 128, width // 128
        qp_runs = [(0, i, qkv_runs) for i in range(qkv_runs)] + [(1, i, proj_runs) for i in range(proj_runs)]
        qkv_grad, proj_grad, _ = fold_last(qp_parts, (qkv_rows.shape, proj_rows.shape), qp_runs, [token])
    else:

        def scatter(own, other):
            matrix = jnp.stack([own, other], axis=1).reshape(-1, own.shape[-1])
            return lax.psum_scatter(matrix, AXES, scatter_dimension=0, tiled=True).astype(F32)

        fc2_grad = scatter(fc2g_own, fc2g_other).reshape(-1, row_width)
        fc1_grad = scatter(fc1g_own, fc1g_other).reshape(-1, row_width)
        qp_grad = scatter(qp_grad_own, qp_grad_other)
        qkv_grad = qp_grad[:, : 3 * width].reshape(-1, row_width)
        proj_grad = qp_grad[:, 3 * width :].reshape(-1, row_width)
        sums = lax.psum(sums, AXES)
        small = [sums[0:2], sums[2:4], sums[4:6], sums[6], sums[10:].reshape(-1), sums[7], sums[8:10]]
    return (
        layer_out,
        input_grad,
        qkv_grad,
        proj_grad,
        fc1_grad,
        fc2_grad,
        *(v.reshape(leaf.shape) for v, leaf in zip(small, (norm_gain, norm_bias, qv_bias, proj_bias, fc1_bias, fc2_bias, layer_scale))),
    )


def solution(mesh):
    split = P(AXES, None)
    return jax.shard_map(
        body,
        mesh=mesh,
        in_specs=(split, P(AXES, None, None)) + (split,) * 4 + (P(),) * 7 + (split,),
        out_specs=(split,) * 6 + (P(),) * 7,
        check_vma=False,
    )
```

```python
from functools import partial

import jax
import jax.numpy as jnp
from jax import lax
from jax.experimental import pallas as pl
from jax.experimental.pallas import tpu as pltpu
from jax.sharding import PartitionSpec as P

H = 12
PREFIX = 5
EPSILON = 1e-06
NEGATIVE = -1e30
AXES = ("wide", "narrow")
COLUMNS = 8
BF16 = jnp.bfloat16
F32 = jnp.float32


def dot(a, b):
    return lax.dot_general(a, b, (((1,), (0,)), ((), ())), preferred_element_type=F32)


def dot_nt(a, b):
    return lax.dot_general(a, b, (((1,), (1,)), ((), ())), preferred_element_type=F32)


def dot_tn(a, b):
    return lax.dot_general(a, b, (((0,), (0,)), ((), ())), preferred_element_type=F32)


TOKEN = (8, 128)


def call(kernel, grid, scalars, ins, outs, scratch=(), after=(), mib=36, alias=None):
    n, m = len(scalars) + len(ins), len(outs)

    def run(*refs):
        rest = refs[n + len(after) :]
        rest[m][...] = jnp.zeros(TOKEN, F32)
        kernel(*refs[:n], *rest[:m], *rest[m + 1 :])

    anywhere = pl.BlockSpec(memory_space=pl.ANY)
    return pl.pallas_call(
        run,
        grid_spec=pltpu.PrefetchScalarGridSpec(
            num_scalar_prefetch=len(scalars),
            grid=grid,
            in_specs=[spec for _, spec in ins] + [anywhere] * len(after),
            out_specs=[out[2] for out in outs] + [full(TOKEN)],
            scratch_shapes=list(scratch),
        ),
        out_shape=[
            pltpu.HBM(out[0], out[1]) if len(out) > 3 else jax.ShapeDtypeStruct(out[0], out[1]) for out in outs
        ]
        + [jax.ShapeDtypeStruct(TOKEN, F32)],
        input_output_aliases={n + k: to for k, to in (alias or {}).items()},
        compiler_params=pltpu.CompilerParams(vmem_limit_bytes=mib * 2**20),
        cost_estimate=pl.CostEstimate(flops=1, bytes_accessed=1, transcendentals=0),
    )(*scalars, *(array for array, _ in ins), *after)


def far(v):
    return pltpu.with_memory_space_constraint(v, pltpu.HBM)


def full(shape):
    return pl.BlockSpec(shape, lambda *_: (0,) * len(shape), pipeline_mode=pl.Buffered(1))


def standardize(v):
    centered = v - jnp.mean(v, axis=-1, keepdims=True)
    inverse = lax.rsqrt(jnp.mean(centered * centered, axis=-1, keepdims=True) + EPSILON)
    return centered * inverse, inverse


def standardize_back(grad, scaled, inverse):
    return inverse * (
        grad
        - jnp.mean(grad, axis=-1, keepdims=True)
        - scaled * jnp.mean(grad * scaled, axis=-1, keepdims=True)
    )


def length_of(grid_ref, image):
    return PREFIX + grid_ref[2 * image] * grid_ref[2 * image + 1]


def spans(grid_ref, pack, images):
    found, start = [], 0
    for i in range(images):
        length = length_of(grid_ref, pack * images + i)
        found.append((start, length))
        start = start + length
    return found


def join(scr, core, own, other):
    for i in range(scr.shape[0]):
        scr[i, core] = own[i]
        scr[i, 1 - core] = other[i]
    blocks, cores, rows, columns = scr.shape
    return scr[...].reshape(blocks * cores * rows, columns)


def part(core, matrix, own, other):
    blocks, rows, columns = own.shape
    cut = matrix.reshape(blocks, 2, rows, columns)
    own[...] = jnp.where(core == 0, cut[:, 0], cut[:, 1])
    other[...] = jnp.where(core == 0, cut[:, 1], cut[:, 0])


def prepare_kernel(grid_ref, tok, cot, gain, bias, ls, x, n1, up, b2g, sums, *, images):
    pack = pl.program_id(0)
    slot = tok.shape[0] // images
    row = lax.broadcasted_iota(jnp.int32, (slot, tok.shape[0]), 0)
    column = lax.broadcasted_iota(jnp.int32, (slot, tok.shape[0]), 1)
    total = jnp.zeros((1, tok.shape[1]), F32)
    for i, (start, length) in enumerate(spans(grid_ref, pack, images)):
        place = jnp.where((column - row == start) & (row < length), 1.0, 0.0).astype(BF16)
        rows = pl.ds(i * slot, slot)
        moved = dot(place, tok[...])
        x[rows] = moved.astype(BF16)
        scaled, _ = standardize(moved)
        n1[rows] = (scaled * gain[0:1] + bias[0:1]).astype(BF16)
        upstream = dot(place, cot[...])
        up[rows] = upstream.astype(BF16)
        low = (ls[1:2] * upstream).astype(BF16)
        b2g[rows] = low
        total = total + jnp.sum(low.astype(F32), axis=0, keepdims=True)

    @pl.when(pack == 0)
    def _():
        sums[...] = jnp.zeros_like(sums)

    sums[...] += total


def unplace(grid_ref, pack, images, size):
    slot = size // images
    row = lax.broadcasted_iota(jnp.int32, (size, slot), 0)
    column = lax.broadcasted_iota(jnp.int32, (size, slot), 1)
    return jnp.concatenate(
        [
            jnp.where((row - column == start) & (column < length), 1.0, 0.0).astype(BF16)
            for start, length in spans(grid_ref, pack, images)
        ],
        axis=1,
    )


def pieces(rows, size=128):
    return [pl.ds(r, size) for r in range(0, rows, size)]


def eights(v):
    return jnp.sum(v.reshape(-1, 8, v.shape[1]), axis=0)


def column_sum(v):
    return jnp.sum(v, axis=0, keepdims=True)


def stacked(v, low):
    zero = jnp.zeros_like(v)
    return jnp.concatenate([jnp.where(low, v, zero), jnp.where(low, zero, v)], axis=0)


def attend_kernel(grid_ref, sc, n1, own, other, offset, proj, att, log_total, scr, *, slot, head):
    step = pl.program_id(0)
    width = n1.shape[1]
    per = n1.shape[0] // slot
    pair = 2 * head
    heads = width // head

    @pl.when(step == 0)
    def _():
        join(scr, sc[0], own, other)

    w = scr[...].reshape(width, 3 * width)
    proj[...] = (dot(n1[...], w) + offset[...]).astype(BF16)
    low = lax.broadcasted_iota(jnp.int32, (slot, pair), 1) < head
    key_at = lax.broadcasted_iota(jnp.int32, (slot, slot), 0)
    for i in range(per):
        ok = key_at < length_of(grid_ref, step * per + i)
        rows = pl.ds(i * slot, slot)
        found = []
        for j in range(width // pair):
            q, k = (proj[rows, pl.ds(t * width + j * pair, pair)] for t in range(2))
            scores = dot_nt(stacked(k, low), q * jnp.asarray(head ** (-0.5), BF16))
            halves = []
            for h in range(2):
                masked = jnp.where(ok, scores[h * slot : (h + 1) * slot], NEGATIVE)
                top = jnp.max(masked, axis=0, keepdims=True)
                exponent = jnp.exp(masked - top)
                total = column_sum(exponent)
                halves.append((exponent * (1.0 / total)).astype(BF16))
                log_total[pl.ds(i * heads + 2 * j + h, 1)] = top + jnp.log(total)
            found.append(jnp.concatenate(halves, axis=0))
        for j, p in enumerate(found):
            v = proj[rows, pl.ds(2 * width + j * pair, pair)]
            att[rows, pl.ds(j * pair, pair)] = dot_tn(p, stacked(v, low)).astype(BF16)


def middle_kernel(sc, att, x, gain, bias, ls, proj_bias, own, other, b1, n2, acc, scr):
    acc[...] = dot(att[...], join(scr, sc[0], own, other))
    for rows in pieces(acc.shape[0]):
        branch = acc[rows] + proj_bias[...]
        b1[rows] = branch
        scaled, _ = standardize(x[rows].astype(F32) + ls[0:1] * branch)
        n2[rows] = (scaled * gain[1:2] + bias[1:2]).astype(BF16)


def hidden_kernel(sc, n2, b2g, fc1_bias, own, other, act, slope, go, gs, scr):
    w1 = join(scr, sc[0], own, other)
    for rows in pieces(n2.shape[0], 256):
        hidden = dot(n2[rows], w1) + fc1_bias[...]
        normal = 0.5 * (1.0 + lax.erf(hidden * 0.5**0.5))
        act[rows] = (hidden * normal).astype(BF16)
        density = (0.5 / jnp.pi) ** 0.5 * jnp.exp(-0.5 * hidden * hidden)
        slope[rows] = normal + hidden * density
    part(sc[0], dot_tn(act[...], b2g[...]).astype(BF16), go, gs)


def hidden_back_kernel(sc, b2g, n2, slope, own, other, hg, sums, go, gs, n2t, scr):
    @pl.when(pl.program_id(0) == 0)
    def _():
        n2t[...] = n2[...].T

    w2 = join(scr, sc[0], own, other)
    total = jnp.zeros((8, sums.shape[1]), F32)
    for rows in pieces(b2g.shape[0], 256):
        low = (dot_nt(b2g[rows], w2) * slope[rows]).astype(BF16)
        hg[rows] = low
        total = total + eights(low.astype(F32))
    sums[...] = column_sum(total)
    part(sc[0], dot(n2t[...], hg[...]).astype(BF16), go, gs)


def middle_back_kernel(sc, hg, own, other, po, ps, b1, x, up, gain, ls, mg, b1g, ag, sums, acc, scr, pscr, *, tiles):
    step = pl.program_id(0)

    @pl.when(step == 0)
    def _():
        acc[...] = dot_nt(hg[...], join(scr, sc[0], own, other))

    @pl.when((step > 0) & (step < tiles))
    def _():
        acc[...] += dot_nt(hg[...], join(scr, sc[0], own, other))

    @pl.when(step == tiles)
    def _():
        join(pscr, sc[0], po, ps)
        sums[...] = jnp.zeros_like(sums)

    @pl.when(step >= tiles)
    def _():
        size = x.shape[0]
        totals = [jnp.zeros((8, x.shape[1]), F32) for _ in range(4)]
        for rows in pieces(size):
            branch = b1[rows]
            scaled, inverse = standardize(x[rows].astype(F32) + ls[0:1] * branch)
            grad = acc[pl.ds(pl.multiple_of((step - tiles) * size + rows.start, 128), rows.size)]
            back = up[rows].astype(F32) + standardize_back(grad * gain[1:2], scaled, inverse)
            mg[rows] = back
            low = (ls[0:1] * back).astype(BF16)
            b1g[rows] = low
            terms = (back * branch, low.astype(F32), grad * scaled, grad)
            totals = [t + eights(v) for t, v in zip(totals, terms)]
        ag[...] = dot_nt(b1g[...], pscr[...].reshape(x.shape[1], x.shape[1])).astype(BF16)
        sums[...] += jnp.concatenate([column_sum(t) for t in totals], axis=0)


def attend_back_kernel(grid_ref, proj, ag, log_total, pg, sums, *, slot, head):
    step = pl.program_id(0)
    width = ag.shape[1]
    per = ag.shape[0] // slot
    pair = 2 * head
    heads = width // head
    factor = head ** (-0.5)
    low = lax.broadcasted_iota(jnp.int32, (slot, pair), 1) < head
    key_at = lax.broadcasted_iota(jnp.int32, (slot, slot), 0)

    @pl.when(step == 0)
    def _():
        sums[...] = jnp.zeros_like(sums)

    for i in range(per):
        ok = key_at < length_of(grid_ref, step * per + i)
        rows = pl.ds(i * slot, slot)
        found = []

        def put(t, j, d):
            d = d.astype(BF16)
            columns = pl.ds(t * width + j * pair, pair)
            pg[rows, columns] = d
            if t != 1:
                sums[:, columns] += eights(d.astype(F32))

        for j in range(width // pair):
            q, k, v = (proj[rows, pl.ds(t * width + j * pair, pair)] for t in range(3))
            out = ag[rows, pl.ds(j * pair, pair)]
            q = q * jnp.asarray(factor, BF16)
            k2 = stacked(k, low)
            scores = dot_nt(k2, q)
            pull = dot_nt(stacked(v, low), out)
            ps, ss = [], []
            for h in range(2):
                half = slice(h * slot, (h + 1) * slot)
                p = jnp.exp(jnp.where(ok, scores[half], NEGATIVE) - log_total[pl.ds(i * heads + 2 * j + h, 1)])
                g = pull[half]
                ps.append(p.astype(BF16))
                ss.append((p * (g - column_sum(g * p))).astype(BF16))
            s = jnp.concatenate(ss, axis=0)
            dk = dot(s, q)
            dv = dot(jnp.concatenate(ps, axis=0), out)
            put(1, j, jnp.where(low, dk[:slot], dk[slot:]))
            put(2, j, jnp.where(low, dv[:slot], dv[slot:]))
            found.append((s, k2))
        for j, (s, k2) in enumerate(found):
            put(0, j, dot_tn(s, k2) * factor)


def weight_kernel(sc, n1, att, pg, b1g, go, gs, n1t):
    step = pl.program_id(0)
    last = pl.num_programs(0) - 1

    @pl.when(step == 0)
    def _():
        n1t[...] = n1[...].T

    @pl.when(step < last)
    def _():
        part(sc[0], dot(n1t[...], pg[...]).astype(BF16), go, gs)

    @pl.when(step == last)
    def _():
        part(sc[0], dot_tn(att[...], b1g[...]).astype(BF16), go, gs)


def input_back_kernel(grid_ref, sc, pg, own, other, x, mg, gain, out, sums, scr, acc, high, mid, *, images):
    pack = pl.program_id(0)

    @pl.when(pack == 0)
    def _():
        join(scr, sc[0], own, other)
        sums[...] = jnp.zeros_like(sums)

    width = x.shape[1]
    acc[...] = dot_nt(pg[...], scr[...].reshape(width, 3 * width))
    totals = [jnp.zeros((8, width), F32) for _ in range(2)]
    for rows in pieces(acc.shape[0]):
        grad = acc[rows]
        scaled, inverse = standardize(x[rows].astype(F32))
        back = mg[rows] + standardize_back(grad * gain[0:1], scaled, inverse)
        totals = [t + eights(v) for t, v in zip(totals, (grad * scaled, grad))]
        big = back.astype(BF16)
        high[rows] = big
        mid[rows] = (back - big.astype(F32)).astype(BF16)
    sums[...] += jnp.concatenate([column_sum(t) for t in totals], axis=0)
    place = unplace(grid_ref, pack, images, x.shape[0])
    out[...] = dot(place, high[...]) + dot(place, mid[...])


def layer_out_kernel(grid_ref, sc, act, own, other, x, b1, up, ls, fc2_bias, out, sums, acc, result, scr, *, images, tiles):
    step = pl.program_id(0)

    @pl.when(step == 0)
    def _():
        acc[...] = dot(act[...], join(scr, sc[0], own, other))

    @pl.when((step > 0) & (step < tiles))
    def _():
        acc[...] += dot(act[...], join(scr, sc[0], own, other))

    @pl.when(step == tiles)
    def _():
        sums[...] = jnp.zeros_like(sums)

    @pl.when(step >= tiles)
    def _():
        pack, size = step - tiles, out.shape[0]
        total = jnp.zeros((8, x.shape[1]), F32)
        for rows in pieces(size):
            branch = acc[pl.ds(pl.multiple_of(pack * size + rows.start, 128), rows.size)] + fc2_bias[...]
            total = total + eights(up[rows].astype(F32) * branch)
            middle = x[rows].astype(F32) + ls[0:1] * b1[rows]
            result[rows] = (middle + ls[1:2] * branch).astype(BF16)
        out[...] = dot(unplace(grid_ref, pack, images, size), result[...]).astype(BF16)
        sums[...] += column_sum(total)


Y, CORE, X, Z = 1, 2, 4, 8


def swap(v, mask):
    return lax.ppermute(v, AXES, [(i, i ^ mask) for i in range(32)])


def move(plan, sc, ins, outs, after, mib=8):
    def kernel(*refs):
        for a, b in plan(*refs):
            b[...] = a[...]

    return call(
        kernel, (1,), (sc,), [(v, full(v.shape)) for v in ins], [(shape, BF16, full(shape)) for shape in outs], (), after, mib
    )


def gather_line(block):
    return [block] + [swap(block, Z * k) for k in (1, 2, 3)]


def gather_stack(line, sc, after, sides=()):
    rows, columns = line[0].shape
    half = columns // 2
    shapes = [(4, rows, half)] * 2 + [(2, 2) + side.shape for side in sides[:1]]

    def plan(sc, *refs):
        ins, outs = refs[: 4 + len(sides)], refs[4 + len(sides) :]
        pairs = [(ins[k].at[:, pl.ds(h * half, half)], outs[h].at[k]) for k in range(4) for h in range(2)]
        return pairs + [(side, outs[2].at[i // 2, i % 2]) for i, side in enumerate(ins[4:])]

    return move(plan, sc, [*line, *sides], shapes, after)


def gather_columns(line, sc, after):
    _, _, rows, half = line[0].shape

    def plan(sc, *refs):
        return [(refs[k].at[h, i], refs[4 + h].at[i, k]) for k in range(4) for h in range(2) for i in range(2)]

    return move(plan, sc, line, [(2, 4, rows, half)] * 2, after)


def pack_rows(qkv, proj, fc1, fc2, width, tiles):
    arrays = (qkv, proj, fc1, fc2)
    rows = proj.shape[0] * 128 // width
    columns = [v.shape[0] * 128 // rows for v in arrays]
    places = [(0, 0), (0, columns[0]), (1, 0), (2, 0)]
    half = columns[3] // 2

    def kernel(*refs):
        ins, outs, scrs = refs[:4], refs[4:8], refs[8:]
        for n, (ref, scr) in enumerate(zip(ins, scrs)):
            scr[...] = ref[...].astype(F32)
            if n < 3:
                blocks = [(i, columns[n] // 128) for i in range(columns[n] // 128)]
            else:
                lanes = width // 128
                blocks = [(k * rows * lanes + i, lanes) for k in range(tiles) for i in range(lanes)]
            for i, (start, stride) in enumerate(blocks):
                to, at = places[n]
                at += i * 128
                if n == 3:
                    to, at = to + at // half, at % half
                outs[to][:, pl.ds(at, 128)] = scr[pl.ds(start, rows, stride=stride)].astype(BF16)

    shapes = [(rows, columns[0] + columns[1]), (rows, columns[2]), (rows, half), (rows, half)]
    scratch = [pltpu.VMEM(v.shape, F32) for v in arrays]
    outs = [(shape, BF16, full(shape)) for shape in shapes]
    return call(kernel, (1,), (), [(v, full(v.shape)) for v in arrays], outs, scratch, (), mib=8)[:4]


def gather_pair(a, b, sc, after):
    def plan(sc, a, xa, b, yb, left, right):
        return [(a, left.at[0]), (xa, left.at[1]), (b, right.at[0]), (yb, right.at[1])]

    return move(plan, sc, (a, swap(a, X), b, swap(b, Y)), [(2,) + a.shape] * 2, after)


def gather_place(left, right, sc, after, runs=1):
    _, _, rows, half = left.shape
    width = 2 * half // runs

    def plan(sc, left, other_left, right, other_right, out):
        pairs = []
        for n, sides in enumerate(((left, other_left), (right, other_right))):
            for i in range(2):
                for j in range(2):
                    for k in range(4):
                        x, y = (i, j) if n == 0 else (j, i)
                        to = out.at[sc[3] ^ k, sc[1] ^ x, sc[2] ^ y]
                        if runs == 1:
                            pairs.append((sides[j].at[i, k], to.at[:, pl.ds(n * half, half)]))
                            continue
                        for r in range(runs // 2):
                            run = n * (runs // 2) + r
                            pairs.append((sides[j].at[i, k, :, pl.ds(r * width, width)], to.at[pl.ds(run * rows, rows)]))
        return pairs

    ins = [far(v) for v in (left, swap(left, Y), right, swap(right, X))]
    own, token = move(plan, sc, ins, [(4, 2, 2, runs * rows, width)], after, 12)
    shape = (COLUMNS, 2 * runs * rows, width)
    return own.reshape(shape), swap(own, CORE).reshape(shape), token


def add(a, b):
    return a.astype(F32) + b.astype(F32)


def fold_core(own, other, sc, after):
    _, rows2, columns = own.shape
    rows, half = rows2 // 2, columns // 2
    by_z = pl.BlockSpec((1, 2, 2, rows, columns), lambda i, *_: (i, 0, 0, 0, 0))
    to_z = pl.BlockSpec((1, 2, rows, half), lambda i, *_: (i, 0, 0, 0))
    left, right = pl.ds(0, half), pl.ds(half, half)

    def kernel(sc, own, got, ka, sa, kb, sb):
        for i in range(2):
            for a, b, flip in ((ka, kb, 0), (sa, sb, 1)):
                y, x = sc[2] ^ flip, sc[1] ^ flip
                a[0, i] = add(own[0, i, y, :, left], got[0, i, y, :, left]).astype(BF16)
                b[0, i] = add(own[0, x, i, :, right], got[0, x, i, :, right]).astype(BF16)

    ins = [(v.reshape(4, 2, 2, rows, columns), by_z) for v in (own, swap(other, CORE))]
    ka, sa, kb, sb, token = call(kernel, (4,), (sc,), ins, [((4, 2, rows, half), BF16, to_z)] * 4, (), after, mib=12)
    return [(ka, sa, Y), (kb, sb, X)], token


def columns_of(parts):
    rows = min(keep.shape[2] for keep, _, _ in parts)
    places, at = [], 0
    for n, (keep, _, _) in enumerate(parts):
        for first in range(0, keep.shape[2], rows):
            places.append((n, first, at, keep.shape[3]))
            at += keep.shape[3]
    return rows, at, places


def fold_first(parts, sc, after):
    groups = [[part for part in parts if part[2] == mask] for mask in (Y, X)]
    ins = [(v, full(v.shape)) for group in groups for keep, send, mask in group for v in (keep, swap(send, mask))]
    layouts = [columns_of(group) for group in groups]
    outs = [((4, rows, width), BF16, full((4, rows, width))) for rows, width, _ in layouts for _ in range(2)]

    def kernel(sc, *refs):
        ins, outs, base = refs[: len(ins_)], refs[len(ins_) :], 0
        for g, (rows, _, places) in enumerate(layouts):
            for n, first, at, width in places:
                keep, got = ins[base + 2 * n], ins[base + 2 * n + 1]
                cut = pl.ds(first, rows)
                for z in range(4):
                    for flip in range(2):
                        here = sc[1 + g] ^ flip
                        to = outs[2 * g + flip]
                        to[z, :, pl.ds(at, width)] = add(keep[z, here, cut], got[z, here, cut]).astype(BF16)
            base += 2 * len(groups[g])

    ins_ = ins
    out = call(kernel, (1,), (sc,), ins, outs, (), after, mib=16)
    return [(out[0], out[1], X), (out[2], out[3], Y)], out[4]


def fold_second(parts, sc, after):
    ins = [(v, full(v.shape)) for keep, send, mask in parts for v in (keep, swap(send, mask))]
    _, rows, width = parts[0][0].shape
    shape = (rows, 2 * width)

    def kernel(sc, *refs):
        ins, outs = refs[:4], refs[4:]
        for k, to in enumerate(outs):
            z = sc[3] ^ k
            for n in range(2):
                to[:, pl.ds(n * width, width)] = add(ins[2 * n][z], ins[2 * n + 1][z]).astype(to.dtype)

    outs = [(shape, F32, full(shape))] + [(shape, BF16, full(shape))] * 3
    return call(kernel, (1,), (sc,), ins, outs, (), after, mib=12)


def fold_sends(parts):
    keep, *sends, token = parts
    return token, [keep] + [swap(v, Z * k) for k, v in zip((1, 2, 3), sends)]


def fold_last(parts, shapes, runs, after):
    def kernel(keep, r1, r2, r3, *outs):
        rows = keep.shape[0]
        for i, (n, first, stride) in enumerate(runs):
            cut = (slice(None), pl.ds(i * 128, 128))
            total = keep[cut] + (r1[cut].astype(F32) + r2[cut].astype(F32) + r3[cut].astype(F32))
            outs[n][pl.ds(first, rows, stride=stride)] = total

    ins = [(v, full(v.shape)) for v in parts]
    return call(kernel, (1,), (), ins, [(shape, F32, full(shape)) for shape in shapes], (), after, mib=12)


def reduce_sends(v, masks):
    return [v] + [swap(v, mask) for mask in masks]


def reduce_level(ins, at, sc, after, split=None):
    v = ins[0]
    shapes, where = split or ([v.shape], [(0, pl.ds(i, 1)) for i in range(v.shape[0])])

    def kernel(sc, *refs):
        line, outs = refs[-1], refs[-1 - len(shapes) : -1]
        mine = sc[at[0]]
        for k in at[1:]:
            mine = 2 * mine + sc[k]
        for k, ref in enumerate(refs[: len(ins)]):
            line[mine ^ k] = ref[...]
        total = line[0]
        for k in range(1, len(ins)):
            total = total + line[k]
        for i, (n, place) in enumerate(where):
            row = total[i : i + 1]
            outs[n][place] = row[0] if len(shapes[n]) == 1 else row

    outs = [(shape, F32, full(shape)) for shape in shapes]
    scratch = [pltpu.VMEM((len(ins),) + v.shape, F32)]
    return call(kernel, (1,), (sc,), [(u, full(v.shape)) for u in ins], outs, scratch, after, mib=8)


def body(
    tokens,
    patch_grid,
    qkv_rows,
    proj_rows,
    fc1_rows,
    fc2_rows,
    norm_gain,
    norm_bias,
    qv_bias,
    proj_bias,
    fc1_bias,
    fc2_bias,
    layer_scale,
    cotangent,
):
    rows, width = tokens.shape
    packs, images, _ = patch_grid.shape
    pack = rows // packs
    slot = pack // images
    head = width // H
    hidden = fc1_bias.shape[0]
    row_width = qkv_rows.shape[1]
    tiles = hidden // width
    tile = min(256, rows)
    swaps = lax.axis_size("wide") == 16 and lax.axis_size("narrow") == 2
    if swaps:
        me = lax.axis_index(AXES)
        sc = jnp.stack([me // CORE % 2, me // X % 2, me % 2, me // Z]).astype(jnp.int32)
    else:
        sc = jnp.zeros((4,), jnp.int32)
    grid_flat = patch_grid.reshape(-1)
    thin, wide_rows = width // (2 * COLUMNS), hidden // (2 * COLUMNS)
    per_tile = COLUMNS // tiles

    by_pack = pl.BlockSpec((pack, width), lambda i, *_: (i, 0))
    by_tile = lambda w: pl.BlockSpec((tile, w), lambda i, *_: (i, 0))
    whole = full((rows, width))
    proj_blocks = pl.BlockSpec((COLUMNS, thin, width), lambda i, *_: (0, 0, 3), pipeline_mode=pl.Buffered(1))
    fc2_blocks = pl.BlockSpec((per_tile, wide_rows, width), lambda i, *_: (i, 0, 0))
    column_blocks = pl.BlockSpec((COLUMNS, thin, width), lambda i, *_: (0, 0, i))
    hidden_tile = pl.BlockSpec((rows, width), lambda i, *_: (0, i))
    vec1, vec2 = full((1, width)), full((2, width))
    hidden_vec = pl.BlockSpec((1, width), lambda i, *_: (0, i))
    qkv_blocks = full((COLUMNS, thin, 3 * width))
    qkv_scr = pltpu.VMEM((COLUMNS, 2, thin, 3 * width), BF16)
    fc2_scr = pltpu.VMEM((per_tile, 2, wide_rows, width), BF16)
    thin_scr = pltpu.VMEM((COLUMNS, 2, thin, width), BF16)
    sum_scr = pltpu.VMEM((rows, width), F32)
    turned_scr = pltpu.VMEM((width, rows), BF16)
    log_block = pl.BlockSpec((tile // slot * H, slot), lambda i, *_: (i, 0))

    halves = lambda v: v.reshape(COLUMNS, 2, -1, v.shape[1]).transpose(1, 0, 2, 3)
    ready = []
    if swaps:
        qp_block, fc1_block, a, b = pack_rows(qkv_rows, proj_rows, fc1_rows, fc2_rows, width, tiles)
        qp_line, fc1_line = gather_line(qp_block), gather_line(fc1_block)
        *qp_ab, message, _ = gather_stack(qp_line, sc, [], (a, swap(a, X), b, swap(b, Y)))
        fc2_line = gather_line(message)
        *qp_pair, token = gather_pair(*qp_ab, sc, [fc1_line[1], fc1_line[3]])
        ready = [token]
    else:
        qp_block = jnp.concatenate([qkv_rows.reshape(-1, 3 * width), proj_rows.reshape(-1, width)], axis=1)
        fc1_block, fc2_block = fc1_rows.reshape(-1, hidden), fc2_rows.reshape(-1, width)
        qp_own, qp_other = halves(lax.all_gather(qp_block, AXES, axis=0, tiled=True))
        fc1_own, fc1_other = halves(lax.all_gather(fc1_block, AXES, axis=0, tiled=True))
        fc2_own, fc2_other = halves(lax.all_gather(fc2_block, AXES, axis=0, tiled=True))

    x, n1, up, b2g, fc2_sums, token = call(
        partial(prepare_kernel, images=images),
        (packs,),
        (grid_flat,),
        [(far(tokens), by_pack), (far(cotangent), by_pack), (norm_gain, vec2), (norm_bias, vec2), (layer_scale, vec2)],
        [((rows, width), BF16, by_pack, "far")] * 4 + [((1, width), F32, vec1)],
        (),
        ready,
        mib=14,
    )

    ready = []
    if swaps:
        *fc1_ab, token = gather_stack(fc1_line, sc, [token, fc2_line[1]])
        qp_own, qp_other, token = gather_place(*qp_pair, sc, [token])
        ready = [token]

    offset = jnp.concatenate([qv_bias[0], jnp.zeros_like(qv_bias[0]), qv_bias[1]])[None]
    proj, att, log_total, token = call(
        partial(attend_kernel, slot=slot, head=head),
        (rows // tile,),
        (grid_flat, sc),
        [(far(n1), by_tile(width)), (qp_own, qkv_blocks), (qp_other, qkv_blocks), (offset, full((1, 3 * width)))],
        [((rows, 3 * width), BF16, by_tile(3 * width), "far"), ((rows, width), BF16, by_tile(width))]
        + [((rows // slot * H, slot), F32, log_block)],
        [qkv_scr],
        ready,
        mib=24,
    )
    ready = []
    if swaps:
        *fc1_pair, token = gather_pair(*fc1_ab, sc, [token, fc2_line[2]])
        ready = [token]
    b1, n2, token = call(
        middle_kernel,
        (1,),
        (sc,),
        [(att, whole), (x, whole), (norm_gain, vec2), (norm_bias, vec2), (layer_scale, vec2), (proj_bias[None], vec1)]
        + [(qp_own, proj_blocks), (qp_other, proj_blocks)],
        [((rows, width), F32, whole, "far"), ((rows, width), BF16, whole)],
        [sum_scr, thin_scr],
        ready,
        mib=20,
    )
    ready = []
    if swaps:
        *fc2_pair, token = gather_columns(fc2_line, sc, [token])
        fc1_own, fc1_other, token = gather_place(*fc1_pair, sc, [token])
        ready = [token]
    cut = tiles - 1

    def some_tiles(first, count, after, alias=None):
        columns = pl.BlockSpec((COLUMNS, thin, width), lambda i, *_: (0, 0, i + first))
        outs = pl.BlockSpec((rows, width), lambda i, *_: (0, i + first))
        blocks = pl.BlockSpec((per_tile, wide_rows, width), lambda i, *_: (i + first, 0, 0))
        return call(
            hidden_kernel,
            (count,),
            (sc,),
            [(n2, whole), (b2g, whole), (fc1_bias[None], pl.BlockSpec((1, width), lambda i, *_: (0, i + first)))]
            + [(fc1_own, columns), (fc1_other, columns)],
            [((rows, hidden), BF16, outs, "far"), ((rows, hidden), F32, outs, "far")]
            + [((COLUMNS, wide_rows, width), BF16, blocks, "far")] * 2,
            [thin_scr],
            after,
            mib=24,
            alias=alias,
        )

    *made, token = some_tiles(0, cut, ready)
    if swaps:
        fc2_own, fc2_other, token = gather_place(*fc2_pair, sc, [token], tiles)
    *made, token = some_tiles(cut, tiles - cut, made + [token], {i: i for i in range(4)})
    act, slope, fc2g_own, fc2g_other = made

    hg, fc1_sums, fc1g_own, fc1g_other, token = call(
        hidden_back_kernel,
        (tiles,),
        (sc,),
        [(far(b2g), whole), (far(n2), whole), (far(slope), hidden_tile), (fc2_own, fc2_blocks), (fc2_other, fc2_blocks)],
        [((rows, hidden), BF16, hidden_tile, "far"), ((1, hidden), F32, hidden_vec)]
        + [((COLUMNS, thin, hidden), BF16, column_blocks, "far")] * 2,
        [turned_scr, fc2_scr],
        mib=28,
    )
    chain = []
    if swaps:
        fc2_parts, token = fold_core(fc2g_own, fc2g_other, sc, [token])
        chain = [token]

    bound = lambda i: jnp.minimum(i, tiles - 1)
    hidden_first = pl.BlockSpec((rows, width), lambda i, *_: (0, bound(i)))
    column_first = pl.BlockSpec((COLUMNS, thin, width), lambda i, *_: (0, 0, bound(i)))
    fc2_first = pl.BlockSpec((per_tile, wide_rows, width), lambda i, *_: (bound(i), 0, 0))
    then = lambda size: pl.BlockSpec((size, width), lambda i, *_: (jnp.maximum(i - tiles, 0), 0))
    mg, b1g, ag, middle_sums, token = call(
        partial(middle_back_kernel, tiles=tiles),
        (tiles + rows // tile,),
        (sc,),
        [(far(hg), hidden_first), (fc1_own, column_first), (fc1_other, column_first)]
        + [(qp_own, proj_blocks), (qp_other, proj_blocks)]
        + [(b1, then(tile)), (x, then(tile)), (up, then(tile)), (norm_gain, vec2), (layer_scale, vec2)],
        [((rows, width), F32, then(tile), "far"), ((rows, width), BF16, then(tile)), ((rows, width), BF16, then(tile))]
        + [((4, width), F32, full((4, width)))],
        [sum_scr, thin_scr, thin_scr],
        chain,
        mib=28,
    )
    chain = []
    if swaps:
        fc1_parts, token = fold_core(fc1g_own, fc1g_other, sc, [token])
        chain = [token]

    pg, proj_sums, token = call(
        partial(attend_back_kernel, slot=slot, head=head),
        (rows // tile,),
        (grid_flat,),
        [(far(proj), by_tile(3 * width)), (ag, by_tile(width)), (log_total, log_block)],
        [((rows, 3 * width), BF16, by_tile(3 * width)), ((8, 3 * width), F32, full((8, 3 * width)))],
        (),
        chain,
        mib=14,
    )
    chain = []
    if swaps:
        fc_parts, token = fold_first(fc1_parts + fc2_parts, sc, [token])
        chain = [token]

    qp_grad_own, qp_grad_other, token = call(
        weight_kernel,
        (4,),
        (sc,),
        [(n1, whole), (att, whole), (pg, pl.BlockSpec((rows, width), lambda i, *_: (0, jnp.minimum(i, 2)))), (b1g, whole)],
        [((COLUMNS, thin, 4 * width), BF16, column_blocks)] * 2,
        [turned_scr],
        chain,
        mib=18,
    )
    layer_out, out_sums, token = call(
        partial(layer_out_kernel, images=images, tiles=tiles),
        (tiles + packs,),
        (grid_flat, sc),
        [(far(act), hidden_first), (fc2_own, fc2_first), (fc2_other, fc2_first), (x, then(pack)), (b1, then(pack)), (up, then(pack))]
        + [(layer_scale, vec2), (fc2_bias[None], vec1)],
        [((rows, width), BF16, then(pack), "far"), ((1, width), F32, vec1)],
        [sum_scr, pltpu.VMEM((pack, width), BF16), fc2_scr],
        [token],
        mib=26,
    )
    chain = []
    if swaps:
        qp_parts, token = fold_core(qp_grad_own, qp_grad_other, sc, [token])
        token, fc_parts = fold_sends(fold_second(fc_parts, sc, [token]))
        chain = [token]

    input_grad, input_sums, token = call(
        partial(input_back_kernel, images=images),
        (packs,),
        (grid_flat, sc),
        [(pg, pl.BlockSpec((pack, 3 * width), lambda i, *_: (i, 0))), (qp_own, qkv_blocks), (qp_other, qkv_blocks)]
        + [(x, by_pack), (mg, by_pack), (norm_gain, vec2)],
        [((rows, width), F32, by_pack, "far"), ((2, width), F32, vec2)],
        [qkv_scr, pltpu.VMEM((pack, width), F32)] + [pltpu.VMEM((pack, width), BF16)] * 2,
        chain,
        mib=26,
    )

    chain = []
    if swaps:
        qp_parts, token = fold_first(qp_parts, sc, [token, fc_parts[1], fc_parts[3]])
        chain = [token]

    def gather_sums(input_sums, middle, proj, fc2, out, fc1, to):
        q, v = column_sum(proj[:, pl.ds(0, width)]), column_sum(proj[:, pl.ds(2 * width, width)])
        lines = (input_sums[0:1], middle[2:3], input_sums[1:2], middle[3:4], q, v, middle[1:2], fc2[...], middle[0:1], out[...])
        for i, line in enumerate(lines):
            to[pl.ds(i, 1)] = line
        for i in range(tiles):
            to[pl.ds(len(lines) + i, 1)] = fc1[:, pl.ds(i * width, width)]

    sums_in = (input_sums, middle_sums, proj_sums, fc2_sums, out_sums, fc1_sums)
    sums, token = call(
        gather_sums,
        (1,),
        (),
        [(v, full(v.shape)) for v in sums_in],
        [((10 + tiles, width), F32, full((10 + tiles, width)))],
        (),
        chain,
    )
    if swaps:
        fc2_rows_of = fc2_rows.shape[0] // tiles
        n1_runs, n2_runs = hidden // 256, width // 256
        fc_runs = []
        for half in range(2):
            fc_runs += [(0, half * n1_runs + i, hidden // 128) for i in range(n1_runs)]
            fc_runs += [(1, k * fc2_rows_of + half * n2_runs + i, width // 128) for k in range(tiles) for i in range(n2_runs)]
        sums, token = reduce_level(reduce_sends(sums, (CORE,)), (0,), sc, [token])
        sums, token = reduce_level(reduce_sends(sums, (Y,)), (2,), sc, [token])
        token, qp_parts = fold_sends(fold_second(qp_parts, sc, [token, fc_parts[2]]))
        sums, token = reduce_level(reduce_sends(sums, (X,)), (1,), sc, [token])
        fc1_grad, fc2_grad, token = fold_last(fc_parts, (fc1_rows.shape, fc2_rows.shape), fc_runs, [token, qp_parts[1]])
        line = lambda i: pl.ds(i * width, width)
        shapes = [(2, width)] * 3 + [(width,), (hidden,), (width,), (2, width)]
        where = [(i // 2, pl.ds(i % 2, 1)) for i in range(6)] + [(3, line(0)), (5, line(0))]
        where += [(6, pl.ds(0, 1)), (6, pl.ds(1, 1))] + [(4, line(i)) for i in range(tiles)]
        sums = reduce_sends(sums, (Z, 2 * Z, 3 * Z))
        *small, token = reduce_level(sums, (3,), sc, [token] + qp_parts[2:], (shapes, where))
        qkv_runs, proj_runs = 3 * width // 128, width // 128
        qp_runs = [(0, i, qkv_runs) for i in range(qkv_runs)] + [(1, i, proj_runs) for i in range(proj_runs)]
        qkv_grad, proj_grad, _ = fold_last(qp_parts, (qkv_rows.shape, proj_rows.shape), qp_runs, [token])
    else:

        def scatter(own, other):
            matrix = jnp.stack([own, other], axis=1).reshape(-1, own.shape[-1])
            return lax.psum_scatter(matrix, AXES, scatter_dimension=0, tiled=True).astype(F32)

        fc2_grad = scatter(fc2g_own, fc2g_other).reshape(-1, row_width)
        fc1_grad = scatter(fc1g_own, fc1g_other).reshape(-1, row_width)
        qp_grad = scatter(qp_grad_own, qp_grad_other)
        qkv_grad = qp_grad[:, : 3 * width].reshape(-1, row_width)
        proj_grad = qp_grad[:, 3 * width :].reshape(-1, row_width)
        sums = lax.psum(sums, AXES)
        small = [sums[0:2], sums[2:4], sums[4:6], sums[6], sums[10:].reshape(-1), sums[7], sums[8:10]]
    return (
        layer_out,
        input_grad,
        qkv_grad,
        proj_grad,
        fc1_grad,
        fc2_grad,
        *(v.reshape(leaf.shape) for v, leaf in zip(small, (norm_gain, norm_bias, qv_bias, proj_bias, fc1_bias, fc2_bias, layer_scale))),
    )


def solution(mesh):
    split = P(AXES, None)
    return jax.shard_map(
        body,
        mesh=mesh,
        in_specs=(split, P(AXES, None, None)) + (split,) * 4 + (P(),) * 7 + (split,),
        out_specs=(split,) * 6 + (P(),) * 7,
        check_vma=False,
    )
```

```python
from functools import partial

import jax
import jax.numpy as jnp
from jax import lax
from jax.experimental import pallas as pl
from jax.experimental.pallas import tpu as pltpu
from jax.sharding import PartitionSpec as P

H = 12
PREFIX = 5
EPSILON = 1e-06
NEGATIVE = -1e30
AXES = ("wide", "narrow")
COLUMNS = 8
BF16 = jnp.bfloat16
F32 = jnp.float32


def dot(a, b):
    return lax.dot_general(a, b, (((1,), (0,)), ((), ())), preferred_element_type=F32)


def dot_nt(a, b):
    return lax.dot_general(a, b, (((1,), (1,)), ((), ())), preferred_element_type=F32)


def dot_tn(a, b):
    return lax.dot_general(a, b, (((0,), (0,)), ((), ())), preferred_element_type=F32)


TOKEN = (8, 128)


def call(kernel, grid, scalars, ins, outs, scratch=(), after=(), mib=36, alias=None):
    n, m = len(scalars) + len(ins), len(outs)

    def run(*refs):
        rest = refs[n + len(after) :]
        rest[m][...] = jnp.zeros(TOKEN, F32)
        kernel(*refs[:n], *rest[:m], *rest[m + 1 :])

    anywhere = pl.BlockSpec(memory_space=pl.ANY)
    return pl.pallas_call(
        run,
        grid_spec=pltpu.PrefetchScalarGridSpec(
            num_scalar_prefetch=len(scalars),
            grid=grid,
            in_specs=[spec for _, spec in ins] + [anywhere] * len(after),
            out_specs=[out[2] for out in outs] + [full(TOKEN)],
            scratch_shapes=list(scratch),
        ),
        out_shape=[
            pltpu.HBM(out[0], out[1]) if len(out) > 3 else jax.ShapeDtypeStruct(out[0], out[1]) for out in outs
        ]
        + [jax.ShapeDtypeStruct(TOKEN, F32)],
        input_output_aliases={n + k: to for k, to in (alias or {}).items()},
        compiler_params=pltpu.CompilerParams(vmem_limit_bytes=mib * 2**20),
        cost_estimate=pl.CostEstimate(flops=1, bytes_accessed=1, transcendentals=0),
    )(*scalars, *(array for array, _ in ins), *after)


def far(v):
    return pltpu.with_memory_space_constraint(v, pltpu.HBM)


def full(shape):
    return pl.BlockSpec(shape, lambda *_: (0,) * len(shape), pipeline_mode=pl.Buffered(1))


def standardize(v):
    centered = v - jnp.mean(v, axis=-1, keepdims=True)
    inverse = lax.rsqrt(jnp.mean(centered * centered, axis=-1, keepdims=True) + EPSILON)
    return centered * inverse, inverse


def standardize_back(grad, scaled, inverse):
    return inverse * (
        grad
        - jnp.mean(grad, axis=-1, keepdims=True)
        - scaled * jnp.mean(grad * scaled, axis=-1, keepdims=True)
    )


def length_of(grid_ref, image):
    return PREFIX + grid_ref[2 * image] * grid_ref[2 * image + 1]


def spans(grid_ref, pack, images):
    found, start = [], 0
    for i in range(images):
        length = length_of(grid_ref, pack * images + i)
        found.append((start, length))
        start = start + length
    return found


def join(scr, core, own, other):
    for i in range(scr.shape[0]):
        scr[i, core] = own[i]
        scr[i, 1 - core] = other[i]
    blocks, cores, rows, columns = scr.shape
    return scr[...].reshape(blocks * cores * rows, columns)


def part(core, matrix, own, other):
    blocks, rows, columns = own.shape
    cut = matrix.reshape(blocks, 2, rows, columns)
    own[...] = jnp.where(core == 0, cut[:, 0], cut[:, 1])
    other[...] = jnp.where(core == 0, cut[:, 1], cut[:, 0])


def prepare_kernel(grid_ref, tok, cot, gain, bias, ls, x, n1, up, b2g, sums, *, images):
    pack = pl.program_id(0)
    slot = tok.shape[0] // images
    row = lax.broadcasted_iota(jnp.int32, (slot, tok.shape[0]), 0)
    column = lax.broadcasted_iota(jnp.int32, (slot, tok.shape[0]), 1)

    def image(i, carry):
        start, total = carry
        length = length_of(grid_ref, pack * images + i)
        place = jnp.where((column - row == start) & (row < length), 1.0, 0.0).astype(BF16)
        rows = pl.ds(pl.multiple_of(i * slot, slot), slot)
        moved = dot(place, tok[...])
        x[rows] = moved.astype(BF16)
        scaled, _ = standardize(moved)
        n1[rows] = (scaled * gain[0:1] + bias[0:1]).astype(BF16)
        upstream = dot(place, cot[...])
        up[rows] = upstream.astype(BF16)
        low = (ls[1:2] * upstream).astype(BF16)
        b2g[rows] = low
        return start + length, total + column_sum(low.astype(F32))

    _, total = lax.fori_loop(0, images, image, (jnp.int32(0), jnp.zeros((1, tok.shape[1]), F32)))

    @pl.when(pack == 0)
    def _():
        sums[...] = jnp.zeros_like(sums)

    sums[...] += total


def unplace(grid_ref, pack, images, size):
    slot = size // images
    row = lax.broadcasted_iota(jnp.int32, (size, slot), 0)
    column = lax.broadcasted_iota(jnp.int32, (size, slot), 1)
    return jnp.concatenate(
        [
            jnp.where((row - column == start) & (column < length), 1.0, 0.0).astype(BF16)
            for start, length in spans(grid_ref, pack, images)
        ],
        axis=1,
    )


def pieces(rows, size=128):
    return [pl.ds(r, size) for r in range(0, rows, size)]


def eights(v):
    return jnp.sum(v.reshape(-1, 8, v.shape[1]), axis=0)


def column_sum(v):
    return jnp.sum(v, axis=0, keepdims=True)


def stacked(v, low):
    zero = jnp.zeros_like(v)
    return jnp.concatenate([jnp.where(low, v, zero), jnp.where(low, zero, v)], axis=0)


def attend_kernel(grid_ref, sc, n1, own, other, offset, proj, att, log_total, scr, *, slot, head):
    step = pl.program_id(0)
    width = n1.shape[1]
    per = n1.shape[0] // slot
    pair = 2 * head
    heads = width // head

    @pl.when(step == 0)
    def _():
        join(scr, sc[0], own, other)

    w = scr[...].reshape(width, 3 * width)
    proj[...] = (dot(n1[...], w) + offset[...]).astype(BF16)
    low = lax.broadcasted_iota(jnp.int32, (slot, pair), 1) < head
    key_at = lax.broadcasted_iota(jnp.int32, (slot, slot), 0)
    for i in range(per):
        ok = key_at < length_of(grid_ref, step * per + i)
        rows = pl.ds(i * slot, slot)
        found = []
        for j in range(width // pair):
            q, k = (proj[rows, pl.ds(t * width + j * pair, pair)] for t in range(2))
            scores = dot_nt(stacked(k, low), q * jnp.asarray(head ** (-0.5), BF16))
            halves = []
            for h in range(2):
                masked = jnp.where(ok, scores[h * slot : (h + 1) * slot], NEGATIVE)
                top = jnp.max(masked, axis=0, keepdims=True)
                exponent = jnp.exp(masked - top)
                total = column_sum(exponent)
                halves.append((exponent * (1.0 / total)).astype(BF16))
                log_total[pl.ds(i * heads + 2 * j + h, 1)] = top + jnp.log(total)
            found.append(jnp.concatenate(halves, axis=0))
        for j, p in enumerate(found):
            v = proj[rows, pl.ds(2 * width + j * pair, pair)]
            att[rows, pl.ds(j * pair, pair)] = dot_tn(p, stacked(v, low)).astype(BF16)


def middle_kernel(sc, att, x, gain, bias, ls, proj_bias, own, other, b1, n2, acc, scr):
    acc[...] = dot(att[...], join(scr, sc[0], own, other))
    for rows in pieces(acc.shape[0]):
        branch = acc[rows] + proj_bias[...]
        b1[rows] = branch
        scaled, _ = standardize(x[rows].astype(F32) + ls[0:1] * branch)
        n2[rows] = (scaled * gain[1:2] + bias[1:2]).astype(BF16)


def hidden_kernel(sc, n2, b2g, fc1_bias, own, other, act, slope, go, gs, scr):
    w1 = join(scr, sc[0], own, other)
    for rows in pieces(n2.shape[0], 256):
        hidden = dot(n2[rows], w1) + fc1_bias[...]
        normal = 0.5 * (1.0 + lax.erf(hidden * 0.5**0.5))
        act[rows] = (hidden * normal).astype(BF16)
        density = (0.5 / jnp.pi) ** 0.5 * jnp.exp(-0.5 * hidden * hidden)
        slope[rows] = normal + hidden * density
    part(sc[0], dot_tn(act[...], b2g[...]).astype(BF16), go, gs)


def hidden_back_kernel(sc, b2g, n2, slope, own, other, hg, sums, go, gs, n2t, scr):
    @pl.when(pl.program_id(0) == 0)
    def _():
        n2t[...] = n2[...].T

    w2 = join(scr, sc[0], own, other)
    total = jnp.zeros((8, sums.shape[1]), F32)
    for rows in pieces(b2g.shape[0], 256):
        low = (dot_nt(b2g[rows], w2) * slope[rows]).astype(BF16)
        hg[rows] = low
        total = total + eights(low.astype(F32))
    sums[...] = column_sum(total)
    part(sc[0], dot(n2t[...], hg[...]).astype(BF16), go, gs)


def middle_back_kernel(sc, hg, own, other, po, ps, b1, x, up, gain, ls, mg, b1g, ag, sums, acc, scr, pscr, *, tiles):
    step = pl.program_id(0)

    @pl.when(step == 0)
    def _():
        acc[...] = jnp.zeros_like(acc)

    @pl.when(step < tiles)
    def _():
        acc[...] += dot_nt(hg[...], join(scr, sc[0], own, other))

    @pl.when(step == tiles)
    def _():
        join(pscr, sc[0], po, ps)
        sums[...] = jnp.zeros_like(sums)

    @pl.when(step >= tiles)
    def _():
        size = x.shape[0]
        totals = [jnp.zeros((8, x.shape[1]), F32) for _ in range(4)]
        for rows in pieces(size):
            branch = b1[rows]
            scaled, inverse = standardize(x[rows].astype(F32) + ls[0:1] * branch)
            grad = acc[pl.ds(pl.multiple_of((step - tiles) * size + rows.start, 128), rows.size)]
            back = up[rows].astype(F32) + standardize_back(grad * gain[1:2], scaled, inverse)
            mg[rows] = back
            low = (ls[0:1] * back).astype(BF16)
            b1g[rows] = low
            terms = (back * branch, low.astype(F32), grad * scaled, grad)
            totals = [t + eights(v) for t, v in zip(totals, terms)]
        ag[...] = dot_nt(b1g[...], pscr[...].reshape(x.shape[1], x.shape[1])).astype(BF16)
        sums[...] += jnp.concatenate([column_sum(t) for t in totals], axis=0)


def attend_back_kernel(grid_ref, proj, ag, log_total, pg, sums, *, slot, head):
    step = pl.program_id(0)
    width = ag.shape[1]
    per = ag.shape[0] // slot
    pair = 2 * head
    heads = width // head
    factor = head ** (-0.5)
    low = lax.broadcasted_iota(jnp.int32, (slot, pair), 1) < head
    key_at = lax.broadcasted_iota(jnp.int32, (slot, slot), 0)

    @pl.when(step == 0)
    def _():
        sums[...] = jnp.zeros_like(sums)

    for i in range(per):
        ok = key_at < length_of(grid_ref, step * per + i)
        rows = pl.ds(i * slot, slot)
        found = []

        def put(t, j, d):
            d = d.astype(BF16)
            columns = pl.ds(t * width + j * pair, pair)
            pg[rows, columns] = d
            if t != 1:
                sums[:, columns] += eights(d.astype(F32))

        for j in range(width // pair):
            q, k, v = (proj[rows, pl.ds(t * width + j * pair, pair)] for t in range(3))
            out = ag[rows, pl.ds(j * pair, pair)]
            q = q * jnp.asarray(factor, BF16)
            k2 = stacked(k, low)
            scores = dot_nt(k2, q)
            pull = dot_nt(stacked(v, low), out)
            ps, ss = [], []
            for h in range(2):
                half = slice(h * slot, (h + 1) * slot)
                p = jnp.exp(jnp.where(ok, scores[half], NEGATIVE) - log_total[pl.ds(i * heads + 2 * j + h, 1)])
                g = pull[half]
                ps.append(p.astype(BF16))
                ss.append((p * (g - column_sum(g * p))).astype(BF16))
            s = jnp.concatenate(ss, axis=0)
            dk = dot(s, q)
            dv = dot(jnp.concatenate(ps, axis=0), out)
            put(1, j, jnp.where(low, dk[:slot], dk[slot:]))
            put(2, j, jnp.where(low, dv[:slot], dv[slot:]))
            found.append((s, k2))
        for j, (s, k2) in enumerate(found):
            put(0, j, dot_tn(s, k2) * factor)


def weight_kernel(sc, n1, att, pg, b1g, go, gs, n1t):
    step = pl.program_id(0)
    last = pl.num_programs(0) - 1

    @pl.when(step == 0)
    def _():
        n1t[...] = n1[...].T

    @pl.when(step < last)
    def _():
        part(sc[0], dot(n1t[...], pg[...]).astype(BF16), go, gs)

    @pl.when(step == last)
    def _():
        part(sc[0], dot_tn(att[...], b1g[...]).astype(BF16), go, gs)


def input_back_kernel(grid_ref, sc, pg, own, other, x, mg, gain, out, sums, scr, acc, high, mid, *, images):
    pack = pl.program_id(0)

    @pl.when(pack == 0)
    def _():
        join(scr, sc[0], own, other)
        sums[...] = jnp.zeros_like(sums)

    width = x.shape[1]
    acc[...] = dot_nt(pg[...], scr[...].reshape(width, 3 * width))
    totals = [jnp.zeros((8, width), F32) for _ in range(2)]
    for rows in pieces(acc.shape[0]):
        grad = acc[rows]
        scaled, inverse = standardize(x[rows].astype(F32))
        back = mg[rows] + standardize_back(grad * gain[0:1], scaled, inverse)
        totals = [t + eights(v) for t, v in zip(totals, (grad * scaled, grad))]
        big = back.astype(BF16)
        high[rows] = big
        mid[rows] = (back - big.astype(F32)).astype(BF16)
    sums[...] += jnp.concatenate([column_sum(t) for t in totals], axis=0)
    place = unplace(grid_ref, pack, images, x.shape[0])
    out[...] = dot(place, high[...]) + dot(place, mid[...])


def layer_out_kernel(grid_ref, sc, act, own, other, x, b1, up, ls, fc2_bias, out, sums, acc, result, scr, *, images, tiles):
    step = pl.program_id(0)

    @pl.when(step == 0)
    def _():
        acc[...] = jnp.zeros_like(acc)

    @pl.when(step < tiles)
    def _():
        acc[...] += dot(act[...], join(scr, sc[0], own, other))

    @pl.when(step == tiles)
    def _():
        sums[...] = jnp.zeros_like(sums)

    @pl.when(step >= tiles)
    def _():
        pack, size = step - tiles, out.shape[0]
        total = jnp.zeros((8, x.shape[1]), F32)
        for rows in pieces(size):
            branch = acc[pl.ds(pl.multiple_of(pack * size + rows.start, 128), rows.size)] + fc2_bias[...]
            total = total + eights(up[rows].astype(F32) * branch)
            middle = x[rows].astype(F32) + ls[0:1] * b1[rows]
            result[rows] = (middle + ls[1:2] * branch).astype(BF16)
        out[...] = dot(unplace(grid_ref, pack, images, size), result[...]).astype(BF16)
        sums[...] += column_sum(total)


Y, CORE, X, Z = 1, 2, 4, 8


def swap(v, mask):
    return lax.ppermute(v, AXES, [(i, i ^ mask) for i in range(32)])


def move(plan, sc, ins, outs, after, mib=8):
    def kernel(*refs):
        for a, b in plan(*refs):
            b[...] = a[...]

    return call(
        kernel, (1,), (sc,), [(v, full(v.shape)) for v in ins], [(shape, BF16, full(shape)) for shape in outs], (), after, mib
    )


def gather_line(block):
    return [block] + [swap(block, Z * k) for k in (1, 2, 3)]


def gather_stack(line, sc, after, sides=()):
    rows, columns = line[0].shape
    half = columns // 2
    shapes = [(4, rows, half)] * 2 + [(2, 2) + side.shape for side in sides[:1]]

    def plan(sc, *refs):
        ins, outs = refs[: 4 + len(sides)], refs[4 + len(sides) :]
        pairs = [(ins[k].at[:, pl.ds(h * half, half)], outs[h].at[k]) for k in range(4) for h in range(2)]
        return pairs + [(side, outs[2].at[i // 2, i % 2]) for i, side in enumerate(ins[4:])]

    return move(plan, sc, [*line, *sides], shapes, after)


def gather_columns(line, sc, after):
    _, _, rows, half = line[0].shape

    def plan(sc, *refs):
        return [(refs[k].at[h, i], refs[4 + h].at[i, k]) for k in range(4) for h in range(2) for i in range(2)]

    return move(plan, sc, line, [(2, 4, rows, half)] * 2, after)


def pack_rows(qkv, proj, fc1, fc2, width, tiles):
    arrays = (qkv, proj, fc1, fc2)
    rows = proj.shape[0] * 128 // width
    columns = [v.shape[0] * 128 // rows for v in arrays]
    places = [(0, 0), (0, columns[0]), (1, 0), (2, 0)]
    half = columns[3] // 2

    def kernel(*refs):
        ins, outs, scrs = refs[:4], refs[4:8], refs[8:]
        for n, (ref, scr) in enumerate(zip(ins, scrs)):
            scr[...] = ref[...].astype(F32)
            if n < 3:
                blocks = [(i, columns[n] // 128) for i in range(columns[n] // 128)]
            else:
                lanes = width // 128
                blocks = [(k * rows * lanes + i, lanes) for k in range(tiles) for i in range(lanes)]
            for i, (start, stride) in enumerate(blocks):
                to, at = places[n]
                at += i * 128
                if n == 3:
                    to, at = to + at // half, at % half
                outs[to][:, pl.ds(at, 128)] = scr[pl.ds(start, rows, stride=stride)].astype(BF16)

    shapes = [(rows, columns[0] + columns[1]), (rows, columns[2]), (rows, half), (rows, half)]
    scratch = [pltpu.VMEM(v.shape, F32) for v in arrays]
    outs = [(shape, BF16, full(shape)) for shape in shapes]
    return call(kernel, (1,), (), [(v, full(v.shape)) for v in arrays], outs, scratch, (), mib=8)[:4]


def gather_pair(a, b, sc, after):
    def plan(sc, a, xa, b, yb, left, right):
        return [(a, left.at[0]), (xa, left.at[1]), (b, right.at[0]), (yb, right.at[1])]

    return move(plan, sc, (a, swap(a, X), b, swap(b, Y)), [(2,) + a.shape] * 2, after)


def gather_place(left, right, sc, after, runs=1):
    _, _, rows, half = left.shape
    width = 2 * half // runs

    def plan(sc, left, other_left, right, other_right, out):
        pairs = []
        for n, sides in enumerate(((left, other_left), (right, other_right))):
            for i in range(2):
                for j in range(2):
                    for k in range(4):
                        x, y = (i, j) if n == 0 else (j, i)
                        to = out.at[sc[3] ^ k, sc[1] ^ x, sc[2] ^ y]
                        if runs == 1:
                            pairs.append((sides[j].at[i, k], to.at[:, pl.ds(n * half, half)]))
                            continue
                        for r in range(runs // 2):
                            run = n * (runs // 2) + r
                            pairs.append((sides[j].at[i, k, :, pl.ds(r * width, width)], to.at[pl.ds(run * rows, rows)]))
        return pairs

    ins = [far(v) for v in (left, swap(left, Y), right, swap(right, X))]
    own, token = move(plan, sc, ins, [(4, 2, 2, runs * rows, width)], after, 12)
    shape = (COLUMNS, 2 * runs * rows, width)
    return own.reshape(shape), swap(own, CORE).reshape(shape), token


def add(a, b):
    return a.astype(F32) + b.astype(F32)


def fold_core(own, other, sc, after):
    _, rows2, columns = own.shape
    rows, half = rows2 // 2, columns // 2
    by_z = pl.BlockSpec((1, 2, 2, rows, columns), lambda i, *_: (i, 0, 0, 0, 0))
    to_z = pl.BlockSpec((1, 2, rows, half), lambda i, *_: (i, 0, 0, 0))
    left, right = pl.ds(0, half), pl.ds(half, half)

    def kernel(sc, own, got, ka, sa, kb, sb):
        for i in range(2):
            for a, b, flip in ((ka, kb, 0), (sa, sb, 1)):
                y, x = sc[2] ^ flip, sc[1] ^ flip
                a[0, i] = add(own[0, i, y, :, left], got[0, i, y, :, left]).astype(BF16)
                b[0, i] = add(own[0, x, i, :, right], got[0, x, i, :, right]).astype(BF16)

    ins = [(v.reshape(4, 2, 2, rows, columns), by_z) for v in (own, swap(other, CORE))]
    ka, sa, kb, sb, token = call(kernel, (4,), (sc,), ins, [((4, 2, rows, half), BF16, to_z)] * 4, (), after, mib=12)
    return [(ka, sa, Y), (kb, sb, X)], token


def columns_of(parts):
    rows = min(keep.shape[2] for keep, _, _ in parts)
    places, at = [], 0
    for n, (keep, _, _) in enumerate(parts):
        for first in range(0, keep.shape[2], rows):
            places.append((n, first, at, keep.shape[3]))
            at += keep.shape[3]
    return rows, at, places


def fold_first(parts, sc, after):
    groups = [[part for part in parts if part[2] == mask] for mask in (Y, X)]
    ins = [(v, full(v.shape)) for group in groups for keep, send, mask in group for v in (keep, swap(send, mask))]
    layouts = [columns_of(group) for group in groups]
    outs = [((4, rows, width), BF16, full((4, rows, width))) for rows, width, _ in layouts for _ in range(2)]

    def kernel(sc, *refs):
        ins, outs, base = refs[: len(ins_)], refs[len(ins_) :], 0
        for g, (rows, _, places) in enumerate(layouts):
            for n, first, at, width in places:
                keep, got = ins[base + 2 * n], ins[base + 2 * n + 1]
                cut = pl.ds(first, rows)
                for z in range(4):
                    for flip in range(2):
                        here = sc[1 + g] ^ flip
                        to = outs[2 * g + flip]
                        to[z, :, pl.ds(at, width)] = add(keep[z, here, cut], got[z, here, cut]).astype(BF16)
            base += 2 * len(groups[g])

    ins_ = ins
    out = call(kernel, (1,), (sc,), ins, outs, (), after, mib=16)
    return [(out[0], out[1], X), (out[2], out[3], Y)], out[4]


def fold_second(parts, sc, after):
    ins = [(v, full(v.shape)) for keep, send, mask in parts for v in (keep, swap(send, mask))]
    _, rows, width = parts[0][0].shape
    shape = (rows, 2 * width)

    def kernel(sc, *refs):
        ins, outs = refs[:4], refs[4:]
        for k, to in enumerate(outs):
            z = sc[3] ^ k
            for n in range(2):
                to[:, pl.ds(n * width, width)] = add(ins[2 * n][z], ins[2 * n + 1][z]).astype(to.dtype)

    outs = [(shape, F32, full(shape))] + [(shape, BF16, full(shape))] * 3
    return call(kernel, (1,), (sc,), ins, outs, (), after, mib=12)


def fold_sends(parts):
    keep, *sends, token = parts
    return token, [keep] + [swap(v, Z * k) for k, v in zip((1, 2, 3), sends)]


def fold_last(parts, shapes, runs, after):
    def kernel(keep, r1, r2, r3, *outs):
        rows = keep.shape[0]
        for i, (n, first, stride) in enumerate(runs):
            cut = (slice(None), pl.ds(i * 128, 128))
            total = keep[cut] + (r1[cut].astype(F32) + r2[cut].astype(F32) + r3[cut].astype(F32))
            outs[n][pl.ds(first, rows, stride=stride)] = total

    ins = [(v, full(v.shape)) for v in parts]
    return call(kernel, (1,), (), ins, [(shape, F32, full(shape)) for shape in shapes], (), after, mib=12)


def reduce_sends(v, masks):
    return [v] + [swap(v, mask) for mask in masks]


def reduce_level(ins, at, sc, after, split=None):
    v = ins[0]
    shapes, where = split or ([v.shape], [(0, pl.ds(i, 1)) for i in range(v.shape[0])])

    def kernel(sc, *refs):
        line, outs = refs[-1], refs[-1 - len(shapes) : -1]
        mine = sc[at[0]]
        for k in at[1:]:
            mine = 2 * mine + sc[k]
        for k, ref in enumerate(refs[: len(ins)]):
            line[mine ^ k] = ref[...]
        total = line[0]
        for k in range(1, len(ins)):
            total = total + line[k]
        for i, (n, place) in enumerate(where):
            row = total[i : i + 1]
            outs[n][place] = row[0] if len(shapes[n]) == 1 else row

    outs = [(shape, F32, full(shape)) for shape in shapes]
    scratch = [pltpu.VMEM((len(ins),) + v.shape, F32)]
    return call(kernel, (1,), (sc,), [(u, full(v.shape)) for u in ins], outs, scratch, after, mib=8)


def body(
    tokens,
    patch_grid,
    qkv_rows,
    proj_rows,
    fc1_rows,
    fc2_rows,
    norm_gain,
    norm_bias,
    qv_bias,
    proj_bias,
    fc1_bias,
    fc2_bias,
    layer_scale,
    cotangent,
):
    rows, width = tokens.shape
    packs, images, _ = patch_grid.shape
    pack = rows // packs
    slot = pack // images
    head = width // H
    hidden = fc1_bias.shape[0]
    row_width = qkv_rows.shape[1]
    tiles = hidden // width
    tile = min(256, rows)
    swaps = lax.axis_size("wide") == 16 and lax.axis_size("narrow") == 2
    if swaps:
        me = lax.axis_index(AXES)
        sc = jnp.stack([me // CORE % 2, me // X % 2, me % 2, me // Z]).astype(jnp.int32)
    else:
        sc = jnp.zeros((4,), jnp.int32)
    grid_flat = patch_grid.reshape(-1)
    thin, wide_rows = width // (2 * COLUMNS), hidden // (2 * COLUMNS)
    per_tile = COLUMNS // tiles

    by_pack = pl.BlockSpec((pack, width), lambda i, *_: (i, 0))
    by_tile = lambda w: pl.BlockSpec((tile, w), lambda i, *_: (i, 0))
    whole = full((rows, width))
    proj_blocks = pl.BlockSpec((COLUMNS, thin, width), lambda i, *_: (0, 0, 3), pipeline_mode=pl.Buffered(1))
    fc2_blocks = pl.BlockSpec((per_tile, wide_rows, width), lambda i, *_: (i, 0, 0))
    column_blocks = pl.BlockSpec((COLUMNS, thin, width), lambda i, *_: (0, 0, i))
    hidden_tile = pl.BlockSpec((rows, width), lambda i, *_: (0, i))
    vec1, vec2 = full((1, width)), full((2, width))
    hidden_vec = pl.BlockSpec((1, width), lambda i, *_: (0, i))
    qkv_blocks = full((COLUMNS, thin, 3 * width))
    qkv_scr = pltpu.VMEM((COLUMNS, 2, thin, 3 * width), BF16)
    fc2_scr = pltpu.VMEM((per_tile, 2, wide_rows, width), BF16)
    thin_scr = pltpu.VMEM((COLUMNS, 2, thin, width), BF16)
    sum_scr = pltpu.VMEM((rows, width), F32)
    turned_scr = pltpu.VMEM((width, rows), BF16)
    log_block = pl.BlockSpec((tile // slot * H, slot), lambda i, *_: (i, 0))

    halves = lambda v: v.reshape(COLUMNS, 2, -1, v.shape[1]).transpose(1, 0, 2, 3)
    ready = []
    if swaps:
        qp_block, fc1_block, a, b = pack_rows(qkv_rows, proj_rows, fc1_rows, fc2_rows, width, tiles)
        qp_line, fc1_line = gather_line(qp_block), gather_line(fc1_block)
        *qp_ab, message, _ = gather_stack(qp_line, sc, [], (a, swap(a, X), b, swap(b, Y)))
        fc2_line = gather_line(message)
        *qp_pair, token = gather_pair(*qp_ab, sc, [fc1_line[1], fc1_line[3]])
        ready = [token]
    else:
        qp_block = jnp.concatenate([qkv_rows.reshape(-1, 3 * width), proj_rows.reshape(-1, width)], axis=1)
        fc1_block, fc2_block = fc1_rows.reshape(-1, hidden), fc2_rows.reshape(-1, width)
        qp_own, qp_other = halves(lax.all_gather(qp_block, AXES, axis=0, tiled=True))
        fc1_own, fc1_other = halves(lax.all_gather(fc1_block, AXES, axis=0, tiled=True))
        fc2_own, fc2_other = halves(lax.all_gather(fc2_block, AXES, axis=0, tiled=True))

    x, n1, up, b2g, fc2_sums, token = call(
        partial(prepare_kernel, images=images),
        (packs,),
        (grid_flat,),
        [(far(tokens), by_pack), (far(cotangent), by_pack), (norm_gain, vec2), (norm_bias, vec2), (layer_scale, vec2)],
        [((rows, width), BF16, by_pack, "far")] * 4 + [((1, width), F32, vec1)],
        (),
        ready,
        mib=14,
    )

    ready = []
    if swaps:
        *fc1_ab, token = gather_stack(fc1_line, sc, [token, fc2_line[1]])
        qp_own, qp_other, token = gather_place(*qp_pair, sc, [token])
        ready = [token]

    offset = jnp.concatenate([qv_bias[0], jnp.zeros_like(qv_bias[0]), qv_bias[1]])[None]
    proj, att, log_total, token = call(
        partial(attend_kernel, slot=slot, head=head),
        (rows // tile,),
        (grid_flat, sc),
        [(far(n1), by_tile(width)), (qp_own, qkv_blocks), (qp_other, qkv_blocks), (offset, full((1, 3 * width)))],
        [((rows, 3 * width), BF16, by_tile(3 * width), "far"), ((rows, width), BF16, by_tile(width))]
        + [((rows // slot * H, slot), F32, log_block)],
        [qkv_scr],
        ready,
        mib=24,
    )
    ready = []
    if swaps:
        *fc1_pair, token = gather_pair(*fc1_ab, sc, [token, fc2_line[2]])
        ready = [token]
    b1, n2, token = call(
        middle_kernel,
        (1,),
        (sc,),
        [(att, whole), (x, whole), (norm_gain, vec2), (norm_bias, vec2), (layer_scale, vec2), (proj_bias[None], vec1)]
        + [(qp_own, proj_blocks), (qp_other, proj_blocks)],
        [((rows, width), F32, whole, "far"), ((rows, width), BF16, whole)],
        [sum_scr, thin_scr],
        ready,
        mib=20,
    )
    ready = []
    if swaps:
        *fc2_pair, token = gather_columns(fc2_line, sc, [token])
        fc1_own, fc1_other, token = gather_place(*fc1_pair, sc, [token])
        ready = [token]
    cut = tiles - 1

    def some_tiles(first, count, after, alias=None):
        columns = pl.BlockSpec((COLUMNS, thin, width), lambda i, *_: (0, 0, i + first))
        outs = pl.BlockSpec((rows, width), lambda i, *_: (0, i + first))
        blocks = pl.BlockSpec((per_tile, wide_rows, width), lambda i, *_: (i + first, 0, 0))
        return call(
            hidden_kernel,
            (count,),
            (sc,),
            [(n2, whole), (b2g, whole), (fc1_bias[None], pl.BlockSpec((1, width), lambda i, *_: (0, i + first)))]
            + [(fc1_own, columns), (fc1_other, columns)],
            [((rows, hidden), BF16, outs, "far"), ((rows, hidden), F32, outs, "far")]
            + [((COLUMNS, wide_rows, width), BF16, blocks, "far")] * 2,
            [thin_scr],
            after,
            mib=24,
            alias=alias,
        )

    *made, token = some_tiles(0, cut, ready)
    if swaps:
        fc2_own, fc2_other, token = gather_place(*fc2_pair, sc, [token], tiles)
    *made, token = some_tiles(cut, tiles - cut, made + [token], {i: i for i in range(4)})
    act, slope, fc2g_own, fc2g_other = made

    hg, fc1_sums, fc1g_own, fc1g_other, token = call(
        hidden_back_kernel,
        (tiles,),
        (sc,),
        [(far(b2g), whole), (far(n2), whole), (far(slope), hidden_tile), (fc2_own, fc2_blocks), (fc2_other, fc2_blocks)],
        [((rows, hidden), BF16, hidden_tile, "far"), ((1, hidden), F32, hidden_vec)]
        + [((COLUMNS, thin, hidden), BF16, column_blocks, "far")] * 2,
        [turned_scr, fc2_scr],
        mib=28,
    )
    chain = []
    if swaps:
        fc2_parts, token = fold_core(fc2g_own, fc2g_other, sc, [token])
        chain = [token]

    bound = lambda i: jnp.minimum(i, tiles - 1)
    hidden_first = pl.BlockSpec((rows, width), lambda i, *_: (0, bound(i)))
    column_first = pl.BlockSpec((COLUMNS, thin, width), lambda i, *_: (0, 0, bound(i)))
    fc2_first = pl.BlockSpec((per_tile, wide_rows, width), lambda i, *_: (bound(i), 0, 0))
    then = lambda size: pl.BlockSpec((size, width), lambda i, *_: (jnp.maximum(i - tiles, 0), 0))
    mg, b1g, ag, middle_sums, token = call(
        partial(middle_back_kernel, tiles=tiles),
        (tiles + rows // tile,),
        (sc,),
        [(far(hg), hidden_first), (fc1_own, column_first), (fc1_other, column_first)]
        + [(qp_own, proj_blocks), (qp_other, proj_blocks)]
        + [(b1, then(tile)), (x, then(tile)), (up, then(tile)), (norm_gain, vec2), (layer_scale, vec2)],
        [((rows, width), F32, then(tile), "far"), ((rows, width), BF16, then(tile)), ((rows, width), BF16, then(tile))]
        + [((4, width), F32, full((4, width)))],
        [sum_scr, thin_scr, thin_scr],
        chain,
        mib=28,
    )
    chain = []
    if swaps:
        fc1_parts, token = fold_core(fc1g_own, fc1g_other, sc, [token])
        chain = [token]

    pg, proj_sums, token = call(
        partial(attend_back_kernel, slot=slot, head=head),
        (rows // tile,),
        (grid_flat,),
        [(far(proj), by_tile(3 * width)), (ag, by_tile(width)), (log_total, log_block)],
        [((rows, 3 * width), BF16, by_tile(3 * width)), ((8, 3 * width), F32, full((8, 3 * width)))],
        (),
        chain,
        mib=14,
    )
    chain = []
    if swaps:
        fc_parts, token = fold_first(fc1_parts + fc2_parts, sc, [token])
        chain = [token]

    qp_grad_own, qp_grad_other, token = call(
        weight_kernel,
        (4,),
        (sc,),
        [(n1, whole), (att, whole), (pg, pl.BlockSpec((rows, width), lambda i, *_: (0, jnp.minimum(i, 2)))), (b1g, whole)],
        [((COLUMNS, thin, 4 * width), BF16, column_blocks)] * 2,
        [turned_scr],
        chain,
        mib=18,
    )
    layer_out, out_sums, token = call(
        partial(layer_out_kernel, images=images, tiles=tiles),
        (tiles + packs,),
        (grid_flat, sc),
        [(far(act), hidden_first), (fc2_own, fc2_first), (fc2_other, fc2_first), (x, then(pack)), (b1, then(pack)), (up, then(pack))]
        + [(layer_scale, vec2), (fc2_bias[None], vec1)],
        [((rows, width), BF16, then(pack), "far"), ((1, width), F32, vec1)],
        [sum_scr, pltpu.VMEM((pack, width), BF16), fc2_scr],
        [token],
        mib=26,
    )
    chain = []
    if swaps:
        qp_parts, token = fold_core(qp_grad_own, qp_grad_other, sc, [token])
        token, fc_parts = fold_sends(fold_second(fc_parts, sc, [token]))
        chain = [token]

    input_grad, input_sums, token = call(
        partial(input_back_kernel, images=images),
        (packs,),
        (grid_flat, sc),
        [(pg, pl.BlockSpec((pack, 3 * width), lambda i, *_: (i, 0))), (qp_own, qkv_blocks), (qp_other, qkv_blocks)]
        + [(x, by_pack), (mg, by_pack), (norm_gain, vec2)],
        [((rows, width), F32, by_pack, "far"), ((2, width), F32, vec2)],
        [qkv_scr, pltpu.VMEM((pack, width), F32)] + [pltpu.VMEM((pack, width), BF16)] * 2,
        chain,
        mib=26,
    )

    chain = []
    if swaps:
        qp_parts, token = fold_first(qp_parts, sc, [token, fc_parts[1], fc_parts[3]])
        chain = [token]

    def gather_sums(input_sums, middle, proj, fc2, out, fc1, to):
        q, v = column_sum(proj[:, pl.ds(0, width)]), column_sum(proj[:, pl.ds(2 * width, width)])
        lines = (input_sums[0:1], middle[2:3], input_sums[1:2], middle[3:4], q, v, middle[1:2], fc2[...], middle[0:1], out[...])
        for i, line in enumerate(lines):
            to[pl.ds(i, 1)] = line
        for i in range(tiles):
            to[pl.ds(len(lines) + i, 1)] = fc1[:, pl.ds(i * width, width)]

    sums_in = (input_sums, middle_sums, proj_sums, fc2_sums, out_sums, fc1_sums)
    sums, token = call(
        gather_sums,
        (1,),
        (),
        [(v, full(v.shape)) for v in sums_in],
        [((10 + tiles, width), F32, full((10 + tiles, width)))],
        (),
        chain,
    )
    if swaps:
        fc2_rows_of = fc2_rows.shape[0] // tiles
        n1_runs, n2_runs = hidden // 256, width // 256
        fc_runs = []
        for half in range(2):
            fc_runs += [(0, half * n1_runs + i, hidden // 128) for i in range(n1_runs)]
            fc_runs += [(1, k * fc2_rows_of + half * n2_runs + i, width // 128) for k in range(tiles) for i in range(n2_runs)]
        sums, token = reduce_level(reduce_sends(sums, (CORE,)), (0,), sc, [token])
        sums, token = reduce_level(reduce_sends(sums, (Y,)), (2,), sc, [token])
        token, qp_parts = fold_sends(fold_second(qp_parts, sc, [token, fc_parts[2]]))
        sums, token = reduce_level(reduce_sends(sums, (X,)), (1,), sc, [token])
        fc1_grad, fc2_grad, token = fold_last(fc_parts, (fc1_rows.shape, fc2_rows.shape), fc_runs, [token, qp_parts[1]])
        line = lambda i: pl.ds(i * width, width)
        shapes = [(2, width)] * 3 + [(width,), (hidden,), (width,), (2, width)]
        where = [(i // 2, pl.ds(i % 2, 1)) for i in range(6)] + [(3, line(0)), (5, line(0))]
        where += [(6, pl.ds(0, 1)), (6, pl.ds(1, 1))] + [(4, line(i)) for i in range(tiles)]
        sums = reduce_sends(sums, (Z, 2 * Z, 3 * Z))
        *small, token = reduce_level(sums, (3,), sc, [token] + qp_parts[2:], (shapes, where))
        qkv_runs, proj_runs = 3 * width // 128, width // 128
        qp_runs = [(0, i, qkv_runs) for i in range(qkv_runs)] + [(1, i, proj_runs) for i in range(proj_runs)]
        qkv_grad, proj_grad, _ = fold_last(qp_parts, (qkv_rows.shape, proj_rows.shape), qp_runs, [token])
    else:

        def scatter(own, other):
            matrix = jnp.stack([own, other], axis=1).reshape(-1, own.shape[-1])
            return lax.psum_scatter(matrix, AXES, scatter_dimension=0, tiled=True).astype(F32)

        fc2_grad = scatter(fc2g_own, fc2g_other).reshape(-1, row_width)
        fc1_grad = scatter(fc1g_own, fc1g_other).reshape(-1, row_width)
        qp_grad = scatter(qp_grad_own, qp_grad_other)
        qkv_grad = qp_grad[:, : 3 * width].reshape(-1, row_width)
        proj_grad = qp_grad[:, 3 * width :].reshape(-1, row_width)
        sums = lax.psum(sums, AXES)
        small = [sums[0:2], sums[2:4], sums[4:6], sums[6], sums[10:].reshape(-1), sums[7], sums[8:10]]
    return (
        layer_out,
        input_grad,
        qkv_grad,
        proj_grad,
        fc1_grad,
        fc2_grad,
        *(v.reshape(leaf.shape) for v, leaf in zip(small, (norm_gain, norm_bias, qv_bias, proj_bias, fc1_bias, fc2_bias, layer_scale))),
    )


def solution(mesh):
    split = P(AXES, None)
    return jax.shard_map(
        body,
        mesh=mesh,
        in_specs=(split, P(AXES, None, None)) + (split,) * 4 + (P(),) * 7 + (split,),
        out_specs=(split,) * 6 + (P(),) * 7,
        check_vma=False,
    )
```

```python
from functools import partial

import jax
import jax.numpy as jnp
from jax import lax
from jax.experimental import pallas as pl
from jax.experimental.pallas import tpu as pltpu
from jax.sharding import PartitionSpec as P

H = 12
PREFIX = 5
EPSILON = 1e-06
NEGATIVE = -1e30
AXES = ("wide", "narrow")
COLUMNS = 8
BF16 = jnp.bfloat16
F32 = jnp.float32


def dot(a, b):
    return lax.dot_general(a, b, (((1,), (0,)), ((), ())), preferred_element_type=F32)


def dot_nt(a, b):
    return lax.dot_general(a, b, (((1,), (1,)), ((), ())), preferred_element_type=F32)


def dot_tn(a, b):
    return lax.dot_general(a, b, (((0,), (0,)), ((), ())), preferred_element_type=F32)


TOKEN = (8, 128)


def call(kernel, grid, scalars, ins, outs, scratch=(), after=(), mib=36, alias=None):
    n, m = len(scalars) + len(ins), len(outs)

    def run(*refs):
        rest = refs[n + len(after) :]
        rest[m][...] = jnp.zeros(TOKEN, F32)
        kernel(*refs[:n], *rest[:m], *rest[m + 1 :])

    anywhere = pl.BlockSpec(memory_space=pl.ANY)
    return pl.pallas_call(
        run,
        grid_spec=pltpu.PrefetchScalarGridSpec(
            num_scalar_prefetch=len(scalars),
            grid=grid,
            in_specs=[spec for _, spec in ins] + [anywhere] * len(after),
            out_specs=[out[2] for out in outs] + [full(TOKEN)],
            scratch_shapes=list(scratch),
        ),
        out_shape=[
            pltpu.HBM(out[0], out[1]) if len(out) > 3 else jax.ShapeDtypeStruct(out[0], out[1]) for out in outs
        ]
        + [jax.ShapeDtypeStruct(TOKEN, F32)],
        input_output_aliases={n + k: to for k, to in (alias or {}).items()},
        compiler_params=pltpu.CompilerParams(vmem_limit_bytes=mib * 2**20),
        cost_estimate=pl.CostEstimate(flops=1, bytes_accessed=1, transcendentals=0),
    )(*scalars, *(array for array, _ in ins), *after)


def far(v):
    return pltpu.with_memory_space_constraint(v, pltpu.HBM)


def full(shape):
    return pl.BlockSpec(shape, lambda *_: (0,) * len(shape), pipeline_mode=pl.Buffered(1))


def standardize(v):
    centered = v - jnp.mean(v, axis=-1, keepdims=True)
    inverse = lax.rsqrt(jnp.mean(centered * centered, axis=-1, keepdims=True) + EPSILON)
    return centered * inverse, inverse


def standardize_back(grad, scaled, inverse):
    return inverse * (
        grad
        - jnp.mean(grad, axis=-1, keepdims=True)
        - scaled * jnp.mean(grad * scaled, axis=-1, keepdims=True)
    )


def length_of(grid_ref, image):
    return PREFIX + grid_ref[2 * image] * grid_ref[2 * image + 1]


def spans(grid_ref, pack, images):
    found, start = [], 0
    for i in range(images):
        length = length_of(grid_ref, pack * images + i)
        found.append((start, length))
        start = start + length
    return found


def join(scr, core, own, other):
    for i in range(scr.shape[0]):
        scr[i, core] = own[i]
        scr[i, 1 - core] = other[i]
    blocks, cores, rows, columns = scr.shape
    return scr[...].reshape(blocks * cores * rows, columns)


def part(core, matrix, own, other):
    blocks, rows, columns = own.shape
    cut = matrix.reshape(blocks, 2, rows, columns)
    own[...] = jnp.where(core == 0, cut[:, 0], cut[:, 1])
    other[...] = jnp.where(core == 0, cut[:, 1], cut[:, 0])


def prepare_kernel(grid_ref, tok, cot, gain, bias, ls, x, n1, up, b2g, sums, *, images):
    pack = pl.program_id(0)
    slot = tok.shape[0] // images
    row = lax.broadcasted_iota(jnp.int32, (slot, tok.shape[0]), 0)
    column = lax.broadcasted_iota(jnp.int32, (slot, tok.shape[0]), 1)

    def image(i, carry):
        start, total = carry
        length = length_of(grid_ref, pack * images + i)
        place = jnp.where((column - row == start) & (row < length), 1.0, 0.0).astype(BF16)
        rows = pl.ds(pl.multiple_of(i * slot, slot), slot)
        moved = dot(place, tok[...])
        x[rows] = moved.astype(BF16)
        scaled, _ = standardize(moved)
        n1[rows] = (scaled * gain[0:1] + bias[0:1]).astype(BF16)
        upstream = dot(place, cot[...])
        up[rows] = upstream.astype(BF16)
        low = (ls[1:2] * upstream).astype(BF16)
        b2g[rows] = low
        return start + length, total + column_sum(low.astype(F32))

    _, total = lax.fori_loop(0, images, image, (jnp.int32(0), jnp.zeros((1, tok.shape[1]), F32)))

    @pl.when(pack == 0)
    def _():
        sums[...] = jnp.zeros_like(sums)

    sums[...] += total


def unplace(grid_ref, pack, images, size):
    slot = size // images
    row = lax.broadcasted_iota(jnp.int32, (size, slot), 0)
    column = lax.broadcasted_iota(jnp.int32, (size, slot), 1)
    return jnp.concatenate(
        [
            jnp.where((row - column == start) & (column < length), 1.0, 0.0).astype(BF16)
            for start, length in spans(grid_ref, pack, images)
        ],
        axis=1,
    )


def pieces(rows, size=128):
    return [pl.ds(r, size) for r in range(0, rows, size)]


def eights(v):
    return jnp.sum(v.reshape(-1, 8, v.shape[1]), axis=0)


def column_sum(v):
    return jnp.sum(v, axis=0, keepdims=True)


def stacked(v, low):
    zero = jnp.zeros_like(v)
    return jnp.concatenate([jnp.where(low, v, zero), jnp.where(low, zero, v)], axis=0)


def attend_kernel(grid_ref, sc, n1, own, other, offset, proj, att, log_total, scr, *, slot, head):
    step = pl.program_id(0)
    width = n1.shape[1]
    per = n1.shape[0] // slot
    pair = 2 * head
    heads = width // head

    @pl.when(step == 0)
    def _():
        join(scr, sc[0], own, other)

    w = scr[...].reshape(width, 3 * width)
    proj[...] = (dot(n1[...], w) + offset[...]).astype(BF16)
    low = lax.broadcasted_iota(jnp.int32, (slot, pair), 1) < head
    key_at = lax.broadcasted_iota(jnp.int32, (slot, slot), 0)
    for i in range(per):
        ok = key_at < length_of(grid_ref, step * per + i)
        rows = pl.ds(i * slot, slot)
        found = []
        for j in range(width // pair):
            q, k = (proj[rows, pl.ds(t * width + j * pair, pair)] for t in range(2))
            scores = dot_nt(stacked(k, low), q * jnp.asarray(head ** (-0.5), BF16))
            halves = []
            for h in range(2):
                masked = jnp.where(ok, scores[h * slot : (h + 1) * slot], NEGATIVE)
                top = jnp.max(masked, axis=0, keepdims=True)
                exponent = jnp.exp(masked - top)
                total = column_sum(exponent)
                halves.append((exponent * (1.0 / total)).astype(BF16))
                log_total[pl.ds(i * heads + 2 * j + h, 1)] = top + jnp.log(total)
            found.append(jnp.concatenate(halves, axis=0))
        for j, p in enumerate(found):
            v = proj[rows, pl.ds(2 * width + j * pair, pair)]
            att[rows, pl.ds(j * pair, pair)] = dot_tn(p, stacked(v, low)).astype(BF16)


def middle_kernel(sc, att, x, gain, bias, ls, proj_bias, own, other, b1, n2, acc, scr):
    acc[...] = dot(att[...], join(scr, sc[0], own, other))
    for rows in pieces(acc.shape[0]):
        branch = acc[rows] + proj_bias[...]
        b1[rows] = branch
        scaled, _ = standardize(x[rows].astype(F32) + ls[0:1] * branch)
        n2[rows] = (scaled * gain[1:2] + bias[1:2]).astype(BF16)


def hidden_kernel(sc, n2, b2g, fc1_bias, own, other, act, slope, go, gs, scr):
    w1 = join(scr, sc[0], own, other)
    for rows in pieces(n2.shape[0]):
        hidden = dot(n2[rows], w1) + fc1_bias[...]
        normal = 0.5 * (1.0 + lax.erf(hidden * 0.5**0.5))
        act[rows] = (hidden * normal).astype(BF16)
        density = (0.5 / jnp.pi) ** 0.5 * jnp.exp(-0.5 * hidden * hidden)
        slope[rows] = normal + hidden * density
    part(sc[0], dot_tn(act[...], b2g[...]).astype(BF16), go, gs)


def hidden_back_kernel(sc, b2g, n2, slope, own, other, hg, sums, go, gs, scr):
    w2 = join(scr, sc[0], own, other)
    total = jnp.zeros((8, sums.shape[1]), F32)
    for rows in pieces(b2g.shape[0], 256):
        low = (dot_nt(b2g[rows], w2) * slope[rows]).astype(BF16)
        hg[rows] = low
        total = total + eights(low.astype(F32))
    sums[...] = column_sum(total)
    part(sc[0], dot_tn(n2[...], hg[...]).astype(BF16), go, gs)


def middle_back_kernel(sc, hg, own, other, po, ps, b1, x, up, gain, ls, mg, b1g, ag, sums, acc, scr, pscr, *, tiles):
    step = pl.program_id(0)

    @pl.when(step == 0)
    def _():
        acc[...] = jnp.zeros_like(acc)

    @pl.when(step < tiles)
    def _():
        acc[...] += dot_nt(hg[...], join(scr, sc[0], own, other))

    @pl.when(step == tiles)
    def _():
        join(pscr, sc[0], po, ps)
        sums[...] = jnp.zeros_like(sums)

    @pl.when(step >= tiles)
    def _():
        size = x.shape[0]
        totals = [jnp.zeros((8, x.shape[1]), F32) for _ in range(4)]
        for rows in pieces(size):
            branch = b1[rows]
            scaled, inverse = standardize(x[rows].astype(F32) + ls[0:1] * branch)
            grad = acc[pl.ds(pl.multiple_of((step - tiles) * size + rows.start, 128), rows.size)]
            back = up[rows].astype(F32) + standardize_back(grad * gain[1:2], scaled, inverse)
            mg[rows] = back
            low = (ls[0:1] * back).astype(BF16)
            b1g[rows] = low
            terms = (back * branch, low.astype(F32), grad * scaled, grad)
            totals = [t + eights(v) for t, v in zip(totals, terms)]
        ag[...] = dot_nt(b1g[...], pscr[...].reshape(x.shape[1], x.shape[1])).astype(BF16)
        sums[...] += jnp.concatenate([column_sum(t) for t in totals], axis=0)


def attend_back_kernel(grid_ref, proj, ag, log_total, pg, sums, *, slot, head):
    step = pl.program_id(0)
    width = ag.shape[1]
    per = ag.shape[0] // slot
    pair = 2 * head
    heads = width // head
    factor = head ** (-0.5)
    low = lax.broadcasted_iota(jnp.int32, (slot, pair), 1) < head
    key_at = lax.broadcasted_iota(jnp.int32, (slot, slot), 0)

    @pl.when(step == 0)
    def _():
        sums[...] = jnp.zeros_like(sums)

    for i in range(per):
        ok = key_at < length_of(grid_ref, step * per + i)
        rows = pl.ds(i * slot, slot)
        found = []

        def put(t, j, d):
            d = d.astype(BF16)
            columns = pl.ds(t * width + j * pair, pair)
            pg[rows, columns] = d
            if t != 1:
                sums[:, columns] += eights(d.astype(F32))

        for j in range(width // pair):
            q, k, v = (proj[rows, pl.ds(t * width + j * pair, pair)] for t in range(3))
            out = ag[rows, pl.ds(j * pair, pair)]
            q = q * jnp.asarray(factor, BF16)
            k2 = stacked(k, low)
            scores = dot_nt(k2, q)
            pull = dot_nt(stacked(v, low), out)
            ps, ss = [], []
            for h in range(2):
                half = slice(h * slot, (h + 1) * slot)
                p = jnp.exp(jnp.where(ok, scores[half], NEGATIVE) - log_total[pl.ds(i * heads + 2 * j + h, 1)])
                g = pull[half]
                ps.append(p.astype(BF16))
                ss.append((p * (g - column_sum(g * p))).astype(BF16))
            s = jnp.concatenate(ss, axis=0)
            dk = dot(s, q)
            dv = dot(jnp.concatenate(ps, axis=0), out)
            put(1, j, jnp.where(low, dk[:slot], dk[slot:]))
            put(2, j, jnp.where(low, dv[:slot], dv[slot:]))
            found.append((s, k2))
        for j, (s, k2) in enumerate(found):
            put(0, j, dot_tn(s, k2) * factor)


def weight_kernel(sc, n1, att, pg, b1g, go, gs, n1t):
    step = pl.program_id(0)
    last = pl.num_programs(0) - 1

    @pl.when(step == 0)
    def _():
        n1t[...] = n1[...].T

    @pl.when(step < last)
    def _():
        part(sc[0], dot(n1t[...], pg[...]).astype(BF16), go, gs)

    @pl.when(step == last)
    def _():
        part(sc[0], dot_tn(att[...], b1g[...]).astype(BF16), go, gs)


def input_back_kernel(grid_ref, sc, pg, own, other, x, mg, gain, out, sums, scr, acc, high, mid, *, images):
    step = pl.program_id(0)
    size, width = x.shape
    per = out.shape[0] // size

    @pl.when(step == 0)
    def _():
        join(scr, sc[0], own, other)
        sums[...] = jnp.zeros_like(sums)

    acc[...] = dot_nt(pg[...], scr[...].reshape(width, 3 * width))
    totals = [jnp.zeros((8, width), F32) for _ in range(2)]
    for rows in pieces(size):
        grad = acc[rows]
        scaled, inverse = standardize(x[rows].astype(F32))
        back = mg[rows] + standardize_back(grad * gain[0:1], scaled, inverse)
        totals = [t + eights(v) for t, v in zip(totals, (grad * scaled, grad))]
        big = back.astype(BF16)
        at = pl.ds(pl.multiple_of(step % per * size + rows.start, 128), rows.size)
        high[at] = big
        mid[at] = (back - big.astype(F32)).astype(BF16)
    sums[...] += jnp.concatenate([column_sum(t) for t in totals], axis=0)

    @pl.when(step % per == per - 1)
    def _():
        place = unplace(grid_ref, step // per, images, out.shape[0])
        out[...] = dot(place, high[...]) + dot(place, mid[...])


def layer_out_kernel(grid_ref, sc, act, own, other, x, b1, up, ls, fc2_bias, out, sums, acc, result, scr, *, images, tiles):
    step = pl.program_id(0)

    @pl.when(step == 0)
    def _():
        acc[...] = jnp.zeros_like(acc)

    @pl.when(step < tiles)
    def _():
        acc[...] += dot(act[...], join(scr, sc[0], own, other))

    @pl.when(step == tiles)
    def _():
        sums[...] = jnp.zeros_like(sums)

    @pl.when(step >= tiles)
    def _():
        pack, size = step - tiles, out.shape[0]
        total = jnp.zeros((8, x.shape[1]), F32)
        for rows in pieces(size):
            branch = acc[pl.ds(pl.multiple_of(pack * size + rows.start, 128), rows.size)] + fc2_bias[...]
            total = total + eights(up[rows].astype(F32) * branch)
            middle = x[rows].astype(F32) + ls[0:1] * b1[rows]
            result[rows] = (middle + ls[1:2] * branch).astype(BF16)
        out[...] = dot(unplace(grid_ref, pack, images, size), result[...]).astype(BF16)
        sums[...] += column_sum(total)


Y, CORE, X, Z = 1, 2, 4, 8


def swap(v, mask):
    return lax.ppermute(v, AXES, [(i, i ^ mask) for i in range(32)])


def move(plan, sc, ins, outs, after, mib=8):
    def kernel(*refs):
        for a, b in plan(*refs):
            b[...] = a[...]

    return call(
        kernel, (1,), (sc,), [(v, full(v.shape)) for v in ins], [(shape, BF16, full(shape)) for shape in outs], (), after, mib
    )


def gather_line(block):
    return [block] + [swap(block, Z * k) for k in (1, 2, 3)]


def gather_stack(line, sc, after, sides=()):
    rows, columns = line[0].shape
    half = columns // 2
    shapes = [(4, rows, half)] * 2 + [(2, 2) + side.shape for side in sides[:1]]

    def plan(sc, *refs):
        ins, outs = refs[: 4 + len(sides)], refs[4 + len(sides) :]
        pairs = [(ins[k].at[:, pl.ds(h * half, half)], outs[h].at[k]) for k in range(4) for h in range(2)]
        return pairs + [(side, outs[2].at[i // 2, i % 2]) for i, side in enumerate(ins[4:])]

    return move(plan, sc, [*line, *sides], shapes, after)


def gather_columns(line, sc, after):
    _, _, rows, half = line[0].shape

    def plan(sc, *refs):
        return [(refs[k].at[h, i], refs[4 + h].at[i, k]) for k in range(4) for h in range(2) for i in range(2)]

    return move(plan, sc, line, [(2, 4, rows, half)] * 2, after)


def pack_rows(qkv, proj, fc1, fc2, width, tiles):
    arrays = (qkv, proj, fc1, fc2)
    rows = proj.shape[0] * 128 // width
    columns = [v.shape[0] * 128 // rows for v in arrays]
    places = [(0, 0), (0, columns[0]), (1, 0), (2, 0)]
    half = columns[3] // 2

    def kernel(*refs):
        ins, outs, scrs = refs[:4], refs[4:8], refs[8:]
        for n, (ref, scr) in enumerate(zip(ins, scrs)):
            scr[...] = ref[...].astype(F32)
            if n < 3:
                blocks = [(i, columns[n] // 128) for i in range(columns[n] // 128)]
            else:
                lanes = width // 128
                blocks = [(k * rows * lanes + i, lanes) for k in range(tiles) for i in range(lanes)]
            for i, (start, stride) in enumerate(blocks):
                to, at = places[n]
                at += i * 128
                if n == 3:
                    to, at = to + at // half, at % half
                outs[to][:, pl.ds(at, 128)] = scr[pl.ds(start, rows, stride=stride)].astype(BF16)

    shapes = [(rows, columns[0] + columns[1]), (rows, columns[2]), (rows, half), (rows, half)]
    scratch = [pltpu.VMEM(v.shape, F32) for v in arrays]
    outs = [(shape, BF16, full(shape)) for shape in shapes]
    return call(kernel, (1,), (), [(far(v), full(v.shape)) for v in arrays], outs, scratch, (), mib=8)[:4]


def gather_pair(a, b, sc, after):
    def plan(sc, a, xa, b, yb, left, right):
        return [(a, left.at[0]), (xa, left.at[1]), (b, right.at[0]), (yb, right.at[1])]

    return move(plan, sc, (a, swap(a, X), b, swap(b, Y)), [(2,) + a.shape] * 2, after)


def gather_place(left, right, sc, after, runs=1):
    _, _, rows, half = left.shape
    width = 2 * half // runs

    def plan(sc, left, other_left, right, other_right, out):
        pairs = []
        for n, sides in enumerate(((left, other_left), (right, other_right))):
            for i in range(2):
                for j in range(2):
                    for k in range(4):
                        x, y = (i, j) if n == 0 else (j, i)
                        to = out.at[sc[3] ^ k, sc[1] ^ x, sc[2] ^ y]
                        if runs == 1:
                            pairs.append((sides[j].at[i, k], to.at[:, pl.ds(n * half, half)]))
                            continue
                        for r in range(runs // 2):
                            run = n * (runs // 2) + r
                            pairs.append((sides[j].at[i, k, :, pl.ds(r * width, width)], to.at[pl.ds(run * rows, rows)]))
        return pairs

    ins = [far(v) for v in (left, swap(left, Y), right, swap(right, X))]
    own, token = move(plan, sc, ins, [(4, 2, 2, runs * rows, width)], after, 12)
    shape = (COLUMNS, 2 * runs * rows, width)
    return own.reshape(shape), swap(own, CORE).reshape(shape), token


def add(a, b):
    return a.astype(F32) + b.astype(F32)


def fold_core(own, other, sc, after):
    _, rows2, columns = own.shape
    rows, half = rows2 // 2, columns // 2
    by_z = pl.BlockSpec((1, 2, 2, rows, columns), lambda i, *_: (i, 0, 0, 0, 0))
    to_z = pl.BlockSpec((1, 2, rows, half), lambda i, *_: (i, 0, 0, 0))
    left, right = pl.ds(0, half), pl.ds(half, half)

    def kernel(sc, own, got, ka, sa, kb, sb):
        for i in range(2):
            for a, b, flip in ((ka, kb, 0), (sa, sb, 1)):
                y, x = sc[2] ^ flip, sc[1] ^ flip
                a[0, i] = add(own[0, i, y, :, left], got[0, i, y, :, left]).astype(BF16)
                b[0, i] = add(own[0, x, i, :, right], got[0, x, i, :, right]).astype(BF16)

    ins = [(v.reshape(4, 2, 2, rows, columns), by_z) for v in (own, swap(other, CORE))]
    ka, sa, kb, sb, token = call(kernel, (4,), (sc,), ins, [((4, 2, rows, half), BF16, to_z)] * 4, (), after, mib=12)
    return [(ka, sa, Y), (kb, sb, X)], token


def columns_of(parts):
    rows = min(keep.shape[2] for keep, _, _ in parts)
    places, at = [], 0
    for n, (keep, _, _) in enumerate(parts):
        for first in range(0, keep.shape[2], rows):
            places.append((n, first, at, keep.shape[3]))
            at += keep.shape[3]
    return rows, at, places


def fold_first(parts, sc, after):
    groups = [[part for part in parts if part[2] == mask] for mask in (Y, X)]
    ins = [(v, full(v.shape)) for group in groups for keep, send, mask in group for v in (keep, swap(send, mask))]
    layouts = [columns_of(group) for group in groups]
    outs = [((4, rows, width), BF16, full((4, rows, width))) for rows, width, _ in layouts for _ in range(2)]

    def kernel(sc, *refs):
        ins, outs, base = refs[: len(ins_)], refs[len(ins_) :], 0
        for g, (rows, _, places) in enumerate(layouts):
            for n, first, at, width in places:
                keep, got = ins[base + 2 * n], ins[base + 2 * n + 1]
                cut = pl.ds(first, rows)
                for z in range(4):
                    for flip in range(2):
                        here = sc[1 + g] ^ flip
                        to = outs[2 * g + flip]
                        to[z, :, pl.ds(at, width)] = add(keep[z, here, cut], got[z, here, cut]).astype(BF16)
            base += 2 * len(groups[g])

    ins_ = ins
    out = call(kernel, (1,), (sc,), ins, outs, (), after, mib=16)
    return [(out[0], out[1], X), (out[2], out[3], Y)], out[4]


def fold_second(parts, sc, after):
    ins = [(v, full(v.shape)) for keep, send, mask in parts for v in (keep, swap(send, mask))]
    _, rows, width = parts[0][0].shape
    shape = (rows, 2 * width)

    def kernel(sc, *refs):
        ins, outs = refs[:4], refs[4:]
        for k, to in enumerate(outs):
            z = sc[3] ^ k
            for n in range(2):
                to[:, pl.ds(n * width, width)] = add(ins[2 * n][z], ins[2 * n + 1][z]).astype(to.dtype)

    outs = [(shape, F32, full(shape))] + [(shape, BF16, full(shape))] * 3
    return call(kernel, (1,), (sc,), ins, outs, (), after, mib=12)


def fold_sends(parts):
    keep, *sends, token = parts
    return token, [keep] + [swap(v, Z * k) for k, v in zip((1, 2, 3), sends)]


def fold_last(parts, shapes, runs, after):
    def kernel(keep, r1, r2, r3, *outs):
        rows = keep.shape[0]
        for i, (n, first, stride) in enumerate(runs):
            cut = (slice(None), pl.ds(i * 128, 128))
            total = keep[cut] + (r1[cut].astype(F32) + r2[cut].astype(F32) + r3[cut].astype(F32))
            outs[n][pl.ds(first, rows, stride=stride)] = total

    ins = [(v, full(v.shape)) for v in parts]
    return call(kernel, (1,), (), ins, [(shape, F32, full(shape)) for shape in shapes], (), after, mib=12)


def reduce_sends(v, masks):
    return [v] + [swap(v, mask) for mask in masks]


def reduce_level(ins, at, sc, after, split=None):
    v = ins[0]
    shapes, where = split or ([v.shape], [(0, pl.ds(i, 1)) for i in range(v.shape[0])])

    def kernel(sc, *refs):
        line, outs = refs[-1], refs[-1 - len(shapes) : -1]
        mine = sc[at[0]]
        for k in at[1:]:
            mine = 2 * mine + sc[k]
        for k, ref in enumerate(refs[: len(ins)]):
            line[mine ^ k] = ref[...]
        total = line[0]
        for k in range(1, len(ins)):
            total = total + line[k]
        for i, (n, place) in enumerate(where):
            row = total[i : i + 1]
            outs[n][place] = row[0] if len(shapes[n]) == 1 else row

    outs = [(shape, F32, full(shape)) for shape in shapes]
    scratch = [pltpu.VMEM((len(ins),) + v.shape, F32)]
    return call(kernel, (1,), (sc,), [(u, full(v.shape)) for u in ins], outs, scratch, after, mib=8)


def body(
    tokens,
    patch_grid,
    qkv_rows,
    proj_rows,
    fc1_rows,
    fc2_rows,
    norm_gain,
    norm_bias,
    qv_bias,
    proj_bias,
    fc1_bias,
    fc2_bias,
    layer_scale,
    cotangent,
):
    rows, width = tokens.shape
    packs, images, _ = patch_grid.shape
    pack = rows // packs
    slot = pack // images
    head = width // H
    hidden = fc1_bias.shape[0]
    row_width = qkv_rows.shape[1]
    tiles = hidden // width
    tile = min(256, rows)
    swaps = lax.axis_size("wide") == 16 and lax.axis_size("narrow") == 2
    if swaps:
        me = lax.axis_index(AXES)
        sc = jnp.stack([me // CORE % 2, me // X % 2, me % 2, me // Z]).astype(jnp.int32)
    else:
        sc = jnp.zeros((4,), jnp.int32)
    grid_flat = patch_grid.reshape(-1)
    thin, wide_rows = width // (2 * COLUMNS), hidden // (2 * COLUMNS)
    per_tile = COLUMNS // tiles

    by_pack = pl.BlockSpec((pack, width), lambda i, *_: (i, 0))
    by_tile = lambda w: pl.BlockSpec((tile, w), lambda i, *_: (i, 0))
    whole = full((rows, width))
    proj_blocks = pl.BlockSpec((COLUMNS, thin, width), lambda i, *_: (0, 0, 3), pipeline_mode=pl.Buffered(1))
    fc2_blocks = pl.BlockSpec((per_tile, wide_rows, width), lambda i, *_: (i, 0, 0))
    column_blocks = pl.BlockSpec((COLUMNS, thin, width), lambda i, *_: (0, 0, i))
    hidden_tile = pl.BlockSpec((rows, width), lambda i, *_: (0, i))
    vec1, vec2 = full((1, width)), full((2, width))
    hidden_vec = pl.BlockSpec((1, width), lambda i, *_: (0, i))
    qkv_blocks = full((COLUMNS, thin, 3 * width))
    qkv_scr = pltpu.VMEM((COLUMNS, 2, thin, 3 * width), BF16)
    fc2_scr = pltpu.VMEM((per_tile, 2, wide_rows, width), BF16)
    thin_scr = pltpu.VMEM((COLUMNS, 2, thin, width), BF16)
    sum_scr = pltpu.VMEM((rows, width), F32)
    turned_scr = pltpu.VMEM((width, rows), BF16)
    log_block = pl.BlockSpec((tile // slot * H, slot), lambda i, *_: (i, 0))

    halves = lambda v: v.reshape(COLUMNS, 2, -1, v.shape[1]).transpose(1, 0, 2, 3)
    ready = []
    if swaps:
        qp_block, fc1_block, a, b = pack_rows(qkv_rows, proj_rows, fc1_rows, fc2_rows, width, tiles)
        qp_line, fc1_line = gather_line(qp_block), gather_line(fc1_block)
        *qp_ab, message, _ = gather_stack(qp_line, sc, [], (a, swap(a, X), b, swap(b, Y)))
        fc2_line = gather_line(message)
        *qp_pair, token = gather_pair(*qp_ab, sc, [fc1_line[1], fc1_line[3]])
        ready = [token]
    else:
        qp_block = jnp.concatenate([qkv_rows.reshape(-1, 3 * width), proj_rows.reshape(-1, width)], axis=1)
        fc1_block, fc2_block = fc1_rows.reshape(-1, hidden), fc2_rows.reshape(-1, width)
        qp_own, qp_other = halves(lax.all_gather(qp_block, AXES, axis=0, tiled=True))
        fc1_own, fc1_other = halves(lax.all_gather(fc1_block, AXES, axis=0, tiled=True))
        fc2_own, fc2_other = halves(lax.all_gather(fc2_block, AXES, axis=0, tiled=True))

    x, n1, up, b2g, fc2_sums, token = call(
        partial(prepare_kernel, images=images),
        (packs,),
        (grid_flat,),
        [(far(tokens), by_pack), (far(cotangent), by_pack), (norm_gain, vec2), (norm_bias, vec2), (layer_scale, vec2)],
        [((rows, width), BF16, by_pack, "far")] * 4 + [((1, width), F32, vec1)],
        (),
        ready,
        mib=14,
    )

    ready = []
    if swaps:
        *fc1_ab, token = gather_stack(fc1_line, sc, [token, fc2_line[1]])
        qp_own, qp_other, token = gather_place(*qp_pair, sc, [token])
        ready = [token]

    offset = jnp.concatenate([qv_bias[0], jnp.zeros_like(qv_bias[0]), qv_bias[1]])[None]
    proj, att, log_total, token = call(
        partial(attend_kernel, slot=slot, head=head),
        (rows // tile,),
        (grid_flat, sc),
        [(far(n1), by_tile(width)), (qp_own, qkv_blocks), (qp_other, qkv_blocks), (offset, full((1, 3 * width)))],
        [((rows, 3 * width), BF16, by_tile(3 * width), "far"), ((rows, width), BF16, by_tile(width))]
        + [((rows // slot * H, slot), F32, log_block)],
        [qkv_scr],
        ready,
        mib=24,
    )
    ready = []
    if swaps:
        *fc1_pair, token = gather_pair(*fc1_ab, sc, [token, fc2_line[2]])
        ready = [token]
    b1, n2, token = call(
        middle_kernel,
        (1,),
        (sc,),
        [(att, whole), (x, whole), (norm_gain, vec2), (norm_bias, vec2), (layer_scale, vec2), (proj_bias[None], vec1)]
        + [(qp_own, proj_blocks), (qp_other, proj_blocks)],
        [((rows, width), F32, whole, "far"), ((rows, width), BF16, whole)],
        [sum_scr, thin_scr],
        ready,
        mib=20,
    )
    ready = []
    if swaps:
        *fc2_pair, token = gather_columns(fc2_line, sc, [token])
        fc1_own, fc1_other, token = gather_place(*fc1_pair, sc, [token])
        ready = [token]
    cut = tiles - 1

    def some_tiles(first, count, after, alias=None):
        columns = pl.BlockSpec((COLUMNS, thin, width), lambda i, *_: (0, 0, i + first))
        outs = pl.BlockSpec((rows, width), lambda i, *_: (0, i + first))
        blocks = pl.BlockSpec((per_tile, wide_rows, width), lambda i, *_: (i + first, 0, 0))
        return call(
            hidden_kernel,
            (count,),
            (sc,),
            [(n2, whole), (b2g, whole), (fc1_bias[None], pl.BlockSpec((1, width), lambda i, *_: (0, i + first)))]
            + [(fc1_own, columns), (fc1_other, columns)],
            [((rows, hidden), BF16, outs, "far"), ((rows, hidden), F32, outs, "far")]
            + [((COLUMNS, wide_rows, width), BF16, blocks, "far")] * 2,
            [thin_scr],
            after,
            mib=24,
            alias=alias,
        )

    *made, token = some_tiles(0, cut, ready)
    if swaps:
        fc2_own, fc2_other, token = gather_place(*fc2_pair, sc, [token], tiles)
    *made, token = some_tiles(cut, tiles - cut, made + [token], {i: i for i in range(4)})
    act, slope, fc2g_own, fc2g_other = made

    hg, fc1_sums, fc1g_own, fc1g_other, token = call(
        hidden_back_kernel,
        (tiles,),
        (sc,),
        [(far(b2g), whole), (far(n2), whole), (far(slope), hidden_tile), (fc2_own, fc2_blocks), (fc2_other, fc2_blocks)],
        [((rows, hidden), BF16, hidden_tile, "far"), ((1, hidden), F32, hidden_vec)]
        + [((COLUMNS, thin, hidden), BF16, column_blocks, "far")] * 2,
        [fc2_scr],
        mib=26,
    )
    chain = []
    if swaps:
        fc2_parts, token = fold_core(fc2g_own, fc2g_other, sc, [token])
        chain = [token]

    bound = lambda i: jnp.minimum(i, tiles - 1)
    hidden_first = pl.BlockSpec((rows, width), lambda i, *_: (0, bound(i)))
    column_first = pl.BlockSpec((COLUMNS, thin, width), lambda i, *_: (0, 0, bound(i)))
    fc2_first = pl.BlockSpec((per_tile, wide_rows, width), lambda i, *_: (bound(i), 0, 0))
    then = lambda size: pl.BlockSpec((size, width), lambda i, *_: (jnp.maximum(i - tiles, 0), 0))
    mg, b1g, ag, middle_sums, token = call(
        partial(middle_back_kernel, tiles=tiles),
        (tiles + rows // tile,),
        (sc,),
        [(far(hg), hidden_first), (fc1_own, column_first), (fc1_other, column_first)]
        + [(qp_own, proj_blocks), (qp_other, proj_blocks)]
        + [(b1, then(tile)), (x, then(tile)), (up, then(tile)), (norm_gain, vec2), (layer_scale, vec2)],
        [((rows, width), F32, then(tile), "far"), ((rows, width), BF16, then(tile)), ((rows, width), BF16, then(tile))]
        + [((4, width), F32, full((4, width)))],
        [sum_scr, thin_scr, thin_scr],
        chain,
        mib=28,
    )
    chain = []
    if swaps:
        fc1_parts, token = fold_core(fc1g_own, fc1g_other, sc, [token])
        chain = [token]

    pg, proj_sums, token = call(
        partial(attend_back_kernel, slot=slot, head=head),
        (rows // tile,),
        (grid_flat,),
        [(far(proj), by_tile(3 * width)), (ag, by_tile(width)), (log_total, log_block)],
        [((rows, 3 * width), BF16, by_tile(3 * width)), ((8, 3 * width), F32, full((8, 3 * width)))],
        (),
        chain,
        mib=14,
    )
    chain = []
    if swaps:
        fc_parts, token = fold_first(fc1_parts + fc2_parts, sc, [token])
        chain = [token]

    qp_grad_own, qp_grad_other, token = call(
        weight_kernel,
        (4,),
        (sc,),
        [(n1, whole), (att, whole), (pg, pl.BlockSpec((rows, width), lambda i, *_: (0, jnp.minimum(i, 2)))), (b1g, whole)],
        [((COLUMNS, thin, 4 * width), BF16, column_blocks)] * 2,
        [turned_scr],
        chain,
        mib=18,
    )
    layer_out, out_sums, token = call(
        partial(layer_out_kernel, images=images, tiles=tiles),
        (tiles + packs,),
        (grid_flat, sc),
        [(far(act), hidden_first), (fc2_own, fc2_first), (fc2_other, fc2_first), (x, then(pack)), (b1, then(pack)), (up, then(pack))]
        + [(layer_scale, vec2), (fc2_bias[None], vec1)],
        [((rows, width), BF16, then(pack), "far"), ((1, width), F32, vec1)],
        [sum_scr, pltpu.VMEM((pack, width), BF16), fc2_scr],
        [token],
        mib=26,
    )
    chain = []
    if swaps:
        qp_parts, token = fold_core(qp_grad_own, qp_grad_other, sc, [token])
        token, fc_parts = fold_sends(fold_second(fc_parts, sc, [token]))
        chain = [token]

    per = pack // tile
    input_grad, input_sums, token = call(
        partial(input_back_kernel, images=images),
        (rows // tile,),
        (grid_flat, sc),
        [(pg, by_tile(3 * width)), (qp_own, qkv_blocks), (qp_other, qkv_blocks)]
        + [(x, by_tile(width)), (mg, by_tile(width)), (norm_gain, vec2)],
        [((rows, width), F32, pl.BlockSpec((pack, width), lambda i, *_: (i // per, 0)), "far"), ((2, width), F32, vec2)],
        [qkv_scr, pltpu.VMEM((tile, width), F32)] + [pltpu.VMEM((pack, width), BF16)] * 2,
        chain,
        mib=24,
    )

    chain = []
    if swaps:
        qp_parts, token = fold_first(qp_parts, sc, [token, fc_parts[1]])
        chain = [token]

    def gather_sums(input_sums, middle, proj, fc2, out, fc1, to):
        q, v = column_sum(proj[:, pl.ds(0, width)]), column_sum(proj[:, pl.ds(2 * width, width)])
        lines = (input_sums[0:1], middle[2:3], input_sums[1:2], middle[3:4], q, v, middle[1:2], fc2[...], middle[0:1], out[...])
        for i, line in enumerate(lines):
            to[pl.ds(i, 1)] = line
        for i in range(tiles):
            to[pl.ds(len(lines) + i, 1)] = fc1[:, pl.ds(i * width, width)]

    sums_in = (input_sums, middle_sums, proj_sums, fc2_sums, out_sums, fc1_sums)
    sums, token = call(
        gather_sums,
        (1,),
        (),
        [(v, full(v.shape)) for v in sums_in],
        [((10 + tiles, width), F32, full((10 + tiles, width)))],
        (),
        chain,
    )
    if swaps:
        fc2_rows_of = fc2_rows.shape[0] // tiles
        n1_runs, n2_runs = hidden // 256, width // 256
        fc_runs = []
        for half in range(2):
            fc_runs += [(0, half * n1_runs + i, hidden // 128) for i in range(n1_runs)]
            fc_runs += [(1, k * fc2_rows_of + half * n2_runs + i, width // 128) for k in range(tiles) for i in range(n2_runs)]
        sums, token = reduce_level(reduce_sends(sums, (CORE,)), (0,), sc, [token])
        sums, token = reduce_level(reduce_sends(sums, (Y,)), (2,), sc, [token])
        token, qp_parts = fold_sends(fold_second(qp_parts, sc, [token, fc_parts[2], fc_parts[3]]))
        sums, token = reduce_level(reduce_sends(sums, (X,)), (1,), sc, [token])
        fc1_grad, fc2_grad, token = fold_last(fc_parts, (fc1_rows.shape, fc2_rows.shape), fc_runs, [token, qp_parts[1]])
        line = lambda i: pl.ds(i * width, width)
        shapes = [(2, width)] * 3 + [(width,), (hidden,), (width,), (2, width)]
        where = [(i // 2, pl.ds(i % 2, 1)) for i in range(6)] + [(3, line(0)), (5, line(0))]
        where += [(6, pl.ds(0, 1)), (6, pl.ds(1, 1))] + [(4, line(i)) for i in range(tiles)]
        sums = reduce_sends(sums, (Z, 2 * Z, 3 * Z))
        *small, token = reduce_level(sums, (3,), sc, [token] + qp_parts[2:], (shapes, where))
        qkv_runs, proj_runs = 3 * width // 128, width // 128
        qp_runs = [(0, i, qkv_runs) for i in range(qkv_runs)] + [(1, i, proj_runs) for i in range(proj_runs)]
        qkv_grad, proj_grad, _ = fold_last(qp_parts, (qkv_rows.shape, proj_rows.shape), qp_runs, [token])
    else:

        def scatter(own, other):
            matrix = jnp.stack([own, other], axis=1).reshape(-1, own.shape[-1])
            return lax.psum_scatter(matrix, AXES, scatter_dimension=0, tiled=True).astype(F32)

        fc2_grad = scatter(fc2g_own, fc2g_other).reshape(-1, row_width)
        fc1_grad = scatter(fc1g_own, fc1g_other).reshape(-1, row_width)
        qp_grad = scatter(qp_grad_own, qp_grad_other)
        qkv_grad = qp_grad[:, : 3 * width].reshape(-1, row_width)
        proj_grad = qp_grad[:, 3 * width :].reshape(-1, row_width)
        sums = lax.psum(sums, AXES)
        small = [sums[0:2], sums[2:4], sums[4:6], sums[6], sums[10:].reshape(-1), sums[7], sums[8:10]]
    return (
        layer_out,
        input_grad,
        qkv_grad,
        proj_grad,
        fc1_grad,
        fc2_grad,
        *(v.reshape(leaf.shape) for v, leaf in zip(small, (norm_gain, norm_bias, qv_bias, proj_bias, fc1_bias, fc2_bias, layer_scale))),
    )


def solution(mesh):
    split = P(AXES, None)
    return jax.shard_map(
        body,
        mesh=mesh,
        in_specs=(split, P(AXES, None, None)) + (split,) * 4 + (P(),) * 7 + (split,),
        out_specs=(split,) * 6 + (P(),) * 7,
        check_vma=False,
    )
```

```python
from functools import partial

import jax
import jax.numpy as jnp
from jax import lax
from jax.experimental import pallas as pl
from jax.experimental.pallas import tpu as pltpu
from jax.sharding import PartitionSpec as P

H = 12
PREFIX = 5
EPSILON = 1e-06
NEGATIVE = -1e30
AXES = ("wide", "narrow")
COLUMNS = 8
BF16 = jnp.bfloat16
F32 = jnp.float32


def dot(a, b):
    return lax.dot_general(a, b, (((1,), (0,)), ((), ())), preferred_element_type=F32)


def dot_nt(a, b):
    return lax.dot_general(a, b, (((1,), (1,)), ((), ())), preferred_element_type=F32)


def dot_tn(a, b):
    return lax.dot_general(a, b, (((0,), (0,)), ((), ())), preferred_element_type=F32)


TOKEN = (8, 128)


def call(kernel, grid, scalars, ins, outs, scratch=(), after=(), mib=36, alias=None):
    n, m = len(scalars) + len(ins), len(outs)

    def run(*refs):
        rest = refs[n + len(after) :]
        rest[m][...] = jnp.zeros(TOKEN, F32)
        kernel(*refs[:n], *rest[:m], *rest[m + 1 :])

    anywhere = pl.BlockSpec(memory_space=pl.ANY)
    return pl.pallas_call(
        run,
        grid_spec=pltpu.PrefetchScalarGridSpec(
            num_scalar_prefetch=len(scalars),
            grid=grid,
            in_specs=[spec for _, spec in ins] + [anywhere] * len(after),
            out_specs=[out[2] for out in outs] + [full(TOKEN)],
            scratch_shapes=list(scratch),
        ),
        out_shape=[
            pltpu.HBM(out[0], out[1]) if len(out) > 3 else jax.ShapeDtypeStruct(out[0], out[1]) for out in outs
        ]
        + [jax.ShapeDtypeStruct(TOKEN, F32)],
        input_output_aliases={n + k: to for k, to in (alias or {}).items()},
        compiler_params=pltpu.CompilerParams(vmem_limit_bytes=mib * 2**20),
        cost_estimate=pl.CostEstimate(flops=1, bytes_accessed=1, transcendentals=0),
    )(*scalars, *(array for array, _ in ins), *after)


def far(v):
    return pltpu.with_memory_space_constraint(v, pltpu.HBM)


def full(shape):
    return pl.BlockSpec(shape, lambda *_: (0,) * len(shape), pipeline_mode=pl.Buffered(1))


def standardize(v):
    centered = v - jnp.mean(v, axis=-1, keepdims=True)
    inverse = lax.rsqrt(jnp.mean(centered * centered, axis=-1, keepdims=True) + EPSILON)
    return centered * inverse, inverse


def standardize_back(grad, scaled, inverse):
    return inverse * (
        grad
        - jnp.mean(grad, axis=-1, keepdims=True)
        - scaled * jnp.mean(grad * scaled, axis=-1, keepdims=True)
    )


def length_of(grid_ref, image):
    return PREFIX + grid_ref[2 * image] * grid_ref[2 * image + 1]


def spans(grid_ref, pack, images):
    found, start = [], 0
    for i in range(images):
        length = length_of(grid_ref, pack * images + i)
        found.append((start, length))
        start = start + length
    return found


def join(scr, core, own, other):
    for i in range(scr.shape[0]):
        scr[i, core] = own[i]
        scr[i, 1 - core] = other[i]
    blocks, cores, rows, columns = scr.shape
    return scr[...].reshape(blocks * cores * rows, columns)


def part(core, matrix, own, other):
    blocks, rows, columns = own.shape
    cut = matrix.reshape(blocks, 2, rows, columns)
    own[...] = jnp.where(core == 0, cut[:, 0], cut[:, 1])
    other[...] = jnp.where(core == 0, cut[:, 1], cut[:, 0])


def prepare_kernel(grid_ref, tok, cot, gain, bias, ls, x, n1, up, b2g, sums, *, images):
    pack = pl.program_id(0)
    slot = tok.shape[0] // images
    row = lax.broadcasted_iota(jnp.int32, (slot, tok.shape[0]), 0)
    column = lax.broadcasted_iota(jnp.int32, (slot, tok.shape[0]), 1)

    def image(i, carry):
        start, total = carry
        length = length_of(grid_ref, pack * images + i)
        place = jnp.where((column - row == start) & (row < length), 1.0, 0.0).astype(BF16)
        rows = pl.ds(pl.multiple_of(i * slot, slot), slot)
        moved = dot(place, tok[...])
        x[rows] = moved.astype(BF16)
        scaled, _ = standardize(moved)
        n1[rows] = (scaled * gain[0:1] + bias[0:1]).astype(BF16)
        upstream = dot(place, cot[...])
        up[rows] = upstream.astype(BF16)
        low = (ls[1:2] * upstream).astype(BF16)
        b2g[rows] = low
        return start + length, total + column_sum(low.astype(F32))

    _, total = lax.fori_loop(0, images, image, (jnp.int32(0), jnp.zeros((1, tok.shape[1]), F32)))

    @pl.when(pack == 0)
    def _():
        sums[...] = jnp.zeros_like(sums)

    sums[...] += total


def unplace(grid_ref, pack, images, size):
    slot = size // images
    row = lax.broadcasted_iota(jnp.int32, (size, slot), 0)
    column = lax.broadcasted_iota(jnp.int32, (size, slot), 1)
    return jnp.concatenate(
        [
            jnp.where((row - column == start) & (column < length), 1.0, 0.0).astype(BF16)
            for start, length in spans(grid_ref, pack, images)
        ],
        axis=1,
    )


def pieces(rows, size=128):
    return [pl.ds(r, size) for r in range(0, rows, size)]


def eights(v):
    return jnp.sum(v.reshape(-1, 8, v.shape[1]), axis=0)


def column_sum(v):
    return jnp.sum(v, axis=0, keepdims=True)


def stacked(v, low):
    zero = jnp.zeros_like(v)
    return jnp.concatenate([jnp.where(low, v, zero), jnp.where(low, zero, v)], axis=0)


def attend_kernel(grid_ref, sc, n1, own, other, offset, proj, att, log_total, scr, *, slot, head):
    step = pl.program_id(0)
    width = n1.shape[1]
    per = n1.shape[0] // slot
    pair = 2 * head
    heads = width // head

    @pl.when(step == 0)
    def _():
        join(scr, sc[0], own, other)

    w = scr[...].reshape(width, 3 * width)
    proj[...] = (dot(n1[...], w) + offset[...]).astype(BF16)
    low = lax.broadcasted_iota(jnp.int32, (slot, pair), 1) < head
    key_at = lax.broadcasted_iota(jnp.int32, (slot, slot), 0)
    for i in range(per):
        ok = key_at < length_of(grid_ref, step * per + i)
        rows = pl.ds(i * slot, slot)
        found = []
        for j in range(width // pair):
            q, k = (proj[rows, pl.ds(t * width + j * pair, pair)] for t in range(2))
            scores = dot_nt(stacked(k, low), q * jnp.asarray(head ** (-0.5), BF16))
            halves = []
            for h in range(2):
                masked = jnp.where(ok, scores[h * slot : (h + 1) * slot], NEGATIVE)
                top = jnp.max(masked, axis=0, keepdims=True)
                exponent = jnp.exp(masked - top)
                total = column_sum(exponent)
                halves.append((exponent * (1.0 / total)).astype(BF16))
                log_total[pl.ds(i * heads + 2 * j + h, 1)] = top + jnp.log(total)
            found.append(jnp.concatenate(halves, axis=0))
        for j, p in enumerate(found):
            v = proj[rows, pl.ds(2 * width + j * pair, pair)]
            att[rows, pl.ds(j * pair, pair)] = dot_tn(p, stacked(v, low)).astype(BF16)


def middle_kernel(sc, att, x, gain, bias, ls, proj_bias, own, other, b1, n2, acc, scr):
    acc[...] = dot(att[...], join(scr, sc[0], own, other))
    for rows in pieces(acc.shape[0]):
        branch = acc[rows] + proj_bias[...]
        b1[rows] = branch
        scaled, _ = standardize(x[rows].astype(F32) + ls[0:1] * branch)
        n2[rows] = (scaled * gain[1:2] + bias[1:2]).astype(BF16)


def hidden_kernel(sc, n2, b2g, fc1_bias, own, other, act, slope, go, gs, scr):
    w1 = join(scr, sc[0], own, other)
    for rows in pieces(n2.shape[0]):
        hidden = dot(n2[rows], w1) + fc1_bias[...]
        normal = 0.5 * (1.0 + lax.erf(hidden * 0.5**0.5))
        act[rows] = (hidden * normal).astype(BF16)
        density = (0.5 / jnp.pi) ** 0.5 * jnp.exp(-0.5 * hidden * hidden)
        slope[rows] = normal + hidden * density
    part(sc[0], dot_tn(act[...], b2g[...]).astype(BF16), go, gs)


def hidden_back_kernel(sc, b2g, n2, slope, own, other, hg, sums, go, gs, scr):
    w2 = join(scr, sc[0], own, other)
    total = jnp.zeros((8, sums.shape[1]), F32)
    for rows in pieces(b2g.shape[0], 256):
        low = (dot_nt(b2g[rows], w2) * slope[rows]).astype(BF16)
        hg[rows] = low
        total = total + eights(low.astype(F32))
    sums[...] = column_sum(total)
    part(sc[0], dot_tn(n2[...], hg[...]).astype(BF16), go, gs)


def middle_back_kernel(sc, hg, own, other, po, ps, b1, x, up, gain, ls, mg, b1g, ag, sums, acc, scr, pscr, *, tiles):
    step = pl.program_id(0)

    @pl.when(step == 0)
    def _():
        acc[...] = jnp.zeros_like(acc)

    @pl.when(step < tiles)
    def _():
        acc[...] += dot_nt(hg[...], join(scr, sc[0], own, other))

    @pl.when(step == tiles)
    def _():
        join(pscr, sc[0], po, ps)
        sums[...] = jnp.zeros_like(sums)

    @pl.when(step >= tiles)
    def _():
        size = x.shape[0]
        totals = [jnp.zeros((8, x.shape[1]), F32) for _ in range(4)]
        for rows in pieces(size):
            branch = b1[rows]
            scaled, inverse = standardize(x[rows].astype(F32) + ls[0:1] * branch)
            grad = acc[pl.ds(pl.multiple_of((step - tiles) * size + rows.start, 128), rows.size)]
            back = up[rows].astype(F32) + standardize_back(grad * gain[1:2], scaled, inverse)
            mg[rows] = back
            low = (ls[0:1] * back).astype(BF16)
            b1g[rows] = low
            terms = (back * branch, low.astype(F32), grad * scaled, grad)
            totals = [t + eights(v) for t, v in zip(totals, terms)]
        ag[...] = dot_nt(b1g[...], pscr[...].reshape(x.shape[1], x.shape[1])).astype(BF16)
        sums[...] += jnp.concatenate([column_sum(t) for t in totals], axis=0)


def attend_back_kernel(grid_ref, proj, ag, log_total, pg, sums, *, slot, head):
    step = pl.program_id(0)
    width = ag.shape[1]
    per = ag.shape[0] // slot
    pair = 2 * head
    heads = width // head
    factor = head ** (-0.5)
    low = lax.broadcasted_iota(jnp.int32, (slot, pair), 1) < head
    key_at = lax.broadcasted_iota(jnp.int32, (slot, slot), 0)

    @pl.when(step == 0)
    def _():
        sums[...] = jnp.zeros_like(sums)

    for i in range(per):
        ok = key_at < length_of(grid_ref, step * per + i)
        rows = pl.ds(i * slot, slot)
        found = []

        def put(t, j, d):
            d = d.astype(BF16)
            columns = pl.ds(t * width + j * pair, pair)
            pg[rows, columns] = d
            if t != 1:
                sums[:, columns] += eights(d.astype(F32))

        for j in range(width // pair):
            q, k, v = (proj[rows, pl.ds(t * width + j * pair, pair)] for t in range(3))
            out = ag[rows, pl.ds(j * pair, pair)]
            q = q * jnp.asarray(factor, BF16)
            k2 = stacked(k, low)
            scores = dot_nt(k2, q)
            pull = dot_nt(stacked(v, low), out)
            ps, ss = [], []
            for h in range(2):
                half = slice(h * slot, (h + 1) * slot)
                p = jnp.exp(jnp.where(ok, scores[half], NEGATIVE) - log_total[pl.ds(i * heads + 2 * j + h, 1)])
                g = pull[half]
                ps.append(p.astype(BF16))
                ss.append((p * (g - column_sum(g * p))).astype(BF16))
            s = jnp.concatenate(ss, axis=0)
            dk = dot(s, q)
            dv = dot(jnp.concatenate(ps, axis=0), out)
            put(1, j, jnp.where(low, dk[:slot], dk[slot:]))
            put(2, j, jnp.where(low, dv[:slot], dv[slot:]))
            found.append((s, k2))
        for j, (s, k2) in enumerate(found):
            put(0, j, dot_tn(s, k2) * factor)


def weight_kernel(sc, n1, att, pg, b1g, go, gs):
    step = pl.program_id(0)
    last = pl.num_programs(0) - 1

    @pl.when(step < last)
    def _():
        part(sc[0], dot_tn(n1[...], pg[...]).astype(BF16), go, gs)

    @pl.when(step == last)
    def _():
        part(sc[0], dot_tn(att[...], b1g[...]).astype(BF16), go, gs)


def input_back_kernel(grid_ref, sc, pg, own, other, x, mg, gain, out, sums, scr, acc, high, mid, *, images):
    step = pl.program_id(0)
    size, width = x.shape
    per = out.shape[0] // size

    @pl.when(step == 0)
    def _():
        join(scr, sc[0], own, other)
        sums[...] = jnp.zeros_like(sums)

    acc[...] = dot_nt(pg[...], scr[...].reshape(width, 3 * width))
    totals = [jnp.zeros((8, width), F32) for _ in range(2)]
    for rows in pieces(size):
        grad = acc[rows]
        scaled, inverse = standardize(x[rows].astype(F32))
        back = mg[rows] + standardize_back(grad * gain[0:1], scaled, inverse)
        totals = [t + eights(v) for t, v in zip(totals, (grad * scaled, grad))]
        big = back.astype(BF16)
        at = pl.ds(pl.multiple_of(step % per * size + rows.start, 128), rows.size)
        high[at] = big
        mid[at] = (back - big.astype(F32)).astype(BF16)
    sums[...] += jnp.concatenate([column_sum(t) for t in totals], axis=0)

    @pl.when(step % per == per - 1)
    def _():
        place = unplace(grid_ref, step // per, images, out.shape[0])
        out[...] = dot(place, high[...]) + dot(place, mid[...])


def layer_out_kernel(grid_ref, sc, act, own, other, x, b1, up, ls, fc2_bias, out, sums, acc, result, scr, *, images, tiles):
    step = pl.program_id(0)

    @pl.when(step == 0)
    def _():
        acc[...] = jnp.zeros_like(acc)

    @pl.when(step < tiles)
    def _():
        acc[...] += dot(act[...], join(scr, sc[0], own, other))

    @pl.when(step == tiles)
    def _():
        sums[...] = jnp.zeros_like(sums)

    @pl.when(step >= tiles)
    def _():
        pack, size = step - tiles, out.shape[0]
        total = jnp.zeros((8, x.shape[1]), F32)
        for rows in pieces(size):
            branch = acc[pl.ds(pl.multiple_of(pack * size + rows.start, 128), rows.size)] + fc2_bias[...]
            total = total + eights(up[rows].astype(F32) * branch)
            middle = x[rows].astype(F32) + ls[0:1] * b1[rows]
            result[rows] = (middle + ls[1:2] * branch).astype(BF16)
        out[...] = dot(unplace(grid_ref, pack, images, size), result[...]).astype(BF16)
        sums[...] += column_sum(total)


Y, CORE, X, Z = 1, 2, 4, 8


def swap(v, mask):
    return lax.ppermute(v, AXES, [(i, i ^ mask) for i in range(32)])


def move(plan, sc, ins, outs, after, mib=8):
    def kernel(*refs):
        for a, b in plan(*refs):
            b[...] = a[...]

    return call(
        kernel, (1,), (sc,), [(v, full(v.shape)) for v in ins], [(shape, BF16, full(shape)) for shape in outs], (), after, mib
    )


def gather_line(block):
    return [block] + [swap(block, Z * k) for k in (1, 2, 3)]


def gather_stack(line, sc, after, sides=()):
    rows, columns = line[0].shape
    half = columns // 2
    shapes = [(4, rows, half)] * 2 + [(2, 2) + side.shape for side in sides[:1]]

    def plan(sc, *refs):
        ins, outs = refs[: 4 + len(sides)], refs[4 + len(sides) :]
        pairs = [(ins[k].at[:, pl.ds(h * half, half)], outs[h].at[k]) for k in range(4) for h in range(2)]
        return pairs + [(side, outs[2].at[i // 2, i % 2]) for i, side in enumerate(ins[4:])]

    return move(plan, sc, [*line, *sides], shapes, after)


def gather_columns(line, sc, after):
    _, _, rows, half = line[0].shape

    def plan(sc, *refs):
        return [(refs[k].at[h, i], refs[4 + h].at[i, k]) for k in range(4) for h in range(2) for i in range(2)]

    return move(plan, sc, line, [(2, 4, rows, half)] * 2, after)


def pack_rows(qkv, proj, fc1, fc2, width, tiles):
    arrays = (qkv, proj, fc1, fc2)
    rows = proj.shape[0] * 128 // width
    columns = [v.shape[0] * 128 // rows for v in arrays]
    places = [(0, 0), (0, columns[0]), (1, 0), (2, 0)]
    half = columns[3] // 2

    def kernel(*refs):
        ins, outs, scrs = refs[:4], refs[4:8], refs[8:]
        for n, (ref, scr) in enumerate(zip(ins, scrs)):
            scr[...] = ref[...].astype(F32)
            if n < 3:
                blocks = [(i, columns[n] // 128) for i in range(columns[n] // 128)]
            else:
                lanes = width // 128
                blocks = [(k * rows * lanes + i, lanes) for k in range(tiles) for i in range(lanes)]
            for i, (start, stride) in enumerate(blocks):
                to, at = places[n]
                at += i * 128
                if n == 3:
                    to, at = to + at // half, at % half
                outs[to][:, pl.ds(at, 128)] = scr[pl.ds(start, rows, stride=stride)].astype(BF16)

    shapes = [(rows, columns[0] + columns[1]), (rows, columns[2]), (rows, half), (rows, half)]
    scratch = [pltpu.VMEM(v.shape, F32) for v in arrays]
    outs = [(shape, BF16, full(shape)) for shape in shapes]
    return call(kernel, (1,), (), [(far(v), full(v.shape)) for v in arrays], outs, scratch, (), mib=8)[:4]


def gather_pair(a, b, sc, after):
    def plan(sc, a, xa, b, yb, left, right):
        return [(a, left.at[0]), (xa, left.at[1]), (b, right.at[0]), (yb, right.at[1])]

    return move(plan, sc, (a, swap(a, X), b, swap(b, Y)), [(2,) + a.shape] * 2, after)


def gather_place(left, right, sc, after, runs=1):
    _, _, rows, half = left.shape
    width = 2 * half // runs

    def plan(sc, left, other_left, right, other_right, out):
        pairs = []
        for n, sides in enumerate(((left, other_left), (right, other_right))):
            for i in range(2):
                for j in range(2):
                    for k in range(4):
                        x, y = (i, j) if n == 0 else (j, i)
                        to = out.at[sc[3] ^ k, sc[1] ^ x, sc[2] ^ y]
                        if runs == 1:
                            pairs.append((sides[j].at[i, k], to.at[:, pl.ds(n * half, half)]))
                            continue
                        for r in range(runs // 2):
                            run = n * (runs // 2) + r
                            pairs.append((sides[j].at[i, k, :, pl.ds(r * width, width)], to.at[pl.ds(run * rows, rows)]))
        return pairs

    ins = [far(v) for v in (left, swap(left, Y), right, swap(right, X))]
    own, token = move(plan, sc, ins, [(4, 2, 2, runs * rows, width)], after, 12)
    shape = (COLUMNS, 2 * runs * rows, width)
    return own.reshape(shape), swap(own, CORE).reshape(shape), token


def add(a, b):
    return a.astype(F32) + b.astype(F32)


def fold_core(own, other, sc, after):
    _, rows2, columns = own.shape
    rows, half = rows2 // 2, columns // 2
    by_z = pl.BlockSpec((1, 2, 2, rows, columns), lambda i, *_: (i, 0, 0, 0, 0))
    to_z = pl.BlockSpec((1, 2, rows, half), lambda i, *_: (i, 0, 0, 0))
    left, right = pl.ds(0, half), pl.ds(half, half)

    def kernel(sc, own, got, ka, sa, kb, sb):
        for i in range(2):
            for a, b, flip in ((ka, kb, 0), (sa, sb, 1)):
                y, x = sc[2] ^ flip, sc[1] ^ flip
                a[0, i] = add(own[0, i, y, :, left], got[0, i, y, :, left]).astype(BF16)
                b[0, i] = add(own[0, x, i, :, right], got[0, x, i, :, right]).astype(BF16)

    ins = [(v.reshape(4, 2, 2, rows, columns), by_z) for v in (own, swap(other, CORE))]
    ka, sa, kb, sb, token = call(kernel, (4,), (sc,), ins, [((4, 2, rows, half), BF16, to_z)] * 4, (), after, mib=12)
    return [(ka, sa, Y), (kb, sb, X)], token


def columns_of(parts):
    rows = min(keep.shape[2] for keep, _, _ in parts)
    places, at = [], 0
    for n, (keep, _, _) in enumerate(parts):
        for first in range(0, keep.shape[2], rows):
            places.append((n, first, at, keep.shape[3]))
            at += keep.shape[3]
    return rows, at, places


def fold_first(parts, sc, after):
    groups = [[part for part in parts if part[2] == mask] for mask in (Y, X)]
    ins = [(v, full(v.shape)) for group in groups for keep, send, mask in group for v in (keep, swap(send, mask))]
    layouts = [columns_of(group) for group in groups]
    outs = [((4, rows, width), BF16, full((4, rows, width))) for rows, width, _ in layouts for _ in range(2)]

    def kernel(sc, *refs):
        ins, outs, base = refs[: len(ins_)], refs[len(ins_) :], 0
        for g, (rows, _, places) in enumerate(layouts):
            for n, first, at, width in places:
                keep, got = ins[base + 2 * n], ins[base + 2 * n + 1]
                cut = pl.ds(first, rows)
                for z in range(4):
                    for flip in range(2):
                        here = sc[1 + g] ^ flip
                        to = outs[2 * g + flip]
                        to[z, :, pl.ds(at, width)] = add(keep[z, here, cut], got[z, here, cut]).astype(BF16)
            base += 2 * len(groups[g])

    ins_ = ins
    out = call(kernel, (1,), (sc,), ins, outs, (), after, mib=16)
    return [(out[0], out[1], X), (out[2], out[3], Y)], out[4]


def fold_second(parts, sc, after):
    ins = [(v, full(v.shape)) for keep, send, mask in parts for v in (keep, swap(send, mask))]
    _, rows, width = parts[0][0].shape
    shape = (rows, 2 * width)

    def kernel(sc, *refs):
        ins, outs = refs[:4], refs[4:]
        for k, to in enumerate(outs):
            z = sc[3] ^ k
            for n in range(2):
                to[:, pl.ds(n * width, width)] = add(ins[2 * n][z], ins[2 * n + 1][z]).astype(to.dtype)

    outs = [(shape, F32, full(shape))] + [(shape, BF16, full(shape))] * 3
    return call(kernel, (1,), (sc,), ins, outs, (), after, mib=12)


def fold_sends(parts):
    keep, *sends, token = parts
    return token, [keep] + [swap(v, Z * k) for k, v in zip((1, 2, 3), sends)]


def fold_last(parts, shapes, runs, after):
    def kernel(keep, r1, r2, r3, *outs):
        rows = keep.shape[0]
        for i, (n, first, stride) in enumerate(runs):
            cut = (slice(None), pl.ds(i * 128, 128))
            total = keep[cut] + (r1[cut].astype(F32) + r2[cut].astype(F32) + r3[cut].astype(F32))
            outs[n][pl.ds(first, rows, stride=stride)] = total

    ins = [(v, full(v.shape)) for v in parts]
    return call(kernel, (1,), (), ins, [(shape, F32, full(shape)) for shape in shapes], (), after, mib=12)


def reduce_sends(v, masks):
    return [v] + [swap(v, mask) for mask in masks]


def reduce_level(ins, at, sc, after, split=None):
    v = ins[0]
    shapes, where = split or ([v.shape], [(0, pl.ds(i, 1)) for i in range(v.shape[0])])

    def kernel(sc, *refs):
        line, outs = refs[-1], refs[-1 - len(shapes) : -1]
        mine = sc[at[0]]
        for k in at[1:]:
            mine = 2 * mine + sc[k]
        for k, ref in enumerate(refs[: len(ins)]):
            line[mine ^ k] = ref[...]
        total = line[0]
        for k in range(1, len(ins)):
            total = total + line[k]
        for i, (n, place) in enumerate(where):
            row = total[i : i + 1]
            outs[n][place] = row[0] if len(shapes[n]) == 1 else row

    outs = [(shape, F32, full(shape)) for shape in shapes]
    scratch = [pltpu.VMEM((len(ins),) + v.shape, F32)]
    return call(kernel, (1,), (sc,), [(u, full(v.shape)) for u in ins], outs, scratch, after, mib=8)


def body(
    tokens,
    patch_grid,
    qkv_rows,
    proj_rows,
    fc1_rows,
    fc2_rows,
    norm_gain,
    norm_bias,
    qv_bias,
    proj_bias,
    fc1_bias,
    fc2_bias,
    layer_scale,
    cotangent,
):
    rows, width = tokens.shape
    packs, images, _ = patch_grid.shape
    pack = rows // packs
    slot = pack // images
    head = width // H
    hidden = fc1_bias.shape[0]
    row_width = qkv_rows.shape[1]
    tiles = hidden // width
    tile = min(256, rows)
    swaps = lax.axis_size("wide") == 16 and lax.axis_size("narrow") == 2
    if swaps:
        me = lax.axis_index(AXES)
        sc = jnp.stack([me // CORE % 2, me // X % 2, me % 2, me // Z]).astype(jnp.int32)
    else:
        sc = jnp.zeros((4,), jnp.int32)
    grid_flat = patch_grid.reshape(-1)
    thin, wide_rows = width // (2 * COLUMNS), hidden // (2 * COLUMNS)
    per_tile = COLUMNS // tiles

    by_pack = pl.BlockSpec((pack, width), lambda i, *_: (i, 0))
    by_tile = lambda w: pl.BlockSpec((tile, w), lambda i, *_: (i, 0))
    whole = full((rows, width))
    proj_blocks = pl.BlockSpec((COLUMNS, thin, width), lambda i, *_: (0, 0, 3), pipeline_mode=pl.Buffered(1))
    fc2_blocks = pl.BlockSpec((per_tile, wide_rows, width), lambda i, *_: (i, 0, 0))
    column_blocks = pl.BlockSpec((COLUMNS, thin, width), lambda i, *_: (0, 0, i))
    hidden_tile = pl.BlockSpec((rows, width), lambda i, *_: (0, i))
    vec1, vec2 = full((1, width)), full((2, width))
    hidden_vec = pl.BlockSpec((1, width), lambda i, *_: (0, i))
    qkv_blocks = full((COLUMNS, thin, 3 * width))
    qkv_scr = pltpu.VMEM((COLUMNS, 2, thin, 3 * width), BF16)
    fc2_scr = pltpu.VMEM((per_tile, 2, wide_rows, width), BF16)
    thin_scr = pltpu.VMEM((COLUMNS, 2, thin, width), BF16)
    sum_scr = pltpu.VMEM((rows, width), F32)
    turned_scr = pltpu.VMEM((width, rows), BF16)
    log_block = pl.BlockSpec((tile // slot * H, slot), lambda i, *_: (i, 0))

    halves = lambda v: v.reshape(COLUMNS, 2, -1, v.shape[1]).transpose(1, 0, 2, 3)
    ready = []
    if swaps:
        qp_block, fc1_block, a, b = pack_rows(qkv_rows, proj_rows, fc1_rows, fc2_rows, width, tiles)
        qp_line, fc1_line = gather_line(qp_block), gather_line(fc1_block)
        *qp_ab, message, _ = gather_stack(qp_line, sc, [], (a, swap(a, X), b, swap(b, Y)))
        fc2_line = gather_line(message)
        *qp_pair, token = gather_pair(*qp_ab, sc, [fc1_line[1], fc1_line[3]])
        ready = [token]
    else:
        qp_block = jnp.concatenate([qkv_rows.reshape(-1, 3 * width), proj_rows.reshape(-1, width)], axis=1)
        fc1_block, fc2_block = fc1_rows.reshape(-1, hidden), fc2_rows.reshape(-1, width)
        qp_own, qp_other = halves(lax.all_gather(qp_block, AXES, axis=0, tiled=True))
        fc1_own, fc1_other = halves(lax.all_gather(fc1_block, AXES, axis=0, tiled=True))
        fc2_own, fc2_other = halves(lax.all_gather(fc2_block, AXES, axis=0, tiled=True))

    x, n1, up, b2g, fc2_sums, token = call(
        partial(prepare_kernel, images=images),
        (packs,),
        (grid_flat,),
        [(far(tokens), by_pack), (far(cotangent), by_pack), (norm_gain, vec2), (norm_bias, vec2), (layer_scale, vec2)],
        [((rows, width), BF16, by_pack, "far")] * 4 + [((1, width), F32, vec1)],
        (),
        ready,
        mib=14,
    )

    ready = []
    if swaps:
        *fc1_ab, token = gather_stack(fc1_line, sc, [token, fc2_line[1]])
        qp_own, qp_other, token = gather_place(*qp_pair, sc, [token])
        ready = [token]

    offset = jnp.concatenate([qv_bias[0], jnp.zeros_like(qv_bias[0]), qv_bias[1]])[None]
    proj, att, log_total, token = call(
        partial(attend_kernel, slot=slot, head=head),
        (rows // tile,),
        (grid_flat, sc),
        [(far(n1), by_tile(width)), (qp_own, qkv_blocks), (qp_other, qkv_blocks), (offset, full((1, 3 * width)))],
        [((rows, 3 * width), BF16, by_tile(3 * width), "far"), ((rows, width), BF16, by_tile(width))]
        + [((rows // slot * H, slot), F32, log_block)],
        [qkv_scr],
        ready,
        mib=24,
    )
    ready = []
    if swaps:
        *fc1_pair, token = gather_pair(*fc1_ab, sc, [token, fc2_line[2]])
        ready = [token]
    b1, n2, token = call(
        middle_kernel,
        (1,),
        (sc,),
        [(att, whole), (x, whole), (norm_gain, vec2), (norm_bias, vec2), (layer_scale, vec2), (proj_bias[None], vec1)]
        + [(qp_own, proj_blocks), (qp_other, proj_blocks)],
        [((rows, width), F32, whole, "far"), ((rows, width), BF16, whole)],
        [sum_scr, thin_scr],
        ready,
        mib=20,
    )
    ready = []
    if swaps:
        *fc2_pair, token = gather_columns(fc2_line, sc, [token])
        fc1_own, fc1_other, token = gather_place(*fc1_pair, sc, [token])
        ready = [token]
    cut = tiles - 1

    def some_tiles(first, count, after, alias=None):
        columns = pl.BlockSpec((COLUMNS, thin, width), lambda i, *_: (0, 0, i + first))
        outs = pl.BlockSpec((rows, width), lambda i, *_: (0, i + first))
        blocks = pl.BlockSpec((per_tile, wide_rows, width), lambda i, *_: (i + first, 0, 0))
        return call(
            hidden_kernel,
            (count,),
            (sc,),
            [(n2, whole), (b2g, whole), (fc1_bias[None], pl.BlockSpec((1, width), lambda i, *_: (0, i + first)))]
            + [(fc1_own, columns), (fc1_other, columns)],
            [((rows, hidden), BF16, outs, "far"), ((rows, hidden), F32, outs, "far")]
            + [((COLUMNS, wide_rows, width), BF16, blocks, "far")] * 2,
            [thin_scr],
            after,
            mib=24,
            alias=alias,
        )

    *made, token = some_tiles(0, cut, ready)
    if swaps:
        fc2_own, fc2_other, token = gather_place(*fc2_pair, sc, [token], tiles)
    *made, token = some_tiles(cut, tiles - cut, made + [token], {i: i for i in range(4)})
    act, slope, fc2g_own, fc2g_other = made

    hg, fc1_sums, fc1g_own, fc1g_other, token = call(
        hidden_back_kernel,
        (tiles,),
        (sc,),
        [(far(b2g), whole), (far(n2), whole), (far(slope), hidden_tile), (fc2_own, fc2_blocks), (fc2_other, fc2_blocks)],
        [((rows, hidden), BF16, hidden_tile, "far"), ((1, hidden), F32, hidden_vec)]
        + [((COLUMNS, thin, hidden), BF16, column_blocks, "far")] * 2,
        [fc2_scr],
        mib=26,
    )
    chain = []
    if swaps:
        fc2_parts, token = fold_core(fc2g_own, fc2g_other, sc, [token])
        chain = [token]

    bound = lambda i: jnp.minimum(i, tiles - 1)
    hidden_first = pl.BlockSpec((rows, width), lambda i, *_: (0, bound(i)))
    column_first = pl.BlockSpec((COLUMNS, thin, width), lambda i, *_: (0, 0, bound(i)))
    fc2_first = pl.BlockSpec((per_tile, wide_rows, width), lambda i, *_: (bound(i), 0, 0))
    then = lambda size: pl.BlockSpec((size, width), lambda i, *_: (jnp.maximum(i - tiles, 0), 0))
    mg, b1g, ag, middle_sums, token = call(
        partial(middle_back_kernel, tiles=tiles),
        (tiles + rows // tile,),
        (sc,),
        [(far(hg), hidden_first), (fc1_own, column_first), (fc1_other, column_first)]
        + [(qp_own, proj_blocks), (qp_other, proj_blocks)]
        + [(b1, then(tile)), (x, then(tile)), (up, then(tile)), (norm_gain, vec2), (layer_scale, vec2)],
        [((rows, width), F32, then(tile), "far"), ((rows, width), BF16, then(tile)), ((rows, width), BF16, then(tile))]
        + [((4, width), F32, full((4, width)))],
        [sum_scr, thin_scr, thin_scr],
        chain,
        mib=28,
    )
    chain = []
    if swaps:
        fc1_parts, token = fold_core(fc1g_own, fc1g_other, sc, [token])
        chain = [token]

    pg, proj_sums, token = call(
        partial(attend_back_kernel, slot=slot, head=head),
        (rows // tile,),
        (grid_flat,),
        [(far(proj), by_tile(3 * width)), (ag, by_tile(width)), (log_total, log_block)],
        [((rows, 3 * width), BF16, by_tile(3 * width)), ((8, 3 * width), F32, full((8, 3 * width)))],
        (),
        chain,
        mib=14,
    )
    chain = []
    if swaps:
        fc_parts, token = fold_first(fc1_parts + fc2_parts, sc, [token])
        chain = [token]

    qp_grad_own, qp_grad_other, token = call(
        weight_kernel,
        (4,),
        (sc,),
        [(n1, whole), (att, whole), (pg, pl.BlockSpec((rows, width), lambda i, *_: (0, jnp.minimum(i, 2)))), (b1g, whole)],
        [((COLUMNS, thin, 4 * width), BF16, column_blocks)] * 2,
        (),
        chain,
        mib=18,
    )
    per = pack // tile
    input_grad, input_sums, token = call(
        partial(input_back_kernel, images=images),
        (rows // tile,),
        (grid_flat, sc),
        [(pg, by_tile(3 * width)), (qp_own, qkv_blocks), (qp_other, qkv_blocks)]
        + [(x, by_tile(width)), (far(mg), by_tile(width)), (norm_gain, vec2)],
        [((rows, width), F32, pl.BlockSpec((pack, width), lambda i, *_: (i // per, 0)), "far"), ((2, width), F32, vec2)],
        [qkv_scr, pltpu.VMEM((tile, width), F32)] + [pltpu.VMEM((pack, width), BF16)] * 2,
        [token],
        mib=24,
    )

    chain = []
    if swaps:
        qp_parts, token = fold_core(qp_grad_own, qp_grad_other, sc, [token])
        token, fc_parts = fold_sends(fold_second(fc_parts, sc, [token]))
        chain = [token]

    layer_out, out_sums, token = call(
        partial(layer_out_kernel, images=images, tiles=tiles),
        (tiles + packs,),
        (grid_flat, sc),
        [(far(act), hidden_first), (fc2_own, fc2_first), (fc2_other, fc2_first), (x, then(pack)), (b1, then(pack)), (up, then(pack))]
        + [(layer_scale, vec2), (fc2_bias[None], vec1)],
        [((rows, width), BF16, then(pack), "far"), ((1, width), F32, vec1)],
        [sum_scr, pltpu.VMEM((pack, width), BF16), fc2_scr],
        chain,
        mib=26,
    )
    chain = []
    if swaps:
        qp_parts, token = fold_first(qp_parts, sc, [token, fc_parts[1]])
        chain = [token]

    def gather_sums(input_sums, middle, proj, fc2, out, fc1, to):
        q, v = column_sum(proj[:, pl.ds(0, width)]), column_sum(proj[:, pl.ds(2 * width, width)])
        lines = (input_sums[0:1], middle[2:3], input_sums[1:2], middle[3:4], q, v, middle[1:2], fc2[...], middle[0:1], out[...])
        for i, line in enumerate(lines):
            to[pl.ds(i, 1)] = line
        for i in range(tiles):
            to[pl.ds(len(lines) + i, 1)] = fc1[:, pl.ds(i * width, width)]

    sums_in = (input_sums, middle_sums, proj_sums, fc2_sums, out_sums, fc1_sums)
    sums, token = call(
        gather_sums,
        (1,),
        (),
        [(v, full(v.shape)) for v in sums_in],
        [((10 + tiles, width), F32, full((10 + tiles, width)))],
        (),
        chain,
    )
    if swaps:
        fc2_rows_of = fc2_rows.shape[0] // tiles
        n1_runs, n2_runs = hidden // 256, width // 256
        fc_runs = []
        for half in range(2):
            fc_runs += [(0, half * n1_runs + i, hidden // 128) for i in range(n1_runs)]
            fc_runs += [(1, k * fc2_rows_of + half * n2_runs + i, width // 128) for k in range(tiles) for i in range(n2_runs)]
        sums, token = reduce_level(reduce_sends(sums, (CORE,)), (0,), sc, [token])
        sums, token = reduce_level(reduce_sends(sums, (Y,)), (2,), sc, [token])
        token, qp_parts = fold_sends(fold_second(qp_parts, sc, [token, fc_parts[2], fc_parts[3]]))
        sums, token = reduce_level(reduce_sends(sums, (X,)), (1,), sc, [token])
        fc1_grad, fc2_grad, token = fold_last(fc_parts, (fc1_rows.shape, fc2_rows.shape), fc_runs, [token, qp_parts[1]])
        line = lambda i: pl.ds(i * width, width)
        shapes = [(2, width)] * 3 + [(width,), (hidden,), (width,), (2, width)]
        where = [(i // 2, pl.ds(i % 2, 1)) for i in range(6)] + [(3, line(0)), (5, line(0))]
        where += [(6, pl.ds(0, 1)), (6, pl.ds(1, 1))] + [(4, line(i)) for i in range(tiles)]
        sums = reduce_sends(sums, (Z, 2 * Z, 3 * Z))
        *small, token = reduce_level(sums, (3,), sc, [token] + qp_parts[2:], (shapes, where))
        qkv_runs, proj_runs = 3 * width // 128, width // 128
        qp_runs = [(0, i, qkv_runs) for i in range(qkv_runs)] + [(1, i, proj_runs) for i in range(proj_runs)]
        qkv_grad, proj_grad, _ = fold_last(qp_parts, (qkv_rows.shape, proj_rows.shape), qp_runs, [token])
    else:

        def scatter(own, other):
            matrix = jnp.stack([own, other], axis=1).reshape(-1, own.shape[-1])
            return lax.psum_scatter(matrix, AXES, scatter_dimension=0, tiled=True).astype(F32)

        fc2_grad = scatter(fc2g_own, fc2g_other).reshape(-1, row_width)
        fc1_grad = scatter(fc1g_own, fc1g_other).reshape(-1, row_width)
        qp_grad = scatter(qp_grad_own, qp_grad_other)
        qkv_grad = qp_grad[:, : 3 * width].reshape(-1, row_width)
        proj_grad = qp_grad[:, 3 * width :].reshape(-1, row_width)
        sums = lax.psum(sums, AXES)
        small = [sums[0:2], sums[2:4], sums[4:6], sums[6], sums[10:].reshape(-1), sums[7], sums[8:10]]
    return (
        layer_out,
        input_grad,
        qkv_grad,
        proj_grad,
        fc1_grad,
        fc2_grad,
        *(v.reshape(leaf.shape) for v, leaf in zip(small, (norm_gain, norm_bias, qv_bias, proj_bias, fc1_bias, fc2_bias, layer_scale))),
    )


def solution(mesh):
    split = P(AXES, None)
    return jax.shard_map(
        body,
        mesh=mesh,
        in_specs=(split, P(AXES, None, None)) + (split,) * 4 + (P(),) * 7 + (split,),
        out_specs=(split,) * 6 + (P(),) * 7,
        check_vma=False,
    )
```

```python
from functools import partial

import jax
import jax.numpy as jnp
from jax import lax
from jax.experimental import pallas as pl
from jax.experimental.pallas import tpu as pltpu
from jax.sharding import PartitionSpec as P

H = 12
PREFIX = 5
EPSILON = 1e-06
NEGATIVE = -1e30
AXES = ("wide", "narrow")
COLUMNS = 8
BF16 = jnp.bfloat16
F32 = jnp.float32


def dot(a, b):
    return lax.dot_general(a, b, (((1,), (0,)), ((), ())), preferred_element_type=F32)


def dot_nt(a, b):
    return lax.dot_general(a, b, (((1,), (1,)), ((), ())), preferred_element_type=F32)


def dot_tn(a, b):
    return lax.dot_general(a, b, (((0,), (0,)), ((), ())), preferred_element_type=F32)


TOKEN = (8, 128)


def call(kernel, grid, scalars, ins, outs, scratch=(), after=(), mib=36, alias=None):
    n, m = len(scalars) + len(ins), len(outs)

    def run(*refs):
        rest = refs[n + len(after) :]
        rest[m][...] = jnp.zeros(TOKEN, F32)
        kernel(*refs[:n], *rest[:m], *rest[m + 1 :])

    anywhere = pl.BlockSpec(memory_space=pl.ANY)
    return pl.pallas_call(
        run,
        grid_spec=pltpu.PrefetchScalarGridSpec(
            num_scalar_prefetch=len(scalars),
            grid=grid,
            in_specs=[spec for _, spec in ins] + [anywhere] * len(after),
            out_specs=[out[2] for out in outs] + [full(TOKEN)],
            scratch_shapes=list(scratch),
        ),
        out_shape=[
            pltpu.HBM(out[0], out[1]) if len(out) > 3 else jax.ShapeDtypeStruct(out[0], out[1]) for out in outs
        ]
        + [jax.ShapeDtypeStruct(TOKEN, F32)],
        input_output_aliases={n + k: to for k, to in (alias or {}).items()},
        compiler_params=pltpu.CompilerParams(vmem_limit_bytes=mib * 2**20),
        cost_estimate=pl.CostEstimate(flops=1, bytes_accessed=1, transcendentals=0),
    )(*scalars, *(array for array, _ in ins), *after)


def far(v):
    return pltpu.with_memory_space_constraint(v, pltpu.HBM)


def full(shape):
    return pl.BlockSpec(shape, lambda *_: (0,) * len(shape), pipeline_mode=pl.Buffered(1))


def standardize(v):
    centered = v - jnp.mean(v, axis=-1, keepdims=True)
    inverse = lax.rsqrt(jnp.mean(centered * centered, axis=-1, keepdims=True) + EPSILON)
    return centered * inverse, inverse


def standardize_back(grad, scaled, inverse):
    return inverse * (
        grad
        - jnp.mean(grad, axis=-1, keepdims=True)
        - scaled * jnp.mean(grad * scaled, axis=-1, keepdims=True)
    )


def length_of(grid_ref, image):
    return PREFIX + grid_ref[2 * image] * grid_ref[2 * image + 1]


def spans(grid_ref, pack, images):
    found, start = [], 0
    for i in range(images):
        length = length_of(grid_ref, pack * images + i)
        found.append((start, length))
        start = start + length
    return found


def join(scr, core, own, other):
    for i in range(scr.shape[0]):
        scr[i, core] = own[i]
        scr[i, 1 - core] = other[i]
    blocks, cores, rows, columns = scr.shape
    return scr[...].reshape(blocks * cores * rows, columns)


def part(core, matrix, own, other):
    blocks, rows, columns = own.shape
    cut = matrix.reshape(blocks, 2, rows, columns)
    own[...] = jnp.where(core == 0, cut[:, 0], cut[:, 1])
    other[...] = jnp.where(core == 0, cut[:, 1], cut[:, 0])


def prepare_kernel(grid_ref, tok, cot, gain, bias, ls, x, n1, up, b2g, sums, *, images):
    pack = pl.program_id(0)
    slot = tok.shape[0] // images
    row = lax.broadcasted_iota(jnp.int32, (slot, tok.shape[0]), 0)
    column = lax.broadcasted_iota(jnp.int32, (slot, tok.shape[0]), 1)

    def image(i, carry):
        start, total = carry
        length = length_of(grid_ref, pack * images + i)
        place = jnp.where((column - row == start) & (row < length), 1.0, 0.0).astype(BF16)
        rows = pl.ds(pl.multiple_of(i * slot, slot), slot)
        moved = dot(place, tok[...])
        x[rows] = moved.astype(BF16)
        scaled, _ = standardize(moved)
        n1[rows] = (scaled * gain[0:1] + bias[0:1]).astype(BF16)
        upstream = dot(place, cot[...])
        up[rows] = upstream.astype(BF16)
        low = (ls[1:2] * upstream).astype(BF16)
        b2g[rows] = low
        return start + length, total + column_sum(low.astype(F32))

    _, total = lax.fori_loop(0, images, image, (jnp.int32(0), jnp.zeros((1, tok.shape[1]), F32)))

    @pl.when(pack == 0)
    def _():
        sums[...] = jnp.zeros_like(sums)

    sums[...] += total


def unplace(grid_ref, pack, images, size):
    slot = size // images
    row = lax.broadcasted_iota(jnp.int32, (size, slot), 0)
    column = lax.broadcasted_iota(jnp.int32, (size, slot), 1)
    return jnp.concatenate(
        [
            jnp.where((row - column == start) & (column < length), 1.0, 0.0).astype(BF16)
            for start, length in spans(grid_ref, pack, images)
        ],
        axis=1,
    )


def pieces(rows, size=128):
    return [pl.ds(r, size) for r in range(0, rows, size)]


def eights(v):
    return jnp.sum(v.reshape(-1, 8, v.shape[1]), axis=0)


def column_sum(v):
    return jnp.sum(v, axis=0, keepdims=True)


def stacked(v, low):
    zero = jnp.zeros_like(v)
    return jnp.concatenate([jnp.where(low, v, zero), jnp.where(low, zero, v)], axis=0)


def attend_kernel(grid_ref, sc, n1, own, other, offset, proj, att, log_total, scr, *, slot, head):
    step = pl.program_id(0)
    width = n1.shape[1]
    per = n1.shape[0] // slot
    pair = 2 * head
    heads = width // head

    @pl.when(step == 0)
    def _():
        join(scr, sc[0], own, other)

    w = scr[...].reshape(width, 3 * width)
    proj[...] = (dot(n1[...], w) + offset[...]).astype(BF16)
    low = lax.broadcasted_iota(jnp.int32, (slot, pair), 1) < head
    key_at = lax.broadcasted_iota(jnp.int32, (slot, slot), 0)
    for i in range(per):
        ok = key_at < length_of(grid_ref, step * per + i)
        rows = pl.ds(i * slot, slot)
        found = []
        for j in range(width // pair):
            q, k = (proj[rows, pl.ds(t * width + j * pair, pair)] for t in range(2))
            scores = dot_nt(stacked(k, low), q * jnp.asarray(head ** (-0.5), BF16))
            halves = []
            for h in range(2):
                masked = jnp.where(ok, scores[h * slot : (h + 1) * slot], NEGATIVE)
                top = jnp.max(masked, axis=0, keepdims=True)
                exponent = jnp.exp(masked - top)
                total = column_sum(exponent)
                halves.append((exponent * (1.0 / total)).astype(BF16))
                log_total[pl.ds(i * heads + 2 * j + h, 1)] = top + jnp.log(total)
            found.append(jnp.concatenate(halves, axis=0))
        for j, p in enumerate(found):
            v = proj[rows, pl.ds(2 * width + j * pair, pair)]
            att[rows, pl.ds(j * pair, pair)] = dot_tn(p, stacked(v, low)).astype(BF16)


def middle_kernel(sc, att, x, gain, bias, ls, proj_bias, own, other, b1, n2, acc, scr):
    acc[...] = dot(att[...], join(scr, sc[0], own, other))
    for rows in pieces(acc.shape[0]):
        branch = acc[rows] + proj_bias[...]
        b1[rows] = branch
        scaled, _ = standardize(x[rows].astype(F32) + ls[0:1] * branch)
        n2[rows] = (scaled * gain[1:2] + bias[1:2]).astype(BF16)


def hidden_kernel(sc, n2, b2g, fc1_bias, own, other, act, slope, go, gs, scr):
    w1 = join(scr, sc[0], own, other)
    for rows in pieces(n2.shape[0]):
        hidden = dot(n2[rows], w1) + fc1_bias[...]
        normal = 0.5 * (1.0 + lax.erf(hidden * 0.5**0.5))
        act[rows] = (hidden * normal).astype(BF16)
        density = (0.5 / jnp.pi) ** 0.5 * jnp.exp(-0.5 * hidden * hidden)
        slope[rows] = normal + hidden * density
    part(sc[0], dot_tn(act[...], b2g[...]).astype(BF16), go, gs)


def hidden_back_kernel(sc, b2g, n2, slope, own, other, hg, sums, go, gs, scr):
    w2 = join(scr, sc[0], own, other)
    total = jnp.zeros((8, sums.shape[1]), F32)
    for rows in pieces(b2g.shape[0], 256):
        low = (dot_nt(b2g[rows], w2) * slope[rows]).astype(BF16)
        hg[rows] = low
        total = total + eights(low.astype(F32))
    sums[...] = column_sum(total)
    part(sc[0], dot_tn(n2[...], hg[...]).astype(BF16), go, gs)


def middle_back_kernel(sc, hg, own, other, po, ps, b1, x, up, gain, ls, mg, b1g, ag, sums, acc, scr, pscr, *, tiles):
    step = pl.program_id(0)

    @pl.when(step == 0)
    def _():
        acc[...] = jnp.zeros_like(acc)

    @pl.when(step < tiles)
    def _():
        acc[...] += dot_nt(hg[...], join(scr, sc[0], own, other))

    @pl.when(step == tiles)
    def _():
        join(pscr, sc[0], po, ps)
        sums[...] = jnp.zeros_like(sums)

    @pl.when(step >= tiles)
    def _():
        size = x.shape[0]
        totals = [jnp.zeros((8, x.shape[1]), F32) for _ in range(4)]
        for rows in pieces(size):
            branch = b1[rows]
            scaled, inverse = standardize(x[rows].astype(F32) + ls[0:1] * branch)
            grad = acc[pl.ds(pl.multiple_of((step - tiles) * size + rows.start, 128), rows.size)]
            back = up[rows].astype(F32) + standardize_back(grad * gain[1:2], scaled, inverse)
            mg[rows] = back
            low = (ls[0:1] * back).astype(BF16)
            b1g[rows] = low
            terms = (back * branch, low.astype(F32), grad * scaled, grad)
            totals = [t + eights(v) for t, v in zip(totals, terms)]
        ag[...] = dot_nt(b1g[...], pscr[...].reshape(x.shape[1], x.shape[1])).astype(BF16)
        sums[...] += jnp.concatenate([column_sum(t) for t in totals], axis=0)


def attend_back_kernel(grid_ref, proj, ag, log_total, pg, sums, *, slot, head):
    step = pl.program_id(0)
    width = ag.shape[1]
    per = ag.shape[0] // slot
    pair = 2 * head
    heads = width // head
    factor = head ** (-0.5)
    low = lax.broadcasted_iota(jnp.int32, (slot, pair), 1) < head
    key_at = lax.broadcasted_iota(jnp.int32, (slot, slot), 0)

    @pl.when(step == 0)
    def _():
        sums[...] = jnp.zeros_like(sums)

    for i in range(per):
        ok = key_at < length_of(grid_ref, step * per + i)
        rows = pl.ds(i * slot, slot)
        found = []

        def put(t, j, d):
            d = d.astype(BF16)
            columns = pl.ds(t * width + j * pair, pair)
            pg[rows, columns] = d
            if t != 1:
                sums[:, columns] += eights(d.astype(F32))

        for j in range(width // pair):
            q, k, v = (proj[rows, pl.ds(t * width + j * pair, pair)] for t in range(3))
            out = ag[rows, pl.ds(j * pair, pair)]
            q = q * jnp.asarray(factor, BF16)
            k2 = stacked(k, low)
            scores = dot_nt(k2, q)
            pull = dot_nt(stacked(v, low), out)
            ps, ss = [], []
            for h in range(2):
                half = slice(h * slot, (h + 1) * slot)
                p = jnp.exp(jnp.where(ok, scores[half], NEGATIVE) - log_total[pl.ds(i * heads + 2 * j + h, 1)])
                g = pull[half]
                ps.append(p.astype(BF16))
                ss.append((p * (g - column_sum(g * p))).astype(BF16))
            s = jnp.concatenate(ss, axis=0)
            dk = dot(s, q)
            dv = dot(jnp.concatenate(ps, axis=0), out)
            put(1, j, jnp.where(low, dk[:slot], dk[slot:]))
            put(2, j, jnp.where(low, dv[:slot], dv[slot:]))
            found.append((s, k2))
        for j, (s, k2) in enumerate(found):
            put(0, j, dot_tn(s, k2) * factor)


def weight_kernel(sc, n1, att, pg, b1g, go, gs):
    step = pl.program_id(0)
    last = pl.num_programs(0) - 1

    @pl.when(step < last)
    def _():
        part(sc[0], dot_tn(n1[...], pg[...]).astype(BF16), go, gs)

    @pl.when(step == last)
    def _():
        part(sc[0], dot_tn(att[...], b1g[...]).astype(BF16), go, gs)


def input_back_kernel(grid_ref, sc, pg, own, other, x, mg, gain, out, sums, scr, acc, high, mid, *, images):
    step = pl.program_id(0)
    size, width = x.shape
    per = out.shape[0] // size

    @pl.when(step == 0)
    def _():
        join(scr, sc[0], own, other)
        sums[...] = jnp.zeros_like(sums)

    acc[...] = dot_nt(pg[...], scr[...].reshape(width, 3 * width))
    totals = [jnp.zeros((8, width), F32) for _ in range(2)]
    for rows in pieces(size):
        grad = acc[rows]
        scaled, inverse = standardize(x[rows].astype(F32))
        back = mg[rows] + standardize_back(grad * gain[0:1], scaled, inverse)
        totals = [t + eights(v) for t, v in zip(totals, (grad * scaled, grad))]
        big = back.astype(BF16)
        at = pl.ds(pl.multiple_of(step % per * size + rows.start, 128), rows.size)
        high[at] = big
        mid[at] = (back - big.astype(F32)).astype(BF16)
    sums[...] += jnp.concatenate([column_sum(t) for t in totals], axis=0)

    @pl.when(step % per == per - 1)
    def _():
        place = unplace(grid_ref, step // per, images, out.shape[0])
        out[...] = dot(place, high[...]) + dot(place, mid[...])


def layer_out_kernel(grid_ref, sc, act, own, other, x, b1, up, ls, fc2_bias, out, sums, acc, result, scr, *, images, tiles):
    step = pl.program_id(0)

    @pl.when(step == 0)
    def _():
        acc[...] = jnp.zeros_like(acc)

    @pl.when(step < tiles)
    def _():
        acc[...] += dot(act[...], join(scr, sc[0], own, other))

    @pl.when(step == tiles)
    def _():
        sums[...] = jnp.zeros_like(sums)

    @pl.when(step >= tiles)
    def _():
        pack, size = step - tiles, out.shape[0]
        total = jnp.zeros((8, x.shape[1]), F32)
        for rows in pieces(size):
            branch = acc[pl.ds(pl.multiple_of(pack * size + rows.start, 128), rows.size)] + fc2_bias[...]
            total = total + eights(up[rows].astype(F32) * branch)
            middle = x[rows].astype(F32) + ls[0:1] * b1[rows]
            result[rows] = (middle + ls[1:2] * branch).astype(BF16)
        out[...] = dot(unplace(grid_ref, pack, images, size), result[...]).astype(BF16)
        sums[...] += column_sum(total)


Y, CORE, X, Z = 1, 2, 4, 8


def swap(v, mask):
    return lax.ppermute(v, AXES, [(i, i ^ mask) for i in range(32)])


def move(plan, sc, ins, outs, after, mib=8):
    def kernel(*refs):
        for a, b in plan(*refs):
            b[...] = a[...]

    return call(
        kernel, (1,), (sc,), [(v, full(v.shape)) for v in ins], [(shape, BF16, full(shape)) for shape in outs], (), after, mib
    )


def gather_line(block):
    return [block] + [swap(block, Z * k) for k in (1, 2, 3)]


def gather_stack(line, sc, after, sides=()):
    rows, columns = line[0].shape
    half = columns // 2
    shapes = [(4, rows, half)] * 2 + [(2, 2) + side.shape for side in sides[:1]]

    def plan(sc, *refs):
        ins, outs = refs[: 4 + len(sides)], refs[4 + len(sides) :]
        pairs = [(ins[k].at[:, pl.ds(h * half, half)], outs[h].at[k]) for k in range(4) for h in range(2)]
        return pairs + [(side, outs[2].at[i // 2, i % 2]) for i, side in enumerate(ins[4:])]

    return move(plan, sc, [*line, *sides], shapes, after)


def gather_columns(line, sc, after):
    _, _, rows, half = line[0].shape

    def plan(sc, *refs):
        return [(refs[k].at[h, i], refs[4 + h].at[i, k]) for k in range(4) for h in range(2) for i in range(2)]

    return move(plan, sc, line, [(2, 4, rows, half)] * 2, after)


def pack_rows(qkv, proj, fc1, fc2, width, tiles):
    arrays = (qkv, proj, fc1, fc2)
    rows = proj.shape[0] * 128 // width
    columns = [v.shape[0] * 128 // rows for v in arrays]
    places = [(0, 0), (0, columns[0]), (1, 0), (2, 0)]
    half = columns[3] // 2

    def kernel(*refs):
        ins, outs, scrs = refs[:4], refs[4:8], refs[8:]
        for n, (ref, scr) in enumerate(zip(ins, scrs)):
            scr[...] = ref[...].astype(F32)
            if n < 3:
                blocks = [(i, columns[n] // 128) for i in range(columns[n] // 128)]
            else:
                lanes = width // 128
                blocks = [(k * rows * lanes + i, lanes) for k in range(tiles) for i in range(lanes)]
            for i, (start, stride) in enumerate(blocks):
                to, at = places[n]
                at += i * 128
                if n == 3:
                    to, at = to + at // half, at % half
                outs[to][:, pl.ds(at, 128)] = scr[pl.ds(start, rows, stride=stride)].astype(BF16)

    shapes = [(rows, columns[0] + columns[1]), (rows, columns[2]), (rows, half), (rows, half)]
    scratch = [pltpu.VMEM(v.shape, F32) for v in arrays]
    outs = [(shape, BF16, full(shape)) for shape in shapes]
    return call(kernel, (1,), (), [(far(v), full(v.shape)) for v in arrays], outs, scratch, (), mib=8)[:4]


def gather_pair(a, b, sc, after):
    def plan(sc, a, xa, b, yb, left, right):
        return [(a, left.at[0]), (xa, left.at[1]), (b, right.at[0]), (yb, right.at[1])]

    return move(plan, sc, (a, swap(a, X), b, swap(b, Y)), [(2,) + a.shape] * 2, after)


def gather_place(left, right, sc, after, runs=1):
    _, _, rows, half = left.shape
    width = 2 * half // runs

    def plan(sc, left, other_left, right, other_right, out):
        pairs = []
        for n, sides in enumerate(((left, other_left), (right, other_right))):
            for i in range(2):
                for j in range(2):
                    for k in range(4):
                        x, y = (i, j) if n == 0 else (j, i)
                        to = out.at[sc[3] ^ k, sc[1] ^ x, sc[2] ^ y]
                        if runs == 1:
                            pairs.append((sides[j].at[i, k], to.at[:, pl.ds(n * half, half)]))
                            continue
                        for r in range(runs // 2):
                            run = n * (runs // 2) + r
                            pairs.append((sides[j].at[i, k, :, pl.ds(r * width, width)], to.at[pl.ds(run * rows, rows)]))
        return pairs

    ins = [left, swap(left, Y), right, swap(right, X)]
    own, token = move(plan, sc, ins, [(4, 2, 2, runs * rows, width)], after, 12)
    shape = (COLUMNS, 2 * runs * rows, width)
    return own.reshape(shape), swap(own, CORE).reshape(shape), token


def add(a, b):
    return a.astype(F32) + b.astype(F32)


def fold_core(own, other, sc, after):
    _, rows2, columns = own.shape
    rows, half = rows2 // 2, columns // 2
    by_z = pl.BlockSpec((1, 2, 2, rows, columns), lambda i, *_: (i, 0, 0, 0, 0))
    to_z = pl.BlockSpec((1, 2, rows, half), lambda i, *_: (i, 0, 0, 0))
    left, right = pl.ds(0, half), pl.ds(half, half)

    def kernel(sc, own, got, ka, sa, kb, sb):
        for i in range(2):
            for a, b, flip in ((ka, kb, 0), (sa, sb, 1)):
                y, x = sc[2] ^ flip, sc[1] ^ flip
                a[0, i] = add(own[0, i, y, :, left], got[0, i, y, :, left]).astype(BF16)
                b[0, i] = add(own[0, x, i, :, right], got[0, x, i, :, right]).astype(BF16)

    ins = [(v.reshape(4, 2, 2, rows, columns), by_z) for v in (own, swap(other, CORE))]
    ka, sa, kb, sb, token = call(kernel, (4,), (sc,), ins, [((4, 2, rows, half), BF16, to_z)] * 4, (), after, mib=12)
    return [(ka, sa, Y), (kb, sb, X)], token


def columns_of(parts):
    rows = min(keep.shape[2] for keep, _, _ in parts)
    places, at = [], 0
    for n, (keep, _, _) in enumerate(parts):
        for first in range(0, keep.shape[2], rows):
            places.append((n, first, at, keep.shape[3]))
            at += keep.shape[3]
    return rows, at, places


def fold_first(parts, sc, after):
    groups = [[part for part in parts if part[2] == mask] for mask in (Y, X)]
    ins = [(v, full(v.shape)) for group in groups for keep, send, mask in group for v in (keep, swap(send, mask))]
    layouts = [columns_of(group) for group in groups]
    outs = [((4, rows, width), BF16, full((4, rows, width))) for rows, width, _ in layouts for _ in range(2)]

    def kernel(sc, *refs):
        ins, outs, base = refs[: len(ins_)], refs[len(ins_) :], 0
        for g, (rows, _, places) in enumerate(layouts):
            for n, first, at, width in places:
                keep, got = ins[base + 2 * n], ins[base + 2 * n + 1]
                cut = pl.ds(first, rows)
                for z in range(4):
                    for flip in range(2):
                        here = sc[1 + g] ^ flip
                        to = outs[2 * g + flip]
                        to[z, :, pl.ds(at, width)] = add(keep[z, here, cut], got[z, here, cut]).astype(BF16)
            base += 2 * len(groups[g])

    ins_ = ins
    out = call(kernel, (1,), (sc,), ins, outs, (), after, mib=16)
    return [(out[0], out[1], X), (out[2], out[3], Y)], out[4]


def fold_second(parts, sc, after):
    ins = [(v, full(v.shape)) for keep, send, mask in parts for v in (keep, swap(send, mask))]
    _, rows, width = parts[0][0].shape
    shape = (rows, 2 * width)

    def kernel(sc, *refs):
        ins, outs = refs[:4], refs[4:]
        for k, to in enumerate(outs):
            z = sc[3] ^ k
            for n in range(2):
                to[:, pl.ds(n * width, width)] = add(ins[2 * n][z], ins[2 * n + 1][z]).astype(to.dtype)

    outs = [(shape, F32, full(shape))] + [(shape, BF16, full(shape))] * 3
    return call(kernel, (1,), (sc,), ins, outs, (), after, mib=12)


def fold_sends(parts):
    keep, *sends, token = parts
    return token, [keep] + [swap(v, Z * k) for k, v in zip((1, 2, 3), sends)]


def fold_last(parts, shapes, runs, after):
    def kernel(keep, r1, r2, r3, *outs):
        rows = keep.shape[0]
        for i, (n, first, stride) in enumerate(runs):
            cut = (slice(None), pl.ds(i * 128, 128))
            total = keep[cut] + (r1[cut].astype(F32) + r2[cut].astype(F32) + r3[cut].astype(F32))
            outs[n][pl.ds(first, rows, stride=stride)] = total

    ins = [(v, full(v.shape)) for v in parts]
    return call(kernel, (1,), (), ins, [(shape, F32, full(shape)) for shape in shapes], (), after, mib=12)


def reduce_sends(v, masks):
    return [v] + [swap(v, mask) for mask in masks]


def reduce_level(ins, at, sc, after, split=None):
    v = ins[0]
    shapes, where = split or ([v.shape], [(0, pl.ds(i, 1)) for i in range(v.shape[0])])

    def kernel(sc, *refs):
        line, outs = refs[-1], refs[-1 - len(shapes) : -1]
        mine = sc[at[0]]
        for k in at[1:]:
            mine = 2 * mine + sc[k]
        for k, ref in enumerate(refs[: len(ins)]):
            line[mine ^ k] = ref[...]
        total = line[0]
        for k in range(1, len(ins)):
            total = total + line[k]
        for i, (n, place) in enumerate(where):
            row = total[i : i + 1]
            outs[n][place] = row[0] if len(shapes[n]) == 1 else row

    outs = [(shape, F32, full(shape)) for shape in shapes]
    scratch = [pltpu.VMEM((len(ins),) + v.shape, F32)]
    return call(kernel, (1,), (sc,), [(u, full(v.shape)) for u in ins], outs, scratch, after, mib=8)


def body(
    tokens,
    patch_grid,
    qkv_rows,
    proj_rows,
    fc1_rows,
    fc2_rows,
    norm_gain,
    norm_bias,
    qv_bias,
    proj_bias,
    fc1_bias,
    fc2_bias,
    layer_scale,
    cotangent,
):
    rows, width = tokens.shape
    packs, images, _ = patch_grid.shape
    pack = rows // packs
    slot = pack // images
    head = width // H
    hidden = fc1_bias.shape[0]
    row_width = qkv_rows.shape[1]
    tiles = hidden // width
    tile = min(256, rows)
    swaps = lax.axis_size("wide") == 16 and lax.axis_size("narrow") == 2
    if swaps:
        me = lax.axis_index(AXES)
        sc = jnp.stack([me // CORE % 2, me // X % 2, me % 2, me // Z]).astype(jnp.int32)
    else:
        sc = jnp.zeros((4,), jnp.int32)
    grid_flat = patch_grid.reshape(-1)
    thin, wide_rows = width // (2 * COLUMNS), hidden // (2 * COLUMNS)
    per_tile = COLUMNS // tiles

    by_pack = pl.BlockSpec((pack, width), lambda i, *_: (i, 0))
    by_tile = lambda w: pl.BlockSpec((tile, w), lambda i, *_: (i, 0))
    whole = full((rows, width))
    proj_blocks = pl.BlockSpec((COLUMNS, thin, width), lambda i, *_: (0, 0, 3), pipeline_mode=pl.Buffered(1))
    fc2_blocks = pl.BlockSpec((per_tile, wide_rows, width), lambda i, *_: (i, 0, 0))
    column_blocks = pl.BlockSpec((COLUMNS, thin, width), lambda i, *_: (0, 0, i))
    hidden_tile = pl.BlockSpec((rows, width), lambda i, *_: (0, i))
    vec1, vec2 = full((1, width)), full((2, width))
    hidden_vec = pl.BlockSpec((1, width), lambda i, *_: (0, i))
    qkv_blocks = full((COLUMNS, thin, 3 * width))
    qkv_scr = pltpu.VMEM((COLUMNS, 2, thin, 3 * width), BF16)
    fc2_scr = pltpu.VMEM((per_tile, 2, wide_rows, width), BF16)
    thin_scr = pltpu.VMEM((COLUMNS, 2, thin, width), BF16)
    sum_scr = pltpu.VMEM((rows, width), F32)
    turned_scr = pltpu.VMEM((width, rows), BF16)
    log_block = pl.BlockSpec((tile // slot * H, slot), lambda i, *_: (i, 0))

    halves = lambda v: v.reshape(COLUMNS, 2, -1, v.shape[1]).transpose(1, 0, 2, 3)
    ready = []
    if swaps:
        qp_block, fc1_block, a, b = pack_rows(qkv_rows, proj_rows, fc1_rows, fc2_rows, width, tiles)
        qp_line, fc1_line = gather_line(qp_block), gather_line(fc1_block)
        *qp_ab, message, _ = gather_stack(qp_line, sc, [], (a, swap(a, X), b, swap(b, Y)))
        fc2_line = gather_line(message)
        *qp_pair, token = gather_pair(*qp_ab, sc, [fc1_line[1], fc1_line[3]])
        ready = [token]
    else:
        qp_block = jnp.concatenate([qkv_rows.reshape(-1, 3 * width), proj_rows.reshape(-1, width)], axis=1)
        fc1_block, fc2_block = fc1_rows.reshape(-1, hidden), fc2_rows.reshape(-1, width)
        qp_own, qp_other = halves(lax.all_gather(qp_block, AXES, axis=0, tiled=True))
        fc1_own, fc1_other = halves(lax.all_gather(fc1_block, AXES, axis=0, tiled=True))
        fc2_own, fc2_other = halves(lax.all_gather(fc2_block, AXES, axis=0, tiled=True))

    x, n1, up, b2g, fc2_sums, token = call(
        partial(prepare_kernel, images=images),
        (packs,),
        (grid_flat,),
        [(far(tokens), by_pack), (far(cotangent), by_pack), (norm_gain, vec2), (norm_bias, vec2), (layer_scale, vec2)],
        [((rows, width), BF16, by_pack, "far")] * 4 + [((1, width), F32, vec1)],
        (),
        ready,
        mib=14,
    )

    ready = []
    if swaps:
        *fc1_ab, token = gather_stack(fc1_line, sc, [token, fc2_line[1]])
        qp_own, qp_other, token = gather_place(*qp_pair, sc, [token])
        ready = [token]

    offset = jnp.concatenate([qv_bias[0], jnp.zeros_like(qv_bias[0]), qv_bias[1]])[None]
    proj, att, log_total, token = call(
        partial(attend_kernel, slot=slot, head=head),
        (rows // tile,),
        (grid_flat, sc),
        [(far(n1), by_tile(width)), (qp_own, qkv_blocks), (qp_other, qkv_blocks), (offset, full((1, 3 * width)))],
        [((rows, 3 * width), BF16, by_tile(3 * width), "far"), ((rows, width), BF16, by_tile(width))]
        + [((rows // slot * H, slot), F32, log_block)],
        [qkv_scr],
        ready,
        mib=24,
    )
    ready = []
    if swaps:
        *fc1_pair, token = gather_pair(*fc1_ab, sc, [token, fc2_line[2]])
        ready = [token]
    b1, n2, token = call(
        middle_kernel,
        (1,),
        (sc,),
        [(att, whole), (x, whole), (norm_gain, vec2), (norm_bias, vec2), (layer_scale, vec2), (proj_bias[None], vec1)]
        + [(qp_own, proj_blocks), (qp_other, proj_blocks)],
        [((rows, width), F32, whole, "far"), ((rows, width), BF16, whole)],
        [sum_scr, thin_scr],
        ready,
        mib=20,
    )
    ready = []
    if swaps:
        *fc2_pair, token = gather_columns(fc2_line, sc, [token])
        fc1_own, fc1_other, token = gather_place(*fc1_pair, sc, [token])
        ready = [token]
    cut = tiles - 1

    def some_tiles(first, count, after, alias=None):
        columns = pl.BlockSpec((COLUMNS, thin, width), lambda i, *_: (0, 0, i + first))
        outs = pl.BlockSpec((rows, width), lambda i, *_: (0, i + first))
        blocks = pl.BlockSpec((per_tile, wide_rows, width), lambda i, *_: (i + first, 0, 0))
        return call(
            hidden_kernel,
            (count,),
            (sc,),
            [(n2, whole), (b2g, whole), (fc1_bias[None], pl.BlockSpec((1, width), lambda i, *_: (0, i + first)))]
            + [(fc1_own, columns), (fc1_other, columns)],
            [((rows, hidden), BF16, outs, "far"), ((rows, hidden), F32, outs, "far")]
            + [((COLUMNS, wide_rows, width), BF16, blocks, "far")] * 2,
            [thin_scr],
            after,
            mib=24,
            alias=alias,
        )

    *made, token = some_tiles(0, cut, ready)
    if swaps:
        fc2_own, fc2_other, token = gather_place(*fc2_pair, sc, [token], tiles)
    *made, token = some_tiles(cut, tiles - cut, made + [token], {i: i for i in range(4)})
    act, slope, fc2g_own, fc2g_other = made

    hg, fc1_sums, fc1g_own, fc1g_other, token = call(
        hidden_back_kernel,
        (tiles,),
        (sc,),
        [(far(b2g), whole), (far(n2), whole), (far(slope), hidden_tile), (fc2_own, fc2_blocks), (fc2_other, fc2_blocks)],
        [((rows, hidden), BF16, hidden_tile, "far"), ((1, hidden), F32, hidden_vec)]
        + [((COLUMNS, thin, hidden), BF16, column_blocks, "far")] * 2,
        [fc2_scr],
        mib=26,
    )
    chain = []
    if swaps:
        fc2_parts, token = fold_core(fc2g_own, fc2g_other, sc, [token])
        chain = [token]

    bound = lambda i: jnp.minimum(i, tiles - 1)
    hidden_first = pl.BlockSpec((rows, width), lambda i, *_: (0, bound(i)))
    column_first = pl.BlockSpec((COLUMNS, thin, width), lambda i, *_: (0, 0, bound(i)))
    fc2_first = pl.BlockSpec((per_tile, wide_rows, width), lambda i, *_: (bound(i), 0, 0))
    then = lambda size: pl.BlockSpec((size, width), lambda i, *_: (jnp.maximum(i - tiles, 0), 0))
    mg, b1g, ag, middle_sums, token = call(
        partial(middle_back_kernel, tiles=tiles),
        (tiles + rows // tile,),
        (sc,),
        [(far(hg), hidden_first), (fc1_own, column_first), (fc1_other, column_first)]
        + [(qp_own, proj_blocks), (qp_other, proj_blocks)]
        + [(b1, then(tile)), (x, then(tile)), (up, then(tile)), (norm_gain, vec2), (layer_scale, vec2)],
        [((rows, width), F32, then(tile), "far"), ((rows, width), BF16, then(tile)), ((rows, width), BF16, then(tile))]
        + [((4, width), F32, full((4, width)))],
        [sum_scr, thin_scr, thin_scr],
        chain,
        mib=28,
    )
    chain = []
    if swaps:
        fc1_parts, token = fold_core(fc1g_own, fc1g_other, sc, [token])
        chain = [token]

    pg, proj_sums, token = call(
        partial(attend_back_kernel, slot=slot, head=head),
        (rows // tile,),
        (grid_flat,),
        [(far(proj), by_tile(3 * width)), (ag, by_tile(width)), (log_total, log_block)],
        [((rows, 3 * width), BF16, by_tile(3 * width)), ((8, 3 * width), F32, full((8, 3 * width)))],
        (),
        chain,
        mib=14,
    )
    chain = []
    if swaps:
        fc_parts, token = fold_first(fc1_parts + fc2_parts, sc, [token])
        chain = [token]

    qp_grad_own, qp_grad_other, token = call(
        weight_kernel,
        (4,),
        (sc,),
        [(n1, whole), (att, whole), (pg, pl.BlockSpec((rows, width), lambda i, *_: (0, jnp.minimum(i, 2)))), (b1g, whole)],
        [((COLUMNS, thin, 4 * width), BF16, column_blocks)] * 2,
        (),
        chain,
        mib=18,
    )
    per = pack // tile
    input_grad, input_sums, token = call(
        partial(input_back_kernel, images=images),
        (rows // tile,),
        (grid_flat, sc),
        [(pg, by_tile(3 * width)), (qp_own, qkv_blocks), (qp_other, qkv_blocks)]
        + [(x, by_tile(width)), (far(mg), by_tile(width)), (norm_gain, vec2)],
        [((rows, width), F32, pl.BlockSpec((pack, width), lambda i, *_: (i // per, 0)), "far"), ((2, width), F32, vec2)],
        [qkv_scr, pltpu.VMEM((tile, width), F32)] + [pltpu.VMEM((pack, width), BF16)] * 2,
        [token],
        mib=24,
    )

    chain = []
    if swaps:
        qp_parts, token = fold_core(qp_grad_own, qp_grad_other, sc, [token])
        token, fc_parts = fold_sends(fold_second(fc_parts, sc, [token]))
        chain = [token]

    layer_out, out_sums, token = call(
        partial(layer_out_kernel, images=images, tiles=tiles),
        (tiles + packs,),
        (grid_flat, sc),
        [(far(act), hidden_first), (fc2_own, fc2_first), (fc2_other, fc2_first), (x, then(pack)), (b1, then(pack)), (up, then(pack))]
        + [(layer_scale, vec2), (fc2_bias[None], vec1)],
        [((rows, width), BF16, then(pack), "far"), ((1, width), F32, vec1)],
        [sum_scr, pltpu.VMEM((pack, width), BF16), fc2_scr],
        chain,
        mib=26,
    )
    chain = []
    if swaps:
        qp_parts, token = fold_first(qp_parts, sc, [token, fc_parts[1]])
        chain = [token]

    def gather_sums(input_sums, middle, proj, fc2, out, fc1, to):
        q, v = column_sum(proj[:, pl.ds(0, width)]), column_sum(proj[:, pl.ds(2 * width, width)])
        lines = (input_sums[0:1], middle[2:3], input_sums[1:2], middle[3:4], q, v, middle[1:2], fc2[...], middle[0:1], out[...])
        for i, line in enumerate(lines):
            to[pl.ds(i, 1)] = line
        for i in range(tiles):
            to[pl.ds(len(lines) + i, 1)] = fc1[:, pl.ds(i * width, width)]

    sums_in = (input_sums, middle_sums, proj_sums, fc2_sums, out_sums, fc1_sums)
    sums, token = call(
        gather_sums,
        (1,),
        (),
        [(v, full(v.shape)) for v in sums_in],
        [((10 + tiles, width), F32, full((10 + tiles, width)))],
        (),
        chain,
    )
    if swaps:
        fc2_rows_of = fc2_rows.shape[0] // tiles
        n1_runs, n2_runs = hidden // 256, width // 256
        fc_runs = []
        for half in range(2):
            fc_runs += [(0, half * n1_runs + i, hidden // 128) for i in range(n1_runs)]
            fc_runs += [(1, k * fc2_rows_of + half * n2_runs + i, width // 128) for k in range(tiles) for i in range(n2_runs)]
        sums, token = reduce_level(reduce_sends(sums, (CORE,)), (0,), sc, [token])
        sums, token = reduce_level(reduce_sends(sums, (Y,)), (2,), sc, [token])
        token, qp_parts = fold_sends(fold_second(qp_parts, sc, [token, fc_parts[2], fc_parts[3]]))
        sums, token = reduce_level(reduce_sends(sums, (X,)), (1,), sc, [token])
        fc1_grad, fc2_grad, token = fold_last(fc_parts, (fc1_rows.shape, fc2_rows.shape), fc_runs, [token, qp_parts[1]])
        line = lambda i: pl.ds(i * width, width)
        shapes = [(2, width)] * 3 + [(width,), (hidden,), (width,), (2, width)]
        where = [(i // 2, pl.ds(i % 2, 1)) for i in range(6)] + [(3, line(0)), (5, line(0))]
        where += [(6, pl.ds(0, 1)), (6, pl.ds(1, 1))] + [(4, line(i)) for i in range(tiles)]
        sums = reduce_sends(sums, (Z, 2 * Z, 3 * Z))
        *small, token = reduce_level(sums, (3,), sc, [token] + qp_parts[2:], (shapes, where))
        qkv_runs, proj_runs = 3 * width // 128, width // 128
        qp_runs = [(0, i, qkv_runs) for i in range(qkv_runs)] + [(1, i, proj_runs) for i in range(proj_runs)]
        qkv_grad, proj_grad, _ = fold_last(qp_parts, (qkv_rows.shape, proj_rows.shape), qp_runs, [token])
    else:

        def scatter(own, other):
            matrix = jnp.stack([own, other], axis=1).reshape(-1, own.shape[-1])
            return lax.psum_scatter(matrix, AXES, scatter_dimension=0, tiled=True).astype(F32)

        fc2_grad = scatter(fc2g_own, fc2g_other).reshape(-1, row_width)
        fc1_grad = scatter(fc1g_own, fc1g_other).reshape(-1, row_width)
        qp_grad = scatter(qp_grad_own, qp_grad_other)
        qkv_grad = qp_grad[:, : 3 * width].reshape(-1, row_width)
        proj_grad = qp_grad[:, 3 * width :].reshape(-1, row_width)
        sums = lax.psum(sums, AXES)
        small = [sums[0:2], sums[2:4], sums[4:6], sums[6], sums[10:].reshape(-1), sums[7], sums[8:10]]
    return (
        layer_out,
        input_grad,
        qkv_grad,
        proj_grad,
        fc1_grad,
        fc2_grad,
        *(v.reshape(leaf.shape) for v, leaf in zip(small, (norm_gain, norm_bias, qv_bias, proj_bias, fc1_bias, fc2_bias, layer_scale))),
    )


def solution(mesh):
    split = P(AXES, None)
    return jax.shard_map(
        body,
        mesh=mesh,
        in_specs=(split, P(AXES, None, None)) + (split,) * 4 + (P(),) * 7 + (split,),
        out_specs=(split,) * 6 + (P(),) * 7,
        check_vma=False,
    )
```
